512 devices in a mesh: lon: 32 (over x_lo, z), lat: 16 (over y, x_hi, core).
Axes of the slice: x: 4 (x_hi: 2, x_lo: 2; x = x_hi * 2 + x_lo), y: 4, z: 16, core: 2. Of those that a mesh axis runs over, the one named last changes fastest.
Arguments:
- potential_warmth: float32 [32, 512, 4096], P(None, 'lat', 'lon'), may hold values from -2 to 30
- practical_saltiness: float32 [32, 512, 4096], P(None, 'lat', 'lon'), may hold values from 33 to 37
- zonal_velocity_array: float32 [32, 512, 4096], P(None, 'lat', 'lon'), may hold values from -3 to 3
- meridional_velocity_array: float32 [32, 512, 4096], P(None, 'lat', 'lon'), may hold values from -3 to 3
- interface_diffusion_number: float32 [32, 512, 4096], P(None, 'lat', 'lon'), may hold values from 0.05 to 5
- open_water_indicator: int32 [32, 512, 4096], P(None, 'lat', 'lon'), may hold values from 0 to 1, as said below
- bottom_layer_index: int32 [512, 4096], P('lat', 'lon'), may hold values from 0 to 32, as said below
Outputs:
- temperature_next: float32 [32, 512, 4096], P(None, 'lat', 'lon')
- salinity_next: float32 [32, 512, 4096], P(None, 'lat', 'lon')
- zonal_next: float32 [32, 512, 4096], P(None, 'lat', 'lon')
- meridional_next: float32 [32, 512, 4096], P(None, 'lat', 'lon')
The draws below stay inside these ranges and needn't reach their ends.
Inputs may be any that keep to these rules, and one draw needn't show every extreme that they name: bottom_layer_index counts the wet levels of a column from the surface; open_water_indicator is 0 at every level k >= bottom_layer_index of the column; some column reaches 32 levels and some column has none. `open_water_indicator`: above the sea floor at most the top two levels of a column are closed.
All inputs are finite; a program needn't handle non-finite values.
Results may differ from the reference program's by a relative error of at most 0.00002.
Values sent between devices are 32-bit elements; how exact they have to be, the bound alone decides.
A program may use at most 64 MiB of HBM per device.

```python
import math
import jax
import jax.numpy as jnp
from jax import lax

DEPTH_LAYERS = 32
LATITUDE_SPAN = 512
LONGITUDE_SPAN = 4096


def basin_depth(key):
    coarse_key, detail_key, chosen_key = jax.random.split(key, 3)
    block_rows = (LATITUDE_SPAN + 31) // 32
    block_cols = (LONGITUDE_SPAN + 127) // 128
    coarse = jax.random.randint(coarse_key, (block_rows, block_cols), -DEPTH_LAYERS, 2 * DEPTH_LAYERS)
    spread = jnp.repeat(jnp.repeat(coarse, 32, axis=0), 128, axis=1)[:LATITUDE_SPAN, :LONGITUDE_SPAN]
    detail = jax.random.randint(detail_key, (LATITUDE_SPAN, LONGITUDE_SPAN), -(DEPTH_LAYERS // 4) - 1, DEPTH_LAYERS // 4 + 2)
    column_depth = jnp.clip(spread + detail, 0, DEPTH_LAYERS)
    chosen = jax.random.randint(chosen_key, (1,), 0, LATITUDE_SPAN * LONGITUDE_SPAN)
    deepest = chosen[0]
    driest = (deepest + 1) % (LATITUDE_SPAN * LONGITUDE_SPAN)
    flattened = column_depth.reshape(-1).at[deepest].set(DEPTH_LAYERS).at[driest].set(0)
    return flattened.reshape(LATITUDE_SPAN, LONGITUDE_SPAN).astype(jnp.int32)


def draw_bottom_layer_index(key, part):
    return basin_depth(key)


def draw_open_water_indicator(key, part):
    column_depth = basin_depth(key)
    key = jax.random.fold_in(key, 7)
    shelf_key, ceiling_key = jax.random.split(key)
    shelves = jax.random.randint(shelf_key, (LATITUDE_SPAN, LONGITUDE_SPAN), 0, 8) == 0
    ceiling = jnp.where(shelves, jax.random.randint(ceiling_key, (LATITUDE_SPAN, LONGITUDE_SPAN), 1, 3), 0)
    level_index = jnp.arange(DEPTH_LAYERS, dtype=jnp.int32).reshape(DEPTH_LAYERS, 1, 1)
    return ((level_index >= ceiling[None]) & (level_index < column_depth[None])).astype(jnp.int32)


def level_of(key, shape, cuts, smallest, high):
    loudness, own = 1.0, jax.random.fold_in(key, 6)
    for dim, shards_of in cuts:
        steps = jnp.exp(jax.random.uniform(jax.random.fold_in(own, dim), (shards_of,), jnp.float32, smallest / len(cuts), high / len(cuts)))
        loudness = loudness * jnp.repeat(steps, shape[dim] // shards_of).reshape([-1 if axis == dim else 1 for axis in range(len(shape))])
    return loudness


def scatter_about(rng, dims, scale, reach, pieces=(), held_as=jnp.bfloat16):
    factor_of = level_of(rng, dims, pieces, -0.22, 0.18) if pieces else 1.0
    result = jax.random.normal(rng, dims, jnp.float32) * scale * factor_of
    return jnp.minimum(jnp.maximum(result, -reach), reach).astype(held_as)


def setup_inputs(seed: int = 0) -> dict:
    seeds = jax.random.split(jax.random.key(seed), 8)
    return {
        "potential_warmth": jnp.clip(-2.0 + 32.0 * jax.random.uniform(seeds[0], (DEPTH_LAYERS, LATITUDE_SPAN, LONGITUDE_SPAN), jnp.float32) ** level_of(seeds[0], (DEPTH_LAYERS, LATITUDE_SPAN, LONGITUDE_SPAN), ((1, 16), (2, 32)), -0.2, 0.2), -2.0, 30.0),
        "practical_saltiness": jnp.clip(33.0 + 4.0 * jax.random.uniform(seeds[1], (DEPTH_LAYERS, LATITUDE_SPAN, LONGITUDE_SPAN), jnp.float32) ** level_of(seeds[1], (DEPTH_LAYERS, LATITUDE_SPAN, LONGITUDE_SPAN), ((1, 16), (2, 32)), -0.2, 0.2), 33.0, 37.0),
        "zonal_velocity_array": scatter_about(seeds[2], (DEPTH_LAYERS, LATITUDE_SPAN, LONGITUDE_SPAN), 0.5, 3.0, ((1, 16), (2, 32)), jnp.float32),
        "meridional_velocity_array": scatter_about(seeds[3], (DEPTH_LAYERS, LATITUDE_SPAN, LONGITUDE_SPAN), 0.5, 3.0, ((1, 16), (2, 32)), jnp.float32),
        "interface_diffusion_number": jnp.clip(jnp.exp(math.log(5.0) - 4.6051702 * jax.random.uniform(seeds[4], (DEPTH_LAYERS, LATITUDE_SPAN, LONGITUDE_SPAN), jnp.float32) ** level_of(seeds[4], (DEPTH_LAYERS, LATITUDE_SPAN, LONGITUDE_SPAN), ((1, 16), (2, 32)), -0.2, 0.2)), 0.05, 5.0),
        "open_water_indicator": draw_open_water_indicator(jax.random.fold_in(seeds[7], 71), 0),
        "bottom_layer_index": draw_bottom_layer_index(jax.random.fold_in(seeds[7], 71), 0),
    }


THERMAL_EXPAND = 0.1655
HALINE_CONTRACT = 0.76554
THERMAL_CABBELING = 0.05952
HALINE_CABBELING = 0.00074914
THERMAL_PRESSURE = 0.0001497
HALINE_PRESSURE = 0.00001109
MIXED_CABBELING = 0.0024341
ADVECT = 0.2
DIFFUSE = 0.08
VISCOUS = 0.08
GRADIENT = 0.1
ROTATION = 0.25
BOTTOM_DRAG = 1.0
OCEAN_DEPTH = 4000.0


def level_depths(layer_number_full):
    return (OCEAN_DEPTH * (jnp.arange(layer_number_full, dtype=jnp.float32) + 0.5) / layer_number_full).reshape(layer_number_full, 1, 1)


def density(temp_field, salt_field, water_point_flags, depth_m):
    thermal = temp_field - 10.0
    haline = salt_field - 35.0
    return (-THERMAL_EXPAND * (1.0 + 0.5 * THERMAL_CABBELING * thermal + THERMAL_PRESSURE * depth_m) * thermal
            + HALINE_CONTRACT * (1.0 - 0.5 * HALINE_CABBELING * haline - HALINE_PRESSURE * depth_m) * haline
            - MIXED_CABBELING * thermal * haline) * water_point_flags


def coriolis_rows(rows_global, whole_latitude_extent):
    return ROTATION * jnp.sin(jnp.pi / 180.0 * (-80.0 + 170.0 * (rows_global.astype(jnp.float32) + 0.5) / whole_latitude_extent))


def offset(source, north_step, east_step):
    height = source.shape[1] - 2
    breadth = source.shape[2] - 2
    return source[:, 1 + north_step:1 + north_step + height, 1 + east_step:1 + east_step + breadth]


def horizontal(padded, coriolis):
    layer_number_full = padded.shape[1]
    density_pad = density(padded[0], padded[1], padded[4], level_depths(layer_number_full))
    pressure_pad = (jnp.cumsum(density_pad, axis=0) - 0.5 * density_pad) / layer_number_full
    water_point_flags = offset(padded[4], 0, 0)
    east_mask = water_point_flags * offset(padded[4], 0, 1)
    west_mask = water_point_flags * offset(padded[4], 0, -1)
    north_mask = water_point_flags * offset(padded[4], 1, 0)
    south_mask = water_point_flags * offset(padded[4], -1, 0)
    zonal = offset(padded[2], 0, 0)
    meridional = offset(padded[3], 0, 0)
    east_face = 0.5 * (zonal + offset(padded[2], 0, 1))
    west_face = 0.5 * (offset(padded[2], 0, -1) + zonal)
    north_face = 0.5 * (meridional + offset(padded[3], 1, 0))
    south_face = 0.5 * (offset(padded[3], -1, 0) + meridional)

    def tracer(source):
        centre = offset(source, 0, 0)
        eastern = offset(source, 0, 1)
        western = offset(source, 0, -1)
        northern = offset(source, 1, 0)
        southern = offset(source, -1, 0)
        flux_east = east_mask * (ADVECT * east_face * 0.5 * (centre + eastern) - DIFFUSE * (eastern - centre))
        flux_west = west_mask * (ADVECT * west_face * 0.5 * (western + centre) - DIFFUSE * (centre - western))
        flux_north = north_mask * (ADVECT * north_face * 0.5 * (centre + northern) - DIFFUSE * (northern - centre))
        flux_south = south_mask * (ADVECT * south_face * 0.5 * (southern + centre) - DIFFUSE * (centre - southern))
        return water_point_flags * (centre - (flux_east - flux_west + flux_north - flux_south))

    def laplace(source):
        centre = offset(source, 0, 0)
        return (east_mask * (offset(source, 0, 1) - centre) - west_mask * (centre - offset(source, 0, -1))
                + north_mask * (offset(source, 1, 0) - centre) - south_mask * (centre - offset(source, -1, 0)))

    centre_p = offset(pressure_pad, 0, 0)
    grad_east = 0.5 * (east_mask * (offset(pressure_pad, 0, 1) - centre_p) + west_mask * (centre_p - offset(pressure_pad, 0, -1)))
    grad_north = 0.5 * (north_mask * (offset(pressure_pad, 1, 0) - centre_p) + south_mask * (centre_p - offset(pressure_pad, -1, 0)))
    zonal_star = water_point_flags * (zonal + VISCOUS * laplace(padded[2]) + coriolis * meridional - GRADIENT * grad_east)
    meridional_star = water_point_flags * (meridional + VISCOUS * laplace(padded[3]) - coriolis * zonal - GRADIENT * grad_north)
    return jnp.stack([tracer(padded[0]), tracer(padded[1]), zonal_star, meridional_star], axis=1)


def vertical_terms(star, interface_diffusion_number, water_point_flags, bottom_layer_index):
    layer_number_full = star.shape[0]
    below_mask = jnp.concatenate([water_point_flags[1:], jnp.zeros_like(water_point_flags[:1])], axis=0)
    below_link = interface_diffusion_number * water_point_flags * below_mask
    above_link = jnp.concatenate([jnp.zeros_like(below_link[:1]), below_link[:-1]], axis=0)
    level_index = jnp.arange(layer_number_full, dtype=jnp.int32).reshape(layer_number_full, 1, 1)
    drag_term = BOTTOM_DRAG * water_point_flags * (level_index == bottom_layer_index[None] - 1).astype(jnp.float32)
    momentum = jnp.array([0.0, 0.0, 1.0, 1.0], jnp.float32).reshape(1, 4, 1, 1)
    diagonal = (1.0 + above_link + below_link)[:, None] + drag_term[:, None] * momentum
    return diagonal, above_link, below_link


def pad_global(field, fold_sign):
    northern = fold_sign * jnp.flip(field[:, -1:, :], axis=2)
    southern = jnp.zeros_like(field[:, :1, :])
    rows_pad = jnp.concatenate([southern, field, northern], axis=1)
    return jnp.concatenate([rows_pad[:, :, -1:], rows_pad, rows_pad[:, :, :1]], axis=2)


def reference(potential_warmth, practical_saltiness, zonal_velocity_array, meridional_velocity_array, interface_diffusion_number, open_water_indicator, bottom_layer_index):
    water_point_flags = open_water_indicator.astype(jnp.float32)
    transported_quantities = (potential_warmth, practical_saltiness, zonal_velocity_array, meridional_velocity_array, water_point_flags)
    fold_signs = (1.0, 1.0, -1.0, -1.0, 1.0)
    padded = jnp.stack([pad_global(field, sign_value) for field, sign_value in zip(transported_quantities, fold_signs)])
    whole_latitude_extent = potential_warmth.shape[1]
    coriolis = coriolis_rows(jnp.arange(whole_latitude_extent, dtype=jnp.int32), whole_latitude_extent).reshape(1, whole_latitude_extent, 1)
    star = horizontal(padded, coriolis)
    diagonal, above_link, below_link = vertical_terms(star, interface_diffusion_number, water_point_flags, bottom_layer_index)

    def forward(carried, items):
        factor_prev, value_prev = carried
        diag_plane, rhs_plane, upper_plane, lower_plane = items
        pivot = diag_plane + upper_plane[None] * factor_prev
        factor_now = -lower_plane[None] / pivot
        value_now = (rhs_plane + upper_plane[None] * value_prev) / pivot
        return (factor_now, value_now), (factor_now, value_now)

    plane = jnp.zeros_like(star[0])
    _, (factors, values) = lax.scan(forward, (plane, plane), (diagonal, star, above_link, below_link))

    def backward(next_value, items):
        factor_now, value_now = items
        current = value_now - factor_now * next_value
        return current, current

    _, solved = lax.scan(backward, plane, (factors, values), reverse=True)
    return solved[:, 0], solved[:, 1], solved[:, 2], solved[:, 3]
```

```python
import functools
import math

import jax
import jax.numpy as jnp
from jax import lax
from jax.experimental import pallas as pl
from jax.experimental.pallas import tpu as pltpu
from jax.sharding import PartitionSpec as P

THERMAL_EXPAND = 0.1655
HALINE_CONTRACT = 0.76554
THERMAL_CABBELING = 0.05952
HALINE_CABBELING = 0.00074914
THERMAL_PRESSURE = 0.0001497
HALINE_PRESSURE = 1.109e-05
MIXED_CABBELING = 0.0024341
ADVECT = 0.2
DIFFUSE = 0.08
VISCOUS = 0.08
GRADIENT = 0.1
ROTATION = 0.25
BOTTOM_DRAG = 1.0
OCEAN_DEPTH = 4000.0

MESH = pl.DeviceIdType.MESH
LEVELS = 32
ROWS = 32
LANES = 128
CELLS = LEVELS * ROWS
FIELDS = 4
MASK_ROW = FIELDS * LEVELS
PRESSURE_SCALE = 0.5 / LEVELS * (0.5 * GRADIENT / VISCOUS)
FACE = 0.25 * ADVECT / DIFFUSE


def half_density(warm, salt, wet, level):
    thermal = warm - 10.0
    haline = salt - 35.0
    depth = (level + 0.5) * (OCEAN_DEPTH / LEVELS)
    s = PRESSURE_SCALE
    by_thermal = -THERMAL_EXPAND * s - (THERMAL_EXPAND * THERMAL_PRESSURE * s) * depth
    by_haline = HALINE_CONTRACT * s - (HALINE_CONTRACT * HALINE_PRESSURE * s) * depth
    value = thermal * (
        by_thermal
        - (0.5 * THERMAL_EXPAND * THERMAL_CABBELING * s) * thermal
        - (MIXED_CABBELING * s) * haline
    ) + haline * (by_haline - (0.5 * HALINE_CONTRACT * HALINE_CABBELING * s) * haline)
    return jnp.where(wet, value, 0.0)


def inverse(x):
    r = pl.reciprocal(x, approx=True)
    return r * (2.0 - x * r)


def iota(axis):
    return lax.broadcasted_iota(jnp.int32, (ROWS, LANES), axis)


def kernel(
    lat_count,
    lon_count,
    warm_hbm,
    salt_hbm,
    zonal_hbm,
    merid_hbm,
    mixing_hbm,
    open_hbm,
    bottom_hbm,
    warm_out,
    salt_out,
    zonal_out,
    merid_out,
    warm,
    salt,
    zonal,
    merid,
    mixing,
    top_open,
    bottom,
    stars,
    link,
    inv_tracer,
    inv_momentum,
    row_send,
    row_recv,
    col_send,
    col_recv,
    col_fix,
    load_sem,
    send_sem,
    recv_sem,
):
    lat = lax.axis_index("lat")
    lon = lax.axis_index("lon")
    is_south = lat == 0
    is_north = lat == lat_count - 1
    east = {"lon": lax.rem(lon + 1, lon_count)}
    west = {"lon": lax.rem(lon + lon_count - 1, lon_count)}
    south = {"lat": jnp.maximum(lat - 1, 0)}
    north_lat = jnp.minimum(lat + 1, lat_count - 1)
    north_lon = jnp.where(is_north, lon_count - 1 - lon, lon)
    north = {"lat": north_lat, "lon": north_lon}

    loads = [
        pltpu.make_async_copy(src, dst, load_sem.at[n])
        for n, (src, dst) in enumerate(
            (
                (bottom_hbm, bottom),
                (open_hbm.at[pl.ds(0, 2 * ROWS)], top_open),
                (warm_hbm, warm.at[pl.ds(0, CELLS)]),
                (salt_hbm, salt.at[pl.ds(0, CELLS)]),
                (zonal_hbm, zonal.at[pl.ds(0, CELLS)]),
                (merid_hbm, merid.at[pl.ds(0, CELLS)]),
                (mixing_hbm, mixing),
            )
        )
    ]
    for load in loads:
        load.start()

    barrier = pltpu.get_barrier_semaphore()
    for target in (east, west, north):
        pl.semaphore_signal(barrier, inc=1, device_id=target, device_id_type=MESH)

    @pl.when(lat > 0)
    def _():
        pl.semaphore_signal(barrier, inc=1, device_id=south, device_id_type=MESH)

    fields = (warm, salt, zonal, merid)
    lane = iota(1)
    row = iota(0)
    for field in fields:
        field[pl.ds(CELLS, 8)] = jnp.zeros((8, LANES), jnp.float32)

    @pl.when(is_south)
    def _():
        row_recv[0] = jnp.zeros((MASK_ROW + 8, LANES), jnp.float32)

    row_global = (lat * ROWS + row).astype(jnp.float32)
    coriolis = ROTATION * jnp.sin(
        math.pi / 180.0 * (-80.0 + 170.0 * (row_global + 0.5) / (ROWS * lat_count))
    )

    for load in loads:
        load.wait()

    deep = bottom[...].astype(jnp.float32)
    open0 = top_open[pl.ds(0, ROWS)].astype(jnp.float32)
    open1 = top_open[pl.ds(ROWS, ROWS)].astype(jnp.float32)
    for side, edge in ((0, 0), (1, ROWS - 1)):
        for n, field in enumerate(fields):
            row_send[side, pl.ds(n * LEVELS, LEVELS)] = field[pl.ds(edge, LEVELS, stride=ROWS)]
        for n, plane in enumerate((deep, open0, open1)):
            row_send[side, pl.ds(MASK_ROW + n, 1)] = plane[edge : edge + 1]
        row_send[side, pl.ds(MASK_ROW + 3, 5)] = jnp.zeros((5, LANES), jnp.float32)

    @pl.when(is_north)
    def _():
        flip = (LANES - 1) - lax.broadcasted_iota(jnp.int32, (8, LANES), 1)
        for tile in range((MASK_ROW + 8) // 8):
            there = pl.ds(tile * 8, 8)
            turned = jnp.take_along_axis(row_send[1, there], flip, axis=1)
            if 2 * LEVELS <= tile * 8 < 4 * LEVELS:
                turned = -turned
            row_send[1, there] = turned

    pl.semaphore_wait(barrier, jnp.where(is_south, 3, 4))

    to_north = pltpu.make_async_remote_copy(
        src_ref=row_send.at[1],
        dst_ref=row_recv.at[jnp.where(is_north, 1, 0)],
        send_sem=send_sem.at[1],
        recv_sem=recv_sem.at[jnp.where(is_north, 1, 0)],
        device_id=north,
        device_id_type=MESH,
    )
    to_north.start()
    to_south = pltpu.make_async_remote_copy(
        src_ref=row_send.at[0],
        dst_ref=row_recv.at[1],
        send_sem=send_sem.at[0],
        recv_sem=recv_sem.at[1],
        device_id=south,
        device_id_type=MESH,
    )

    @pl.when(lat > 0)
    def _():
        to_south.start()

    def pack(k, sums):
        easts, wests = sums
        for n, field in enumerate(fields):
            at = n * LEVELS + k
            turned = pltpu.roll(field[pl.ds(pl.multiple_of(k * ROWS, ROWS), ROWS)], at + 1, axis=1)
            easts = jnp.where(lane == at, turned, easts)
            wests = jnp.where(lane == lax.rem(at + 1, LANES), turned, wests)
        return easts, wests

    nothing = jnp.zeros((ROWS, LANES), jnp.float32)
    easts, wests = lax.fori_loop(0, LEVELS, pack, (nothing, nothing), unroll=4)
    col_send[1, pl.ds(0, ROWS)] = easts
    col_send[0, pl.ds(0, ROWS)] = wests
    east_masks = nothing
    west_masks = nothing
    for n, plane in enumerate((deep, open0, open1)):
        turned = pltpu.roll(plane, n + 1, axis=1)
        east_masks = jnp.where(lane == n, turned, east_masks)
        west_masks = jnp.where(lane == n + 1, turned, west_masks)
    col_send[1, pl.ds(ROWS, ROWS)] = east_masks
    col_send[0, pl.ds(ROWS, ROWS)] = west_masks
    to_east = pltpu.make_async_remote_copy(
        src_ref=col_send.at[1],
        dst_ref=col_recv.at[0],
        send_sem=send_sem.at[3],
        recv_sem=recv_sem.at[2],
        device_id=east,
        device_id_type=MESH,
    )
    to_west = pltpu.make_async_remote_copy(
        src_ref=col_send.at[0],
        dst_ref=col_recv.at[1],
        send_sem=send_sem.at[2],
        recv_sem=recv_sem.at[3],
        device_id=west,
        device_id_type=MESH,
    )
    to_east.start()
    to_west.start()

    depth_here = bottom[...]
    not_east = lane < LANES - 1
    not_north = row < ROWS - 1
    depth_east = jnp.where(
        not_east, jnp.minimum(depth_here, pltpu.roll(depth_here, LANES - 1, axis=1)), 0
    )
    depth_north = jnp.where(
        not_north, jnp.minimum(depth_here, pltpu.roll(depth_here, ROWS - 1, axis=0)), 0
    )

    def level(k, masks, carried):
        above, g_above, pressure_sum = carried
        wet, wet_east, wet_north, wet_below = masks
        k_float = jnp.asarray(k, jnp.int32).astype(jnp.float32)
        start = k * ROWS
        here = pl.ds(start if isinstance(k, int) else pl.multiple_of(start, ROWS), ROWS)
        shifted = pl.ds(start + 1, ROWS)
        t, s, u, v = (field[here] for field in fields)
        t_n, s_n, u_n, v_n = (field[shifted] for field in fields)
        t_e, s_e, u_e, v_e = (pltpu.roll(x, LANES - 1, axis=1) for x in (t, s, u, v))

        half = half_density(t, s, wet, k_float)
        pressure = pressure_sum + half
        pressure_sum = pressure + half
        p_e = pltpu.roll(pressure, LANES - 1, axis=1)
        p_n = pltpu.roll(pressure, ROWS - 1, axis=0)

        a_e = FACE * (u + u_e)
        a_n = FACE * (v + v_n)
        ahead_e = jnp.where(wet_east, a_e - 1.0, 0.0)
        behind_e = jnp.where(wet_east, a_e + 1.0, 0.0)
        ahead_n = jnp.where(wet_north, a_n - 1.0, 0.0)
        behind_n = jnp.where(wet_north, a_n + 1.0, 0.0)

        def spread(f_e, f_n):
            return (f_e - pltpu.roll(f_e, 1, axis=1)) + (f_n - pltpu.roll(f_n, 1, axis=0))

        def tracer(q, q_e, q_n):
            f_e = ahead_e * q_e + behind_e * q
            f_n = ahead_n * q_n + behind_n * q
            return jnp.where(wet, q - DIFFUSE * spread(f_e, f_n), 0.0)

        stars[0, here] = tracer(t, t_e, t_n)
        stars[1, here] = tracer(s, s_e, s_n)

        du_e = jnp.where(wet_east, u_e - u, 0.0)
        dp_e = jnp.where(wet_east, p_e - pressure, 0.0)
        du_n = jnp.where(wet_north, u_n - u, 0.0)
        lap_u = ((du_e - dp_e) - pltpu.roll(du_e + dp_e, 1, axis=1)) + (
            du_n - pltpu.roll(du_n, 1, axis=0)
        )
        stars[2, here] = jnp.where(wet, u + VISCOUS * lap_u + coriolis * v, 0.0)
        dv_n = jnp.where(wet_north, v_n - v, 0.0)
        dp_n = jnp.where(wet_north, p_n - pressure, 0.0)
        dv_e = jnp.where(wet_east, v_e - v, 0.0)
        lap_v = ((dv_n - dp_n) - pltpu.roll(dv_n + dp_n, 1, axis=0)) + (
            dv_e - pltpu.roll(dv_e, 1, axis=1)
        )
        stars[3, here] = jnp.where(wet, v + VISCOUS * lap_v - coriolis * u, 0.0)

        below = jnp.where(wet_below, mixing[here], 0.0)
        diagonal = (1.0 + below) + above * (1.0 - g_above)
        inv = inverse(diagonal)
        dragged = jnp.logical_and(depth_here == k + 1, wet)
        inv_m = inverse(diagonal + jnp.where(dragged, BOTTOM_DRAG, 0.0))
        link[here] = below
        inv_tracer[here] = inv
        inv_momentum[here] = inv_m
        return below, below * inv, pressure_sum

    def open_pair(plane):
        wet = plane > 0.5
        wet_east = jnp.where(not_east, plane * pltpu.roll(plane, LANES - 1, axis=1), 0.0) > 0.5
        wet_north = jnp.where(not_north, plane * pltpu.roll(plane, ROWS - 1, axis=0), 0.0) > 0.5
        return wet, wet_east, wet_north

    carried = (nothing, nothing, nothing)
    carried = level(0, open_pair(open0) + (open0 * open1 > 0.5,), carried)
    carried = level(
        1,
        open_pair(open1) + (jnp.logical_and(open1 > 0.5, depth_here > 2),),
        carried,
    )

    def deeper(k, carried):
        masks = (depth_here > k, depth_east > k, depth_north > k, depth_here > k + 1)
        return level(k, masks, carried)

    lax.fori_loop(2, LEVELS, deeper, carried)

    pltpu.make_async_remote_copy(
        src_ref=row_send.at[1],
        dst_ref=row_recv.at[1],
        send_sem=send_sem.at[1],
        recv_sem=recv_sem.at[1],
        device_id=north,
        device_id_type=MESH,
    ).wait_recv()

    @pl.when(lat > 0)
    def _():
        pltpu.make_async_remote_copy(
            src_ref=row_send.at[0],
            dst_ref=row_recv.at[0],
            send_sem=send_sem.at[0],
            recv_sem=recv_sem.at[0],
            device_id=south,
            device_id_type=MESH,
        ).wait_recv()

    def wet_levels(level_index, depth, first, second):
        return jnp.where(
            level_index == 0,
            first,
            jnp.where(
                level_index == 1,
                second,
                jnp.where(level_index.astype(jnp.float32) < depth, 1.0, 0.0),
            ),
        )

    def summed(half, axis, index):
        total = half
        for step in (1, 2, 4, 8, 16):
            total = total + jnp.where(index >= step, pltpu.roll(total, step, axis=axis), 0.0)
        return 2.0 * total - half

    def edge_faces(q, q_o, a, face):
        return jnp.where(face, (a - 1.0) * q_o + (a + 1.0) * q, 0.0)

    for side, edge in ((0, 0), (1, ROWS - 1)):
        there = pl.ds(edge, LEVELS, stride=ROWS)
        own = [field[there] for field in fields]
        other = [row_recv[side, pl.ds(n * LEVELS, LEVELS)] for n in range(FIELDS)]
        own_wet = wet_levels(row, deep[edge : edge + 1], open0[edge : edge + 1], open1[edge : edge + 1])
        other_wet = wet_levels(
            row, *(row_recv[side, pl.ds(MASK_ROW + n, 1)] for n in range(3))
        )
        own_p = summed(half_density(own[0], own[1], own_wet > 0.5, row.astype(jnp.float32)), 0, row)
        other_p = summed(
            half_density(other[0], other[1], other_wet > 0.5, row.astype(jnp.float32)), 0, row
        )
        face = own_wet * other_wet > 0.5
        sign = 1.0 if side else -1.0
        a = (sign * FACE) * (own[3] + other[3])
        for n in (0, 1):
            stars[n, there] += -DIFFUSE * edge_faces(own[n], other[n], a, face)
        stars[2, there] += jnp.where(face, VISCOUS * (other[2] - own[2]), 0.0)
        stars[3, there] += jnp.where(
            face, VISCOUS * ((other[3] - own[3]) - sign * (other_p - own_p)), 0.0
        )

    for side, sem in ((0, 2), (1, 3)):
        pltpu.make_async_remote_copy(
            src_ref=col_send.at[side],
            dst_ref=col_recv.at[side],
            send_sem=send_sem.at[sem],
            recv_sem=recv_sem.at[sem],
            device_id=east,
            device_id_type=MESH,
        ).wait_recv()
    level_lane = lax.rem(lane, LEVELS)
    level_lane_float = level_lane.astype(jnp.float32)
    first_group = lane < LEVELS
    fixes = []
    for side in (0, 1):
        own = col_send[side, pl.ds(0, ROWS)]
        other = col_recv[side, pl.ds(0, ROWS)]
        own_mask = col_send[side, pl.ds(ROWS, ROWS)]
        other_mask = col_recv[side, pl.ds(ROWS, ROWS)]
        if side == 0:
            own = pltpu.roll(own, LANES - 1, axis=1)
            own_mask = pltpu.roll(own_mask, LANES - 1, axis=1)
        else:
            other = pltpu.roll(other, LANES - 1, axis=1)
            other_mask = pltpu.roll(other_mask, LANES - 1, axis=1)

        def spread_mask(mask):
            return wet_levels(
                level_lane,
                *(jnp.broadcast_to(mask[:, n : n + 1], (ROWS, LANES)) for n in range(3)),
            )

        own_wet = spread_mask(own_mask)
        other_wet = spread_mask(other_mask)

        def pressure_of(packed, wet):
            half = half_density(
                packed,
                pltpu.roll(packed, LANES - LEVELS, axis=1),
                jnp.logical_and(wet > 0.5, first_group),
                level_lane_float,
            )
            return summed(half, 1, lane)

        jump_p = pressure_of(other, other_wet) - pressure_of(own, own_wet)
        face = own_wet * other_wet > 0.5
        sign = 1.0 if side else -1.0
        both = own + other
        a = (sign * FACE) * jnp.where(
            first_group, pltpu.roll(both, 2 * LEVELS, axis=1), pltpu.roll(both, 3 * LEVELS, axis=1)
        )
        tracers = -DIFFUSE * edge_faces(own, other, a, face)
        jump = other - own
        jump = jnp.where(
            lane < 3 * LEVELS, jump - sign * pltpu.roll(jump_p, 2 * LEVELS, axis=1), jump
        )
        currents = jnp.where(face, VISCOUS * jump, 0.0)
        fixes.append(jnp.where(lane < 2 * LEVELS, tracers, currents))
    west_fix = pltpu.roll(fixes[0], 1, axis=1)
    east_fix = fixes[1]
    even_lane = lax.rem(lane, 2) == 0
    col_fix[0] = jnp.where(even_lane, east_fix, west_fix)
    col_fix[1] = jnp.where(even_lane, west_fix, east_fix)

    edge_lane = jnp.logical_or(lane == 0, lane == LANES - 1)

    def forward(k, carried):
        above, *values = carried
        here = pl.ds(pl.multiple_of(k * ROWS, ROWS), ROWS)
        fix = col_fix[lax.rem(k, 2)]
        invs = (inv_tracer[here], inv_momentum[here])
        new = []
        for n in range(FIELDS):
            turned = pltpu.roll(fix, LANES - 1 - n * LEVELS - k, axis=1)
            star = stars[n, here] + jnp.where(edge_lane, turned, 0.0)
            value = (star + above * values[n]) * invs[n // 2]
            stars[n, here] = value
            new.append(value)
        return (link[here], *new)

    _, *values = lax.fori_loop(0, LEVELS, forward, (nothing,) * 5)

    outs = (warm_out, salt_out, zonal_out, merid_out)
    last = pl.ds(CELLS - ROWS, ROWS)
    for n in range(FIELDS):
        outs[n][last] = values[n]

    def backward(step, values):
        k = LEVELS - 2 - step
        here = pl.ds(pl.multiple_of(k * ROWS, ROWS), ROWS)
        ratio = link[here] * inv_tracer[here]
        new = []
        for n in range(FIELDS):
            value = stars[n, here] + ratio * values[n]
            outs[n][here] = value
            new.append(value)
        return tuple(new)

    lax.fori_loop(0, LEVELS - 1, backward, tuple(values))

    to_north.wait_send()
    to_east.wait_send()
    to_west.wait_send()

    @pl.when(lat > 0)
    def _():
        to_south.wait_send()


def solution(mesh):
    lat_count = mesh.shape["lat"]
    lon_count = mesh.shape["lon"]

    def step(warm, salt, zonal, merid, mixing, open_water, bottom):
        flat = [x.reshape(CELLS, LANES) for x in (warm, salt, zonal, merid, mixing, open_water)]
        f32 = jnp.float32
        outs = pl.pallas_call(
            functools.partial(kernel, lat_count, lon_count),
            out_shape=[pltpu.VMEM((CELLS, LANES), f32)] * FIELDS,
            in_specs=[pl.BlockSpec(memory_space=pl.ANY)] * 7,
            out_specs=[pl.BlockSpec(memory_space=pltpu.VMEM)] * FIELDS,
            scratch_shapes=[
                *[pltpu.VMEM((CELLS + 8, LANES), f32)] * FIELDS,
                pltpu.VMEM((CELLS, LANES), f32),
                pltpu.VMEM((2 * ROWS, LANES), jnp.int32),
                pltpu.VMEM((ROWS, LANES), jnp.int32),
                pltpu.VMEM((FIELDS, CELLS, LANES), f32),
                pltpu.VMEM((CELLS, LANES), f32),
                pltpu.VMEM((CELLS, LANES), f32),
                pltpu.VMEM((CELLS, LANES), f32),
                pltpu.VMEM((2, MASK_ROW + 8, LANES), f32),
                pltpu.VMEM((2, MASK_ROW + 8, LANES), f32),
                pltpu.VMEM((2, 2 * ROWS, LANES), f32),
                pltpu.VMEM((2, 2 * ROWS, LANES), f32),
                pltpu.VMEM((2, ROWS, LANES), f32),
                pltpu.SemaphoreType.DMA((7,)),
                pltpu.SemaphoreType.DMA((4,)),
                pltpu.SemaphoreType.DMA((4,)),
            ],
            compiler_params=pltpu.CompilerParams(
                collective_id=0, has_side_effects=True, vmem_limit_bytes=16 * 1024 * 1024
            ),
        )(*[pltpu.with_memory_space_constraint(x, pltpu.HBM) for x in (*flat, bottom)])
        return tuple(x.reshape(LEVELS, ROWS, LANES) for x in outs)

    tile = P(None, "lat", "lon")
    return jax.shard_map(
        step,
        mesh=mesh,
        in_specs=(tile,) * 6 + (P("lat", "lon"),),
        out_specs=(tile,) * 4,
        check_vma=False,
    )
```

```python
import functools
import math

import jax
import jax.numpy as jnp
from jax import lax
from jax.experimental import pallas as pl
from jax.experimental.pallas import tpu as pltpu
from jax.sharding import PartitionSpec as P

THERMAL_EXPAND = 0.1655
HALINE_CONTRACT = 0.76554
THERMAL_CABBELING = 0.05952
HALINE_CABBELING = 0.00074914
THERMAL_PRESSURE = 0.0001497
HALINE_PRESSURE = 1.109e-05
MIXED_CABBELING = 0.0024341
ADVECT = 0.2
DIFFUSE = 0.08
VISCOUS = 0.08
GRADIENT = 0.1
ROTATION = 0.25
BOTTOM_DRAG = 1.0
OCEAN_DEPTH = 4000.0

MESH = pl.DeviceIdType.MESH
LEVELS = 32
ROWS = 32
LANES = 128
CELLS = LEVELS * ROWS
FIELDS = 4
MASK_ROW = FIELDS * LEVELS
EDGE = 16
PRESSURE_SCALE = 0.5 / LEVELS * (0.5 * GRADIENT / VISCOUS)
FACE = 0.25 * ADVECT / DIFFUSE


def half_density(warm, salt, wet, level):
    thermal = warm - 10.0
    haline = salt - 35.0
    depth = (level + 0.5) * (OCEAN_DEPTH / LEVELS)
    s = PRESSURE_SCALE
    by_thermal = -THERMAL_EXPAND * s - (THERMAL_EXPAND * THERMAL_PRESSURE * s) * depth
    by_haline = HALINE_CONTRACT * s - (HALINE_CONTRACT * HALINE_PRESSURE * s) * depth
    value = thermal * (
        by_thermal
        - (0.5 * THERMAL_EXPAND * THERMAL_CABBELING * s) * thermal
        - (MIXED_CABBELING * s) * haline
    ) + haline * (by_haline - (0.5 * HALINE_CONTRACT * HALINE_CABBELING * s) * haline)
    return jnp.where(wet, value, 0.0)


def inverse(x):
    r = pl.reciprocal(x, approx=True)
    return r * (2.0 - x * r)


def iota(axis):
    return lax.broadcasted_iota(jnp.int32, (ROWS, LANES), axis)


def kernel(
    lat_count,
    lon_count,
    warm_hbm,
    salt_hbm,
    zonal_hbm,
    merid_hbm,
    mixing_hbm,
    open_hbm,
    bottom_hbm,
    warm_out,
    salt_out,
    zonal_out,
    merid_out,
    col_out,
    warm,
    salt,
    zonal,
    merid,
    mixing,
    top_open,
    bottom,
    link,
    inv_tracer,
    inv_momentum,
    row_send,
    row_recv,
    col_send,
    col_recv,
    edge_inv,
    edge_down,
    edge_up,
    edge_value,
    square,
    load_sem,
    send_sem,
    recv_sem,
):
    lat = lax.axis_index("lat")
    lon = lax.axis_index("lon")
    is_south = lat == 0
    is_north = lat == lat_count - 1
    east = {"lon": lax.rem(lon + 1, lon_count)}
    west = {"lon": lax.rem(lon + lon_count - 1, lon_count)}
    south = {"lat": jnp.maximum(lat - 1, 0)}
    north_lat = jnp.minimum(lat + 1, lat_count - 1)
    north_lon = jnp.where(is_north, lon_count - 1 - lon, lon)
    north = {"lat": north_lat, "lon": north_lon}
    fields = (warm, salt, zonal, merid)
    outs = (warm_out, salt_out, zonal_out, merid_out)

    loads = [
        pltpu.make_async_copy(src, dst, load_sem.at[n])
        for n, (src, dst) in enumerate(
            (
                (bottom_hbm, bottom),
                (open_hbm.at[pl.ds(0, 2 * ROWS)], top_open),
                (warm_hbm, warm.at[pl.ds(0, CELLS)]),
                (salt_hbm, salt.at[pl.ds(0, CELLS)]),
                (zonal_hbm, zonal.at[pl.ds(0, CELLS)]),
                (merid_hbm, merid.at[pl.ds(0, CELLS)]),
                (mixing_hbm, mixing),
            )
        )
    ]
    for load in loads:
        load.start()

    barrier = pltpu.get_barrier_semaphore()
    for target in (east, west, north):
        pl.semaphore_signal(barrier, inc=1, device_id=target, device_id_type=MESH)

    @pl.when(lat > 0)
    def _():
        pl.semaphore_signal(barrier, inc=1, device_id=south, device_id_type=MESH)

    lane = iota(1)
    row = iota(0)
    nothing = jnp.zeros((ROWS, LANES), jnp.float32)
    for field in fields:
        field[pl.ds(CELLS, 8)] = jnp.zeros((8, LANES), jnp.float32)

    @pl.when(is_south)
    def _():
        row_recv[0] = jnp.zeros((MASK_ROW + 8, LANES), jnp.float32)

    row_global = (lat * ROWS + row).astype(jnp.float32)
    coriolis = ROTATION * jnp.sin(
        math.pi / 180.0 * (-80.0 + 170.0 * (row_global + 0.5) / (ROWS * lat_count))
    )

    def at_level(k):
        return pl.ds(pl.multiple_of(k * ROWS, ROWS), ROWS)

    def pack(source, n, sums):
        def one(k, sums):
            easts, wests = sums
            at = n * LEVELS + k
            turned = pltpu.roll(source(k), at + 1, axis=1)
            easts = jnp.where(lane == at, turned, easts)
            wests = jnp.where(lane == lax.rem(at + 1, LANES), turned, wests)
            return easts, wests

        return lax.fori_loop(0, LEVELS, one, sums, unroll=8)

    loads[0].wait()
    loads[1].wait()
    deep = bottom[...].astype(jnp.float32)
    open0 = top_open[pl.ds(0, ROWS)].astype(jnp.float32)
    open1 = top_open[pl.ds(ROWS, ROWS)].astype(jnp.float32)
    mask_planes = (deep, open0, open1)
    for side, edge in ((0, 0), (1, ROWS - 1)):
        for n, plane in enumerate(mask_planes):
            row_send[side, pl.ds(MASK_ROW + n, 1)] = plane[edge : edge + 1]
        row_send[side, pl.ds(MASK_ROW + 3, 5)] = jnp.zeros((5, LANES), jnp.float32)
    east_masks = nothing
    west_masks = nothing
    for n, plane in enumerate(mask_planes):
        turned = pltpu.roll(plane, n + 1, axis=1)
        east_masks = jnp.where(lane == n, turned, east_masks)
        west_masks = jnp.where(lane == n + 1, turned, west_masks)
    col_send[1, pl.ds(ROWS, ROWS)] = east_masks
    col_send[0, pl.ds(ROWS, ROWS)] = west_masks
    packed = (nothing, nothing)
    for n, field in enumerate(fields):
        loads[2 + n].wait()
        for side, edge in ((0, 0), (1, ROWS - 1)):
            row_send[side, pl.ds(n * LEVELS, LEVELS)] = field[pl.ds(edge, LEVELS, stride=ROWS)]
        packed = pack(lambda k, field=field: field[at_level(k)], n, packed)
    col_send[1, pl.ds(0, ROWS)] = packed[0]
    col_send[0, pl.ds(0, ROWS)] = packed[1]

    @pl.when(is_north)
    def _():
        flip = (LANES - 1) - lax.broadcasted_iota(jnp.int32, (8, LANES), 1)
        for tile in range((MASK_ROW + 8) // 8):
            there = pl.ds(tile * 8, 8)
            turned = jnp.take_along_axis(row_send[1, there], flip, axis=1)
            if 2 * LEVELS <= tile * 8 < 4 * LEVELS:
                turned = -turned
            row_send[1, there] = turned

    pl.semaphore_wait(barrier, jnp.where(is_south, 3, 4))

    to_north = pltpu.make_async_remote_copy(
        src_ref=row_send.at[1],
        dst_ref=row_recv.at[jnp.where(is_north, 1, 0)],
        send_sem=send_sem.at[1],
        recv_sem=recv_sem.at[jnp.where(is_north, 1, 0)],
        device_id=north,
        device_id_type=MESH,
    )
    to_south = pltpu.make_async_remote_copy(
        src_ref=row_send.at[0],
        dst_ref=row_recv.at[1],
        send_sem=send_sem.at[0],
        recv_sem=recv_sem.at[1],
        device_id=south,
        device_id_type=MESH,
    )
    to_east = pltpu.make_async_remote_copy(
        src_ref=col_send.at[1],
        dst_ref=col_recv.at[0],
        send_sem=send_sem.at[3],
        recv_sem=recv_sem.at[2],
        device_id=east,
        device_id_type=MESH,
    )
    to_west = pltpu.make_async_remote_copy(
        src_ref=col_send.at[0],
        dst_ref=col_recv.at[1],
        send_sem=send_sem.at[2],
        recv_sem=recv_sem.at[3],
        device_id=west,
        device_id_type=MESH,
    )
    to_north.start()

    @pl.when(lat > 0)
    def _():
        to_south.start()

    to_east.start()
    to_west.start()

    loads[6].wait()
    depth_here = bottom[...]
    not_east = lane < LANES - 1
    not_north = row < ROWS - 1
    depth_east = jnp.where(
        not_east, jnp.minimum(depth_here, pltpu.roll(depth_here, LANES - 1, axis=1)), 0
    )
    depth_north = jnp.where(
        not_north, jnp.minimum(depth_here, pltpu.roll(depth_here, ROWS - 1, axis=0)), 0
    )
    link[pl.ds(0, ROWS)] = nothing

    def level(k, masks, carried):
        above, g_above, pressure_sum = carried
        wet, wet_east, wet_north, wet_below = masks
        k_float = jnp.asarray(k, jnp.int32).astype(jnp.float32)
        start = k * ROWS
        here = pl.ds(start if isinstance(k, int) else pl.multiple_of(start, ROWS), ROWS)
        shifted = pl.ds(start + 1, ROWS)
        t, s, u, v = (field[here] for field in fields)
        t_n, s_n, u_n, v_n = (field[shifted] for field in fields)
        t_e, s_e, u_e, v_e = (pltpu.roll(x, LANES - 1, axis=1) for x in (t, s, u, v))

        half = half_density(t, s, wet, k_float)
        pressure = pressure_sum + half
        pressure_sum = pressure + half
        p_e = pltpu.roll(pressure, LANES - 1, axis=1)
        p_n = pltpu.roll(pressure, ROWS - 1, axis=0)

        a_e = FACE * (u + u_e)
        a_n = FACE * (v + v_n)
        ahead_e = jnp.where(wet_east, a_e - 1.0, 0.0)
        behind_e = jnp.where(wet_east, a_e + 1.0, 0.0)
        ahead_n = jnp.where(wet_north, a_n - 1.0, 0.0)
        behind_n = jnp.where(wet_north, a_n + 1.0, 0.0)

        def spread(f_e, f_n):
            return (f_e - pltpu.roll(f_e, 1, axis=1)) + (f_n - pltpu.roll(f_n, 1, axis=0))

        def tracer(q, q_e, q_n):
            f_e = ahead_e * q_e + behind_e * q
            f_n = ahead_n * q_n + behind_n * q
            return jnp.where(wet, q - DIFFUSE * spread(f_e, f_n), 0.0)

        warm_out[here] = tracer(t, t_e, t_n)
        salt_out[here] = tracer(s, s_e, s_n)

        du_e = jnp.where(wet_east, u_e - u, 0.0)
        dp_e = jnp.where(wet_east, p_e - pressure, 0.0)
        du_n = jnp.where(wet_north, u_n - u, 0.0)
        lap_u = ((du_e - dp_e) - pltpu.roll(du_e + dp_e, 1, axis=1)) + (
            du_n - pltpu.roll(du_n, 1, axis=0)
        )
        zonal_out[here] = jnp.where(wet, u + VISCOUS * lap_u + coriolis * v, 0.0)
        dv_n = jnp.where(wet_north, v_n - v, 0.0)
        dp_n = jnp.where(wet_north, p_n - pressure, 0.0)
        dv_e = jnp.where(wet_east, v_e - v, 0.0)
        lap_v = ((dv_n - dp_n) - pltpu.roll(dv_n + dp_n, 1, axis=0)) + (
            dv_e - pltpu.roll(dv_e, 1, axis=1)
        )
        merid_out[here] = jnp.where(wet, v + VISCOUS * lap_v - coriolis * u, 0.0)

        below = jnp.where(wet_below, mixing[here], 0.0)
        diagonal = (1.0 + below) + above * (1.0 - g_above)
        inv = inverse(diagonal)
        dragged = jnp.logical_and(depth_here == k + 1, wet)
        inv_m = inverse(diagonal + jnp.where(dragged, BOTTOM_DRAG, 0.0))
        link[pl.ds(start + ROWS, ROWS)] = below
        inv_tracer[here] = inv
        inv_momentum[here] = inv_m
        return below, below * inv, pressure_sum

    def open_pair(plane):
        wet = plane > 0.5
        wet_east = jnp.where(not_east, plane * pltpu.roll(plane, LANES - 1, axis=1), 0.0) > 0.5
        wet_north = jnp.where(not_north, plane * pltpu.roll(plane, ROWS - 1, axis=0), 0.0) > 0.5
        return wet, wet_east, wet_north

    carried = (nothing, nothing, nothing)
    carried = level(0, open_pair(open0) + (open0 * open1 > 0.5,), carried)
    carried = level(
        1,
        open_pair(open1) + (jnp.logical_and(open1 > 0.5, depth_here > 2),),
        carried,
    )

    def deeper(k, carried):
        masks = (depth_here > k, depth_east > k, depth_north > k, depth_here > k + 1)
        return level(k, masks, carried)

    lax.fori_loop(2, LEVELS, deeper, carried)

    def forward(k, values):
        here = at_level(k)
        above = link[here]
        invs = (inv_tracer[here], inv_momentum[here])
        new = []
        for n in range(FIELDS):
            value = (outs[n][here] + above * values[n]) * invs[n // 2]
            outs[n][here] = value
            new.append(value)
        return tuple(new)

    values = lax.fori_loop(0, LEVELS, forward, (nothing,) * 4, unroll=2)

    def backward(step, values):
        k = LEVELS - 2 - step
        here = at_level(k)
        ratio = link[at_level(k + 1)] * inv_tracer[here]
        new = []
        for n in range(FIELDS):
            value = outs[n][here] + ratio * values[n]
            outs[n][here] = value
            new.append(value)
        return tuple(new)

    lax.fori_loop(0, LEVELS - 1, backward, values, unroll=2)

    for side, edge in ((0, 0), (1, ROWS - 1)):
        there = pl.ds(edge, LEVELS, stride=ROWS)
        above = link[there]
        below = link[pl.ds(ROWS + edge, LEVELS, stride=ROWS)]
        inv_t = inv_tracer[there]
        inv_m = inv_momentum[there]
        up = below * inv_t
        for n in range(FIELDS):
            to = pl.ds(side * FIELDS + n, LEVELS, stride=EDGE)
            edge_inv[to] = inv_m if n > 1 else inv_t
            edge_down[to] = above * (inv_m if n > 1 else inv_t)
            edge_up[to] = up
    packed = (nothing, nothing)
    packed = pack(lambda k: link[at_level(k)], 0, packed)
    packed = pack(lambda k: inv_tracer[at_level(k)], 1, packed)
    packed = pack(lambda k: inv_momentum[at_level(k)], 2, packed)
    packed = pack(lambda k: link[at_level(k + 1)], 3, packed)

    def side_by_side(wests, easts):
        square[pl.ds(0, ROWS)] = wests
        square[pl.ds(ROWS, ROWS)] = easts
        square[pl.ds(2 * ROWS, ROWS)] = nothing
        square[pl.ds(3 * ROWS, ROWS)] = nothing
        return square[...].T

    coefs = side_by_side(pltpu.roll(packed[1], LANES - 1, axis=1), packed[0])
    above, inv_t, inv_m, below = (coefs[n * LEVELS : (n + 1) * LEVELS] for n in range(4))
    for n in range(FIELDS):
        to = pl.ds(2 * FIELDS + n, LEVELS, stride=EDGE)
        edge_inv[to] = inv_m if n > 1 else inv_t
        edge_down[to] = above * (inv_m if n > 1 else inv_t)
        edge_up[to] = below * inv_t
        spare = pl.ds(3 * FIELDS + n, LEVELS, stride=EDGE)
        edge_down[spare] = nothing
        edge_up[spare] = nothing
        edge_value[spare] = nothing

    def wet_levels(level_index, depth, first, second):
        return jnp.where(
            level_index == 0,
            first,
            jnp.where(
                level_index == 1,
                second,
                jnp.where(level_index.astype(jnp.float32) < depth, 1.0, 0.0),
            ),
        )

    def summed(half, axis, index):
        total = half
        for step in (1, 2, 4, 8, 16):
            total = total + jnp.where(index >= step, pltpu.roll(total, step, axis=axis), 0.0)
        return 2.0 * total - half

    def edge_faces(q, q_o, a, face):
        return jnp.where(face, (a - 1.0) * q_o + (a + 1.0) * q, 0.0)

    pltpu.make_async_remote_copy(
        src_ref=row_send.at[1],
        dst_ref=row_recv.at[1],
        send_sem=send_sem.at[1],
        recv_sem=recv_sem.at[1],
        device_id=north,
        device_id_type=MESH,
    ).wait_recv()

    @pl.when(lat > 0)
    def _():
        pltpu.make_async_remote_copy(
            src_ref=row_send.at[0],
            dst_ref=row_recv.at[0],
            send_sem=send_sem.at[0],
            recv_sem=recv_sem.at[0],
            device_id=south,
            device_id_type=MESH,
        ).wait_recv()

    row_float = row.astype(jnp.float32)
    for side, edge in ((0, 0), (1, ROWS - 1)):
        there = pl.ds(edge, LEVELS, stride=ROWS)
        own = [field[there] for field in fields]
        other = [row_recv[side, pl.ds(n * LEVELS, LEVELS)] for n in range(FIELDS)]
        own_wet = wet_levels(row, *(plane[edge : edge + 1] for plane in mask_planes))
        other_wet = wet_levels(
            row, *(row_recv[side, pl.ds(MASK_ROW + n, 1)] for n in range(3))
        )
        own_p = summed(half_density(own[0], own[1], own_wet > 0.5, row_float), 0, row)
        other_p = summed(half_density(other[0], other[1], other_wet > 0.5, row_float), 0, row)
        face = own_wet * other_wet > 0.5
        sign = 1.0 if side else -1.0
        a = (sign * FACE) * (own[3] + other[3])
        fixes = (
            -DIFFUSE * edge_faces(own[0], other[0], a, face),
            -DIFFUSE * edge_faces(own[1], other[1], a, face),
            jnp.where(face, VISCOUS * (other[2] - own[2]), 0.0),
            jnp.where(face, VISCOUS * ((other[3] - own[3]) - sign * (other_p - own_p)), 0.0),
        )
        for n, fix in enumerate(fixes):
            to = pl.ds(side * FIELDS + n, LEVELS, stride=EDGE)
            edge_value[to] = fix * edge_inv[to]

    for side, sem in ((0, 2), (1, 3)):
        pltpu.make_async_remote_copy(
            src_ref=col_send.at[side],
            dst_ref=col_recv.at[side],
            send_sem=send_sem.at[sem],
            recv_sem=recv_sem.at[sem],
            device_id=east,
            device_id_type=MESH,
        ).wait_recv()
    level_lane = lax.rem(lane, LEVELS)
    level_lane_float = level_lane.astype(jnp.float32)
    first_group = lane < LEVELS
    fixes = []
    for side in (0, 1):
        own = col_send[side, pl.ds(0, ROWS)]
        other = col_recv[side, pl.ds(0, ROWS)]
        own_mask = col_send[side, pl.ds(ROWS, ROWS)]
        other_mask = col_recv[side, pl.ds(ROWS, ROWS)]
        if side == 0:
            own = pltpu.roll(own, LANES - 1, axis=1)
            own_mask = pltpu.roll(own_mask, LANES - 1, axis=1)
        else:
            other = pltpu.roll(other, LANES - 1, axis=1)
            other_mask = pltpu.roll(other_mask, LANES - 1, axis=1)

        def spread_mask(mask):
            return wet_levels(
                level_lane,
                *(jnp.broadcast_to(mask[:, n : n + 1], (ROWS, LANES)) for n in range(3)),
            )

        own_wet = spread_mask(own_mask)
        other_wet = spread_mask(other_mask)

        def pressure_of(packed, wet):
            half = half_density(
                packed,
                pltpu.roll(packed, LANES - LEVELS, axis=1),
                jnp.logical_and(wet > 0.5, first_group),
                level_lane_float,
            )
            return summed(half, 1, lane)

        jump_p = pressure_of(other, other_wet) - pressure_of(own, own_wet)
        face = own_wet * other_wet > 0.5
        sign = 1.0 if side else -1.0
        both = own + other
        a = (sign * FACE) * jnp.where(
            first_group, pltpu.roll(both, 2 * LEVELS, axis=1), pltpu.roll(both, 3 * LEVELS, axis=1)
        )
        tracers = -DIFFUSE * edge_faces(own, other, a, face)
        jump = other - own
        jump = jnp.where(
            lane < 3 * LEVELS, jump - sign * pltpu.roll(jump_p, 2 * LEVELS, axis=1), jump
        )
        currents = jnp.where(face, VISCOUS * jump, 0.0)
        fixes.append(jnp.where(lane < 2 * LEVELS, tracers, currents))
    turned = side_by_side(*fixes)
    for n in range(FIELDS):
        to = pl.ds(2 * FIELDS + n, LEVELS, stride=EDGE)
        edge_value[to] = turned[n * LEVELS : (n + 1) * LEVELS] * edge_inv[to]

    def edge_level(k):
        return pl.ds(pl.multiple_of(k * EDGE, EDGE), EDGE)

    def edge_forward(k, value):
        here = edge_level(k)
        value = edge_value[here] + edge_down[here] * value
        edge_value[here] = value
        return value

    value = lax.fori_loop(
        0, LEVELS, edge_forward, jnp.zeros((EDGE, LANES), jnp.float32), unroll=8
    )

    def edge_backward(step, value):
        here = edge_level(LEVELS - 2 - step)
        value = edge_value[here] + edge_up[here] * value
        edge_value[here] = value
        return value

    lax.fori_loop(0, LEVELS - 1, edge_backward, value, unroll=8)

    for side, edge in ((0, 0), (1, ROWS - 1)):
        there = pl.ds(edge, LEVELS, stride=ROWS)
        for n in range(FIELDS):
            outs[n][there] += edge_value[pl.ds(side * FIELDS + n, LEVELS, stride=EDGE)]
    for n in range(FIELDS):
        square[pl.ds(n * LEVELS, LEVELS)] = edge_value[pl.ds(2 * FIELDS + n, LEVELS, stride=EDGE)]
    turned = square[...].T
    west_fix = pltpu.roll(turned[:ROWS], 1, axis=1)
    east_fix = turned[ROWS : 2 * ROWS]
    even_lane = lax.rem(lane, 2) == 0
    col_out[pl.ds(0, ROWS)] = jnp.where(even_lane, east_fix, west_fix)
    col_out[pl.ds(ROWS, ROWS)] = jnp.where(even_lane, west_fix, east_fix)

    to_north.wait_send()
    to_east.wait_send()
    to_west.wait_send()

    @pl.when(lat > 0)
    def _():
        to_south.wait_send()


def finish(warm, salt, zonal, merid, col_fix, warm_hbm, salt_hbm, zonal_hbm, merid_hbm, done, sem):
    lane = iota(1)
    edge_lane = jnp.logical_or(lane == 0, lane == LANES - 1)
    sources = (warm, salt, zonal, merid)
    targets = (warm_hbm, salt_hbm, zonal_hbm, merid_hbm)
    stores = []
    for n in range(FIELDS):

        def add(pair, _, n=n):
            for odd in range(2):
                k = 2 * pair + odd
                here = pl.ds(pl.multiple_of(k * ROWS, ROWS), ROWS)
                fix = col_fix[pl.ds(odd * ROWS, ROWS)]
                turned = pltpu.roll(fix, LANES - 1 - n * LEVELS - k, axis=1)
                done[n, here] = sources[n][here] + jnp.where(edge_lane, turned, 0.0)
            return 0

        lax.fori_loop(0, LEVELS // 2, add, 0, unroll=4)
        store = pltpu.make_async_copy(done.at[n], targets[n], sem.at[n])
        store.start()
        stores.append(store)
    for store in stores:
        store.wait()


def result(space, rows):
    return space((rows, LANES), jnp.float32)


def keep_in(x, space):
    return pltpu.with_memory_space_constraint(x, space)


def solution(mesh):
    lat_count = mesh.shape["lat"]
    lon_count = mesh.shape["lon"]

    def step(warm, salt, zonal, merid, mixing, open_water, bottom):
        flat = [x.reshape(CELLS, LANES) for x in (warm, salt, zonal, merid, mixing, open_water)]
        f32 = jnp.float32
        solved = pl.pallas_call(
            functools.partial(kernel, lat_count, lon_count),
            out_shape=[
                *[result(pltpu.VMEM, CELLS)] * FIELDS,
                result(pltpu.VMEM, 2 * ROWS),
            ],
            in_specs=[pl.BlockSpec(memory_space=pl.ANY)] * 7,
            out_specs=[pl.BlockSpec(memory_space=pltpu.VMEM)] * (FIELDS + 1),
            scratch_shapes=[
                *[pltpu.VMEM((CELLS + 8, LANES), f32)] * FIELDS,
                pltpu.VMEM((CELLS, LANES), f32),
                pltpu.VMEM((2 * ROWS, LANES), jnp.int32),
                pltpu.VMEM((ROWS, LANES), jnp.int32),
                pltpu.VMEM((CELLS + ROWS, LANES), f32),
                pltpu.VMEM((CELLS, LANES), f32),
                pltpu.VMEM((CELLS, LANES), f32),
                pltpu.VMEM((2, MASK_ROW + 8, LANES), f32),
                pltpu.VMEM((2, MASK_ROW + 8, LANES), f32),
                pltpu.VMEM((2, 2 * ROWS, LANES), f32),
                pltpu.VMEM((2, 2 * ROWS, LANES), f32),
                *[pltpu.VMEM((LEVELS * EDGE, LANES), f32)] * 4,
                pltpu.VMEM((LANES, LANES), f32),
                pltpu.SemaphoreType.DMA((7,)),
                pltpu.SemaphoreType.DMA((4,)),
                pltpu.SemaphoreType.DMA((4,)),
            ],
            compiler_params=pltpu.CompilerParams(
                collective_id=0, has_side_effects=True, vmem_limit_bytes=16 * 1024 * 1024
            ),
        )(*[keep_in(x, pltpu.HBM) for x in (*flat, bottom)])
        outs = pl.pallas_call(
            finish,
            out_shape=[result(pltpu.HBM, CELLS)] * FIELDS,
            in_specs=[pl.BlockSpec(memory_space=pltpu.VMEM)] * (FIELDS + 1),
            out_specs=[pl.BlockSpec(memory_space=pltpu.HBM)] * FIELDS,
            scratch_shapes=[
                pltpu.VMEM((FIELDS, CELLS, LANES), f32),
                pltpu.SemaphoreType.DMA((FIELDS,)),
            ],
            compiler_params=pltpu.CompilerParams(vmem_limit_bytes=8 * 1024 * 1024),
        )(*[keep_in(x, pltpu.VMEM) for x in solved])
        return tuple(x.reshape(LEVELS, ROWS, LANES) for x in outs)

    tile = P(None, "lat", "lon")
    return jax.shard_map(
        step,
        mesh=mesh,
        in_specs=(tile,) * 6 + (P("lat", "lon"),),
        out_specs=(tile,) * 4,
        check_vma=False,
    )
```

```python
import functools
import math

import jax
import jax.numpy as jnp
from jax import lax
from jax.experimental import pallas as pl
from jax.experimental.pallas import tpu as pltpu
from jax.sharding import PartitionSpec as P

THERMAL_EXPAND = 0.1655
HALINE_CONTRACT = 0.76554
THERMAL_CABBELING = 0.05952
HALINE_CABBELING = 0.00074914
THERMAL_PRESSURE = 0.0001497
HALINE_PRESSURE = 1.109e-05
MIXED_CABBELING = 0.0024341
ADVECT = 0.2
DIFFUSE = 0.08
VISCOUS = 0.08
GRADIENT = 0.1
ROTATION = 0.25
BOTTOM_DRAG = 1.0
OCEAN_DEPTH = 4000.0

MESH = pl.DeviceIdType.MESH
LEVELS = 32
ROWS = 32
LANES = 128
CELLS = LEVELS * ROWS
FIELDS = 4
MASK_ROW = FIELDS * LEVELS
EDGE = 16
UNROLL = 3
FOLD_TURNS = (1, 3, 5, 3, 0, 0, 0, 0)
PRESSURE_SCALE = 0.5 / LEVELS * (0.5 * GRADIENT / VISCOUS)
FACE = 0.25 * ADVECT / DIFFUSE


def half_density(warm, salt, wet, level):
    thermal = warm - 10.0
    haline = salt - 35.0
    depth = (level + 0.5) * (OCEAN_DEPTH / LEVELS)
    s = PRESSURE_SCALE
    by_thermal = -THERMAL_EXPAND * s - (THERMAL_EXPAND * THERMAL_PRESSURE * s) * depth
    by_haline = HALINE_CONTRACT * s - (HALINE_CONTRACT * HALINE_PRESSURE * s) * depth
    value = thermal * (
        by_thermal
        - (0.5 * THERMAL_EXPAND * THERMAL_CABBELING * s) * thermal
        - (MIXED_CABBELING * s) * haline
    ) + haline * (by_haline - (0.5 * HALINE_CONTRACT * HALINE_CABBELING * s) * haline)
    return jnp.where(wet, value, 0.0)


def inverse(x):
    r = pl.reciprocal(x, approx=True)
    return r * (2.0 - x * r)


def iota(axis):
    return lax.broadcasted_iota(jnp.int32, (ROWS, LANES), axis)


def kernel(
    lat_count,
    lon_count,
    warm_hbm,
    salt_hbm,
    zonal_hbm,
    merid_hbm,
    mixing_hbm,
    open_hbm,
    bottom_hbm,
    warm_out,
    salt_out,
    zonal_out,
    merid_out,
    col_out,
    warm,
    salt,
    zonal,
    merid,
    mixing,
    top_open,
    bottom,
    link,
    inv_tracer,
    inv_momentum,
    row_send,
    row_recv,
    col_send,
    col_recv,
    edge_inv,
    edge_down,
    edge_up,
    edge_value,
    square,
    load_sem,
    send_sem,
    recv_sem,
):
    lat = lax.axis_index("lat")
    lon = lax.axis_index("lon")
    is_south = lat == 0
    is_north = lat == lat_count - 1
    east = {"lon": lax.rem(lon + 1, lon_count)}
    west = {"lon": lax.rem(lon + lon_count - 1, lon_count)}
    south = {"lat": jnp.maximum(lat - 1, 0)}
    north_lat = jnp.minimum(lat + 1, lat_count - 1)
    north_lon = jnp.where(is_north, lon_count - 1 - lon, lon)
    north = {"lat": north_lat, "lon": north_lon}
    fields = (warm, salt, zonal, merid)
    outs = (warm_out, salt_out, zonal_out, merid_out)

    span = lon_count // 2
    place = lax.rem(lon, span)
    lat_odd = lax.rem(lat, 2) == 1
    answers_west = place == 0
    fold_late = jnp.logical_and(is_north, place >= span // 2)
    answers_north = jnp.logical_and(lat_odd, jnp.logical_not(fold_late))
    first_west = jnp.logical_not(answers_west)
    first_north = jnp.logical_not(answers_north)

    barrier = pltpu.get_barrier_semaphore()

    def greet(target):
        pl.semaphore_signal(barrier, inc=1, device_id=target, device_id_type=MESH)

    pl.when(jnp.logical_not(fold_late))(lambda: greet(north))
    pl.when(lat_odd)(lambda: greet(south))
    pl.when(place < span - 1)(lambda: greet(east))
    greet(west)
    greetings = (
        1
        + jnp.where(first_west, 1, 0)
        + jnp.where(first_north, 1, 0)
        + jnp.where(is_south, 0, 1)
    )

    loads = [
        pltpu.make_async_copy(src, dst, load_sem.at[n])
        for n, (src, dst) in enumerate(
            (
                (bottom_hbm, bottom),
                (open_hbm.at[pl.ds(0, 2 * ROWS)], top_open),
                (warm_hbm, warm.at[pl.ds(0, CELLS)]),
                (salt_hbm, salt.at[pl.ds(0, CELLS)]),
                (zonal_hbm, zonal.at[pl.ds(0, CELLS)]),
                (merid_hbm, merid.at[pl.ds(0, CELLS)]),
                (mixing_hbm, mixing),
            )
        )
    ]
    for load in loads:
        load.start()

    lane = iota(1)
    row = iota(0)
    nothing = jnp.zeros((ROWS, LANES), jnp.float32)
    for field in fields:
        field[pl.ds(CELLS, 8)] = jnp.zeros((8, LANES), jnp.float32)

    @pl.when(is_south)
    def _():
        row_recv[0] = jnp.zeros((MASK_ROW + 8, LANES), jnp.float32)

    row_global = (lat * ROWS + row).astype(jnp.float32)
    coriolis = ROTATION * jnp.sin(
        math.pi / 180.0 * (-80.0 + 170.0 * (row_global + 0.5) / (ROWS * lat_count))
    )

    def at_level(k):
        return pl.ds(k * ROWS if isinstance(k, int) else pl.multiple_of(k * ROWS, ROWS), ROWS)

    def pack(source, n, sums):
        easts, wests = sums
        for k in range(LEVELS):
            at = n * LEVELS + k
            turned = pltpu.roll(source(k), (at + 1) % LANES, axis=1)
            easts = jnp.where(lane == at, turned, easts)
            wests = jnp.where(lane == (at + 1) % LANES, turned, wests)
        return easts, wests

    loads[0].wait()
    loads[1].wait()
    deep = bottom[...].astype(jnp.float32)
    open0 = top_open[pl.ds(0, ROWS)].astype(jnp.float32)
    open1 = top_open[pl.ds(ROWS, ROWS)].astype(jnp.float32)
    mask_planes = (deep, open0, open1)
    for side, edge in ((0, 0), (1, ROWS - 1)):
        for n, plane in enumerate(mask_planes):
            row_send[side, pl.ds(MASK_ROW + n, 1)] = plane[edge : edge + 1]
        row_send[side, pl.ds(MASK_ROW + 3, 5)] = jnp.zeros((5, LANES), jnp.float32)
    east_masks = nothing
    west_masks = nothing
    for n, plane in enumerate(mask_planes):
        turned = pltpu.roll(plane, n + 1, axis=1)
        east_masks = jnp.where(lane == n, turned, east_masks)
        west_masks = jnp.where(lane == n + 1, turned, west_masks)
    col_send[1, pl.ds(ROWS, ROWS)] = east_masks
    col_send[0, pl.ds(ROWS, ROWS)] = west_masks
    packed = (nothing, nothing)
    for n, field in enumerate(fields):
        loads[2 + n].wait()
        for side, edge in ((0, 0), (1, ROWS - 1)):
            row_send[side, pl.ds(n * LEVELS, LEVELS)] = field[pl.ds(edge, LEVELS, stride=ROWS)]
        packed = pack(lambda k, field=field: field[at_level(k)], n, packed)
    col_send[1, pl.ds(0, ROWS)] = packed[0]
    col_send[0, pl.ds(0, ROWS)] = packed[1]

    @pl.when(is_north)
    def _():
        flip = (LANES - 1) - lax.broadcasted_iota(jnp.int32, (8, LANES), 1)
        for tile in range((MASK_ROW + 8) // 8):
            there = pl.ds(tile * 8, 8)
            turned = jnp.take_along_axis(row_send[1, there], flip, axis=1)
            if 2 * LEVELS <= tile * 8 < 4 * LEVELS:
                turned = -turned
            row_send[1, there] = turned

    to_north = pltpu.make_async_remote_copy(
        src_ref=row_send.at[1],
        dst_ref=row_recv.at[jnp.where(is_north, 1, 0)],
        send_sem=send_sem.at[1],
        recv_sem=recv_sem.at[jnp.where(is_north, 1, 0)],
        device_id=north,
        device_id_type=MESH,
    )
    to_south = pltpu.make_async_remote_copy(
        src_ref=row_send.at[0],
        dst_ref=row_recv.at[1],
        send_sem=send_sem.at[0],
        recv_sem=recv_sem.at[1],
        device_id=south,
        device_id_type=MESH,
    )
    to_east = pltpu.make_async_remote_copy(
        src_ref=col_send.at[1],
        dst_ref=col_recv.at[0],
        send_sem=send_sem.at[3],
        recv_sem=recv_sem.at[2],
        device_id=east,
        device_id_type=MESH,
    )
    to_west = pltpu.make_async_remote_copy(
        src_ref=col_send.at[0],
        dst_ref=col_recv.at[1],
        send_sem=send_sem.at[2],
        recv_sem=recv_sem.at[3],
        device_id=west,
        device_id_type=MESH,
    )
    pl.semaphore_wait(barrier, greetings)
    north_turn = 0
    for n, turn in enumerate(FOLD_TURNS):
        north_turn = jnp.where(jnp.logical_and(fold_late, place == span - 1 - n), turn, north_turn)
    to_east.start()
    pl.when(first_west)(to_west.start)
    pl.when(jnp.logical_and(first_north, north_turn == 0))(to_north.start)
    pl.when(lat > 0)(to_south.start)

    def side_by_side(wests, easts):
        square[pl.ds(0, ROWS)] = wests
        square[pl.ds(ROWS, ROWS)] = easts
        square[pl.ds(2 * ROWS, ROWS)] = nothing
        square[pl.ds(3 * ROWS, ROWS)] = nothing
        return square[...].T

    loads[6].wait()
    depth_here = bottom[...]
    not_east = lane < LANES - 1
    not_north = row < ROWS - 1
    depth_east = jnp.where(
        not_east, jnp.minimum(depth_here, pltpu.roll(depth_here, LANES - 1, axis=1)), 0
    )
    depth_north = jnp.where(
        not_north, jnp.minimum(depth_here, pltpu.roll(depth_here, ROWS - 1, axis=0)), 0
    )
    link[pl.ds(0, ROWS)] = nothing

    def level(k, masks, carried):
        above, g_above, pressure_sum = carried
        wet, wet_east, wet_north, wet_below = masks
        k_float = jnp.asarray(k, jnp.int32).astype(jnp.float32)
        start = k * ROWS
        here = pl.ds(start if isinstance(k, int) else pl.multiple_of(start, ROWS), ROWS)
        shifted = pl.ds(start + 1, ROWS)
        t, s, u, v = (field[here] for field in fields)
        t_n, s_n, u_n, v_n = (field[shifted] for field in fields)
        t_e, s_e, u_e, v_e = (pltpu.roll(x, LANES - 1, axis=1) for x in (t, s, u, v))

        half = half_density(t, s, wet, k_float)
        pressure = pressure_sum + half
        pressure_sum = pressure + half
        p_e = pltpu.roll(pressure, LANES - 1, axis=1)
        p_n = pltpu.roll(pressure, ROWS - 1, axis=0)

        a_e = FACE * (u + u_e)
        a_n = FACE * (v + v_n)
        ahead_e = jnp.where(wet_east, a_e - 1.0, 0.0)
        behind_e = jnp.where(wet_east, a_e + 1.0, 0.0)
        ahead_n = jnp.where(wet_north, a_n - 1.0, 0.0)
        behind_n = jnp.where(wet_north, a_n + 1.0, 0.0)

        def spread(f_e, f_n):
            return (f_e - pltpu.roll(f_e, 1, axis=1)) + (f_n - pltpu.roll(f_n, 1, axis=0))

        def tracer(q, q_e, q_n):
            f_e = ahead_e * q_e + behind_e * q
            f_n = ahead_n * q_n + behind_n * q
            return jnp.where(wet, q - DIFFUSE * spread(f_e, f_n), 0.0)

        warm_out[here] = tracer(t, t_e, t_n)
        salt_out[here] = tracer(s, s_e, s_n)

        du_e = jnp.where(wet_east, u_e - u, 0.0)
        dp_e = jnp.where(wet_east, p_e - pressure, 0.0)
        du_n = jnp.where(wet_north, u_n - u, 0.0)
        lap_u = ((du_e - dp_e) - pltpu.roll(du_e + dp_e, 1, axis=1)) + (
            du_n - pltpu.roll(du_n, 1, axis=0)
        )
        zonal_out[here] = jnp.where(wet, u + VISCOUS * lap_u + coriolis * v, 0.0)
        dv_n = jnp.where(wet_north, v_n - v, 0.0)
        dp_n = jnp.where(wet_north, p_n - pressure, 0.0)
        dv_e = jnp.where(wet_east, v_e - v, 0.0)
        lap_v = ((dv_n - dp_n) - pltpu.roll(dv_n + dp_n, 1, axis=0)) + (
            dv_e - pltpu.roll(dv_e, 1, axis=1)
        )
        merid_out[here] = jnp.where(wet, v + VISCOUS * lap_v - coriolis * u, 0.0)

        below = jnp.where(wet_below, mixing[here], 0.0)
        diagonal = (1.0 + below) + above * (1.0 - g_above)
        inv = inverse(diagonal)
        dragged = jnp.logical_and(depth_here == k + 1, wet)
        inv_m = inverse(diagonal + jnp.where(dragged, BOTTOM_DRAG, 0.0))
        link[pl.ds(start + ROWS, ROWS)] = below
        inv_tracer[here] = inv
        inv_momentum[here] = inv_m
        return below, below * inv, pressure_sum

    def open_pair(plane):
        wet = plane > 0.5
        wet_east = jnp.where(not_east, plane * pltpu.roll(plane, LANES - 1, axis=1), 0.0) > 0.5
        wet_north = jnp.where(not_north, plane * pltpu.roll(plane, ROWS - 1, axis=0), 0.0) > 0.5
        return wet, wet_east, wet_north

    carried = (nothing, nothing, nothing)
    carried = level(0, open_pair(open0) + (open0 * open1 > 0.5,), carried)
    carried = level(
        1,
        open_pair(open1) + (jnp.logical_and(open1 > 0.5, depth_here > 2),),
        carried,
    )

    def deeper(k, carried):
        masks = (depth_here > k, depth_east > k, depth_north > k, depth_here > k + 1)
        return level(k, masks, carried)

    def group(step, carried):
        pl.when(jnp.logical_and(first_north, north_turn == step + 1))(to_north.start)
        for n in range(UNROLL):
            carried = deeper(2 + UNROLL * step + n, carried)
        return carried

    lax.fori_loop(0, (LEVELS - 2) // UNROLL, group, carried)

    def forward(k, values):
        here = at_level(k)
        above = link[here]
        invs = (inv_tracer[here], inv_momentum[here])
        new = []
        for n in range(FIELDS):
            value = (outs[n][here] + above * values[n]) * invs[n // 2]
            outs[n][here] = value
            new.append(value)
        return tuple(new)

    values = lax.fori_loop(0, LEVELS, forward, (nothing,) * 4, unroll=2)

    def backward(step, values):
        k = LEVELS - 2 - step
        here = at_level(k)
        ratio = link[at_level(k + 1)] * inv_tracer[here]
        new = []
        for n in range(FIELDS):
            value = outs[n][here] + ratio * values[n]
            outs[n][here] = value
            new.append(value)
        return tuple(new)

    lax.fori_loop(0, LEVELS - 1, backward, values, unroll=2)

    for side, edge in ((0, 0), (1, ROWS - 1)):
        there = pl.ds(edge, LEVELS, stride=ROWS)
        above = link[there]
        below = link[pl.ds(ROWS + edge, LEVELS, stride=ROWS)]
        inv_t = inv_tracer[there]
        inv_m = inv_momentum[there]
        up = below * inv_t
        for n in range(FIELDS):
            to = pl.ds(side * FIELDS + n, LEVELS, stride=EDGE)
            edge_inv[to] = inv_m if n > 1 else inv_t
            edge_down[to] = above * (inv_m if n > 1 else inv_t)
            edge_up[to] = up
    packed = (nothing, nothing)
    packed = pack(lambda k: link[at_level(k)], 0, packed)
    packed = pack(lambda k: inv_tracer[at_level(k)], 1, packed)
    packed = pack(lambda k: inv_momentum[at_level(k)], 2, packed)
    packed = pack(lambda k: link[at_level(k + 1)], 3, packed)

    coefs = side_by_side(pltpu.roll(packed[1], LANES - 1, axis=1), packed[0])
    above, inv_t, inv_m, below = (coefs[n * LEVELS : (n + 1) * LEVELS] for n in range(4))
    for n in range(FIELDS):
        to = pl.ds(2 * FIELDS + n, LEVELS, stride=EDGE)
        edge_inv[to] = inv_m if n > 1 else inv_t
        edge_down[to] = above * (inv_m if n > 1 else inv_t)
        edge_up[to] = below * inv_t
        spare = pl.ds(3 * FIELDS + n, LEVELS, stride=EDGE)
        edge_down[spare] = nothing
        edge_up[spare] = nothing
        edge_value[spare] = nothing

    def wet_levels(level_index, depth, first, second):
        return jnp.where(
            level_index == 0,
            first,
            jnp.where(
                level_index == 1,
                second,
                jnp.where(level_index.astype(jnp.float32) < depth, 1.0, 0.0),
            ),
        )

    def summed(half, axis, index):
        total = half
        for step in (1, 2, 4, 8, 16):
            total = total + jnp.where(index >= step, pltpu.roll(total, step, axis=axis), 0.0)
        return 2.0 * total - half

    def edge_faces(q, q_o, a, face):
        return jnp.where(face, (a - 1.0) * q_o + (a + 1.0) * q, 0.0)

    def arrival(source, target, slot, sem):
        return pltpu.make_async_remote_copy(
            src_ref=source.at[slot],
            dst_ref=target.at[slot],
            send_sem=send_sem.at[sem],
            recv_sem=recv_sem.at[sem],
            device_id=east,
            device_id_type=MESH,
        )

    from_south = arrival(row_send, row_recv, 0, 0)
    from_north = arrival(row_send, row_recv, 1, 1)
    from_west = arrival(col_send, col_recv, 0, 2)
    from_east = arrival(col_send, col_recv, 1, 3)

    row_float = row.astype(jnp.float32)
    row_edges = []
    for side, edge in ((0, 0), (1, ROWS - 1)):
        own = [field[pl.ds(edge, LEVELS, stride=ROWS)] for field in fields]
        wet = wet_levels(row, *(plane[edge : edge + 1] for plane in mask_planes))
        pressure = summed(half_density(own[0], own[1], wet > 0.5, row_float), 0, row)
        row_edges.append((own, wet, pressure))

    level_lane = lax.rem(lane, LEVELS)
    level_lane_float = level_lane.astype(jnp.float32)
    first_group = lane < LEVELS

    def spread_mask(mask):
        return wet_levels(
            level_lane,
            *(jnp.broadcast_to(mask[:, n : n + 1], (ROWS, LANES)) for n in range(3)),
        )

    def pressure_of(packed, wet):
        half = half_density(
            packed,
            pltpu.roll(packed, LANES - LEVELS, axis=1),
            jnp.logical_and(wet > 0.5, first_group),
            level_lane_float,
        )
        return summed(half, 1, lane)

    col_edges = []
    for side in (0, 1):
        own = col_send[side, pl.ds(0, ROWS)]
        mask = col_send[side, pl.ds(ROWS, ROWS)]
        if side == 0:
            own = pltpu.roll(own, LANES - 1, axis=1)
            mask = pltpu.roll(mask, LANES - 1, axis=1)
        wet = spread_mask(mask)
        col_edges.append((own, wet, pressure_of(own, wet)))

    @pl.when(answers_north)
    def _():
        from_north.wait_recv()
        to_north.start()

    pl.when(first_north)(from_north.wait_recv)
    pl.when(lat > 0)(from_south.wait_recv)

    for side in (0, 1):
        own, own_wet, own_p = row_edges[side]
        other = [row_recv[side, pl.ds(n * LEVELS, LEVELS)] for n in range(FIELDS)]
        other_wet = wet_levels(
            row, *(row_recv[side, pl.ds(MASK_ROW + n, 1)] for n in range(3))
        )
        other_p = summed(half_density(other[0], other[1], other_wet > 0.5, row_float), 0, row)
        face = own_wet * other_wet > 0.5
        sign = 1.0 if side else -1.0
        a = (sign * FACE) * (own[3] + other[3])
        fixes = (
            -DIFFUSE * edge_faces(own[0], other[0], a, face),
            -DIFFUSE * edge_faces(own[1], other[1], a, face),
            jnp.where(face, VISCOUS * (other[2] - own[2]), 0.0),
            jnp.where(face, VISCOUS * ((other[3] - own[3]) - sign * (other_p - own_p)), 0.0),
        )
        for n, fix in enumerate(fixes):
            to = pl.ds(side * FIELDS + n, LEVELS, stride=EDGE)
            edge_value[to] = fix * edge_inv[to]

    from_east.wait_recv()

    @pl.when(answers_west)
    def _():
        from_west.wait_recv()
        to_west.start()

    pl.when(first_west)(from_west.wait_recv)

    fixes = []
    for side in (0, 1):
        own, own_wet, own_p = col_edges[side]
        other = col_recv[side, pl.ds(0, ROWS)]
        other_mask = col_recv[side, pl.ds(ROWS, ROWS)]
        if side == 1:
            other = pltpu.roll(other, LANES - 1, axis=1)
            other_mask = pltpu.roll(other_mask, LANES - 1, axis=1)
        other_wet = spread_mask(other_mask)
        jump_p = pressure_of(other, other_wet) - own_p
        face = own_wet * other_wet > 0.5
        sign = 1.0 if side else -1.0
        both = own + other
        a = (sign * FACE) * jnp.where(
            first_group, pltpu.roll(both, 2 * LEVELS, axis=1), pltpu.roll(both, 3 * LEVELS, axis=1)
        )
        tracers = -DIFFUSE * edge_faces(own, other, a, face)
        jump = other - own
        jump = jnp.where(
            lane < 3 * LEVELS, jump - sign * pltpu.roll(jump_p, 2 * LEVELS, axis=1), jump
        )
        currents = jnp.where(face, VISCOUS * jump, 0.0)
        fixes.append(jnp.where(lane < 2 * LEVELS, tracers, currents))
    turned = side_by_side(*fixes)
    for n in range(FIELDS):
        to = pl.ds(2 * FIELDS + n, LEVELS, stride=EDGE)
        edge_value[to] = turned[n * LEVELS : (n + 1) * LEVELS] * edge_inv[to]

    def edge_level(k):
        return pl.ds(pl.multiple_of(k * EDGE, EDGE), EDGE)

    def edge_forward(k, value):
        here = edge_level(k)
        value = edge_value[here] + edge_down[here] * value
        edge_value[here] = value
        return value

    value = lax.fori_loop(
        0, LEVELS, edge_forward, jnp.zeros((EDGE, LANES), jnp.float32), unroll=8
    )

    def edge_backward(step, value):
        here = edge_level(LEVELS - 2 - step)
        value = edge_value[here] + edge_up[here] * value
        edge_value[here] = value
        return value

    lax.fori_loop(0, LEVELS - 1, edge_backward, value, unroll=8)

    for side, edge in ((0, 0), (1, ROWS - 1)):
        there = pl.ds(edge, LEVELS, stride=ROWS)
        for n in range(FIELDS):
            outs[n][there] += edge_value[pl.ds(side * FIELDS + n, LEVELS, stride=EDGE)]
    for n in range(FIELDS):
        square[pl.ds(n * LEVELS, LEVELS)] = edge_value[pl.ds(2 * FIELDS + n, LEVELS, stride=EDGE)]
    turned = square[...].T
    west_fix = pltpu.roll(turned[:ROWS], 1, axis=1)
    east_fix = turned[ROWS : 2 * ROWS]
    even_lane = lax.rem(lane, 2) == 0
    col_out[pl.ds(0, ROWS)] = jnp.where(even_lane, east_fix, west_fix)
    col_out[pl.ds(ROWS, ROWS)] = jnp.where(even_lane, west_fix, east_fix)

    to_north.wait_send()
    to_east.wait_send()
    to_west.wait_send()

    @pl.when(lat > 0)
    def _():
        to_south.wait_send()


def finish(warm, salt, zonal, merid, col_fix, warm_hbm, salt_hbm, zonal_hbm, merid_hbm, done, sem):
    lane = iota(1)
    edge_lane = jnp.logical_or(lane == 0, lane == LANES - 1)
    sources = (warm, salt, zonal, merid)
    targets = (warm_hbm, salt_hbm, zonal_hbm, merid_hbm)
    stores = []
    for n in range(FIELDS):

        for k in range(LEVELS):
            here = pl.ds(k * ROWS, ROWS)
            fix = col_fix[pl.ds(k % 2 * ROWS, ROWS)]
            turned = pltpu.roll(fix, LANES - 1 - n * LEVELS - k, axis=1)
            done[n, here] = sources[n][here] + jnp.where(edge_lane, turned, 0.0)
        store = pltpu.make_async_copy(done.at[n], targets[n], sem.at[n])
        store.start()
        stores.append(store)
    for store in stores:
        store.wait()


def result(space, rows):
    return space((rows, LANES), jnp.float32)


def keep_in(x, space):
    return pltpu.with_memory_space_constraint(x, space)


def solution(mesh):
    lat_count = mesh.shape["lat"]
    lon_count = mesh.shape["lon"]

    def step(warm, salt, zonal, merid, mixing, open_water, bottom):
        flat = [x.reshape(CELLS, LANES) for x in (warm, salt, zonal, merid, mixing, open_water)]
        f32 = jnp.float32
        solved = pl.pallas_call(
            functools.partial(kernel, lat_count, lon_count),
            out_shape=[
                *[result(pltpu.VMEM, CELLS)] * FIELDS,
                result(pltpu.VMEM, 2 * ROWS),
            ],
            in_specs=[pl.BlockSpec(memory_space=pl.ANY)] * 7,
            out_specs=[pl.BlockSpec(memory_space=pltpu.VMEM)] * (FIELDS + 1),
            scratch_shapes=[
                *[pltpu.VMEM((CELLS + 8, LANES), f32)] * FIELDS,
                pltpu.VMEM((CELLS, LANES), f32),
                pltpu.VMEM((2 * ROWS, LANES), jnp.int32),
                pltpu.VMEM((ROWS, LANES), jnp.int32),
                pltpu.VMEM((CELLS + ROWS, LANES), f32),
                pltpu.VMEM((CELLS, LANES), f32),
                pltpu.VMEM((CELLS, LANES), f32),
                pltpu.VMEM((2, MASK_ROW + 8, LANES), f32),
                pltpu.VMEM((2, MASK_ROW + 8, LANES), f32),
                pltpu.VMEM((2, 2 * ROWS, LANES), f32),
                pltpu.VMEM((2, 2 * ROWS, LANES), f32),
                *[pltpu.VMEM((LEVELS * EDGE, LANES), f32)] * 4,
                pltpu.VMEM((LANES, LANES), f32),
                pltpu.SemaphoreType.DMA((7,)),
                pltpu.SemaphoreType.DMA((4,)),
                pltpu.SemaphoreType.DMA((4,)),
            ],
            compiler_params=pltpu.CompilerParams(
                collective_id=0, has_side_effects=True, vmem_limit_bytes=16 * 1024 * 1024
            ),
        )(*[keep_in(x, pltpu.HBM) for x in (*flat, bottom)])
        outs = pl.pallas_call(
            finish,
            out_shape=[result(pltpu.HBM, CELLS)] * FIELDS,
            in_specs=[pl.BlockSpec(memory_space=pltpu.VMEM)] * (FIELDS + 1),
            out_specs=[pl.BlockSpec(memory_space=pltpu.HBM)] * FIELDS,
            scratch_shapes=[
                pltpu.VMEM((FIELDS, CELLS, LANES), f32),
                pltpu.SemaphoreType.DMA((FIELDS,)),
            ],
            compiler_params=pltpu.CompilerParams(vmem_limit_bytes=8 * 1024 * 1024),
        )(*[keep_in(x, pltpu.VMEM) for x in solved])
        return tuple(x.reshape(LEVELS, ROWS, LANES) for x in outs)

    tile = P(None, "lat", "lon")
    return jax.shard_map(
        step,
        mesh=mesh,
        in_specs=(tile,) * 6 + (P("lat", "lon"),),
        out_specs=(tile,) * 4,
        check_vma=False,
    )
```

```python
import functools
import math

import jax
import jax.numpy as jnp
from jax import lax
from jax.experimental import pallas as pl
from jax.experimental.pallas import tpu as pltpu
from jax.sharding import PartitionSpec as P

THERMAL_EXPAND = 0.1655
HALINE_CONTRACT = 0.76554
THERMAL_CABBELING = 0.05952
HALINE_CABBELING = 0.00074914
THERMAL_PRESSURE = 0.0001497
HALINE_PRESSURE = 1.109e-05
MIXED_CABBELING = 0.0024341
ADVECT = 0.2
DIFFUSE = 0.08
VISCOUS = 0.08
GRADIENT = 0.1
ROTATION = 0.25
BOTTOM_DRAG = 1.0
OCEAN_DEPTH = 4000.0

MESH = pl.DeviceIdType.MESH
LEVELS = 32
ROWS = 32
LANES = 128
CELLS = LEVELS * ROWS
FIELDS = 4
MASK_ROW = FIELDS * LEVELS
EDGE = 16
UNROLL = 3
BLOCK = 4
FOLD_TURNS = (0, 1, 3, 5, 0, 0, 0, 0)
PRESSURE_SCALE = 0.5 / LEVELS * (0.5 * GRADIENT / VISCOUS)
FACE = 0.25 * ADVECT / DIFFUSE


def half_density(warm, salt, wet, level):
    thermal = warm - 10.0
    haline = salt - 35.0
    depth = (level + 0.5) * (OCEAN_DEPTH / LEVELS)
    s = PRESSURE_SCALE
    by_thermal = -THERMAL_EXPAND * s - (THERMAL_EXPAND * THERMAL_PRESSURE * s) * depth
    by_haline = HALINE_CONTRACT * s - (HALINE_CONTRACT * HALINE_PRESSURE * s) * depth
    value = thermal * (
        by_thermal
        - (0.5 * THERMAL_EXPAND * THERMAL_CABBELING * s) * thermal
        - (MIXED_CABBELING * s) * haline
    ) + haline * (by_haline - (0.5 * HALINE_CONTRACT * HALINE_CABBELING * s) * haline)
    return jnp.where(wet, value, 0.0)


def inverse(x):
    r = pl.reciprocal(x, approx=True)
    return r * (2.0 - x * r)


def iota(axis):
    return lax.broadcasted_iota(jnp.int32, (ROWS, LANES), axis)


def kernel(
    lat_count,
    lon_count,
    warm_hbm,
    salt_hbm,
    zonal_hbm,
    merid_hbm,
    mixing_hbm,
    open_hbm,
    bottom_hbm,
    warm_out,
    salt_out,
    zonal_out,
    merid_out,
    col_out,
    edge_value,
    warm,
    salt,
    zonal,
    merid,
    mixing,
    top_open,
    bottom,
    link,
    inv_tracer,
    inv_momentum,
    row_send,
    row_recv,
    col_send,
    col_recv,
    edge_inv,
    edge_down,
    edge_up,
    edge_down_block,
    edge_up_block,
    edge_half,
    edge_weight,
    load_sem,
    send_sem,
    recv_sem,
    go_west,
    go_north,
):
    lat = lax.axis_index("lat")
    lon = lax.axis_index("lon")
    is_south = lat == 0
    is_north = lat == lat_count - 1
    east = {"lon": lax.rem(lon + 1, lon_count)}
    west = {"lon": lax.rem(lon + lon_count - 1, lon_count)}
    south = {"lat": jnp.maximum(lat - 1, 0)}
    north_lat = jnp.minimum(lat + 1, lat_count - 1)
    north_lon = jnp.where(is_north, lon_count - 1 - lon, lon)
    north = {"lat": north_lat, "lon": north_lon}
    fields = (warm, salt, zonal, merid)
    outs = (warm_out, salt_out, zonal_out, merid_out)

    span = lon_count // 2
    place = lax.rem(lon, span)
    is_last = place == span - 1
    lat_odd = lax.rem(lat, 2) == 1
    answers_west = jnp.logical_or(place == 0, is_last)
    fold_late = jnp.logical_and(is_north, place >= span // 2)
    answers_north = jnp.logical_and(lat_odd, jnp.logical_not(fold_late))
    first_west = jnp.logical_not(answers_west)
    first_north = jnp.logical_not(answers_north)

    barrier = pltpu.get_barrier_semaphore()

    def greet(target):
        pl.semaphore_signal(barrier, inc=1, device_id=target, device_id_type=MESH)

    pl.when(jnp.logical_not(fold_late))(lambda: greet(north))
    pl.when(lat_odd)(lambda: greet(south))
    pl.when(place < span - 2)(lambda: greet(east))
    greet(west)
    greetings = (
        1
        + jnp.where(first_west, 1, 0)
        + jnp.where(first_north, 1, 0)
        + jnp.where(is_south, 0, 1)
    )

    meets_early = jnp.logical_and(is_last, lax.rem(lat, 4) != 0)

    def meet():
        pl.semaphore_wait(barrier, greetings)

        def go(sem, target):
            pl.semaphore_signal(sem, inc=1, device_id=target, device_id_type=MESH)

        pl.when(place >= span - 2)(lambda: go(go_west, east))
        pl.when(jnp.logical_and(jnp.logical_not(lat_odd), lat > 0))(lambda: go(go_north, south))
        pl.when(fold_late)(lambda: go(go_north, north))

    loads = [
        pltpu.make_async_copy(src, dst, load_sem.at[n])
        for n, (src, dst) in enumerate(
            (
                (bottom_hbm, bottom),
                (open_hbm.at[pl.ds(0, 2 * ROWS)], top_open),
                (warm_hbm, warm.at[pl.ds(0, CELLS)]),
                (salt_hbm, salt.at[pl.ds(0, CELLS)]),
                (zonal_hbm, zonal.at[pl.ds(0, CELLS)]),
                (merid_hbm, merid.at[pl.ds(0, CELLS)]),
                (mixing_hbm, mixing),
            )
        )
    ]
    for load in loads[:6]:
        load.start()

    lane = iota(1)
    row = iota(0)
    nothing = jnp.zeros((ROWS, LANES), jnp.float32)
    for field in fields:
        field[pl.ds(CELLS, 8)] = jnp.zeros((8, LANES), jnp.float32)

    @pl.when(is_south)
    def _():
        row_recv[0] = jnp.zeros((MASK_ROW + 8, LANES), jnp.float32)

    row_global = (lat * ROWS + row).astype(jnp.float32)
    coriolis = ROTATION * jnp.sin(
        math.pi / 180.0 * (-80.0 + 170.0 * (row_global + 0.5) / (ROWS * lat_count))
    )

    def at_level(k):
        return pl.ds(k * ROWS if isinstance(k, int) else pl.multiple_of(k * ROWS, ROWS), ROWS)

    def pack(source, n, sums):
        easts, wests = sums
        for k in range(LEVELS):
            at = n * LEVELS + k
            turned = pltpu.roll(source(k), (at + 1) % LANES, axis=1)
            easts = jnp.where(lane == at, turned, easts)
            wests = jnp.where(lane == (at + 1) % LANES, turned, wests)
        return easts, wests

    pl.when(meets_early)(meet)
    loads[0].wait()
    loads[1].wait()
    deep = bottom[...].astype(jnp.float32)
    open0 = top_open[pl.ds(0, ROWS)].astype(jnp.float32)
    open1 = top_open[pl.ds(ROWS, ROWS)].astype(jnp.float32)
    mask_planes = (deep, open0, open1)
    for side, edge in ((0, 0), (1, ROWS - 1)):
        for n, plane in enumerate(mask_planes):
            row_send[side, pl.ds(MASK_ROW + n, 1)] = plane[edge : edge + 1]
        row_send[side, pl.ds(MASK_ROW + 3, 5)] = jnp.zeros((5, LANES), jnp.float32)
    east_masks = nothing
    west_masks = nothing
    for n, plane in enumerate(mask_planes):
        turned = pltpu.roll(plane, n + 1, axis=1)
        east_masks = jnp.where(lane == n, turned, east_masks)
        west_masks = jnp.where(lane == n + 1, turned, west_masks)
    west_masks = pltpu.roll(west_masks, LANES - 1, axis=1)
    turned = jnp.concatenate([east_masks, west_masks, west_masks, east_masks], axis=0).T[:8]
    col_send[1, pl.ds(ROWS, 8)] = turned
    col_send[0, pl.ds(ROWS, 8)] = turned
    own_planes = pltpu.roll(turned, LANES - 2 * ROWS, axis=1)
    packed = (nothing, nothing)
    for n, field in enumerate(fields):
        loads[2 + n].wait()
        if n == 1:
            loads[6].start()
        for side, edge in ((0, 0), (1, ROWS - 1)):
            row_send[side, pl.ds(n * LEVELS, LEVELS)] = field[pl.ds(edge, LEVELS, stride=ROWS)]
        packed = pack(lambda k, field=field: field[at_level(k)], n, packed)
    col_send[1, pl.ds(0, ROWS)] = packed[0]
    col_send[0, pl.ds(0, ROWS)] = pltpu.roll(packed[1], LANES - 1, axis=1)

    @pl.when(is_north)
    def _():
        flip = (LANES - 1) - lax.broadcasted_iota(jnp.int32, (8, LANES), 1)
        for tile in range((MASK_ROW + 8) // 8):
            there = pl.ds(tile * 8, 8)
            turned = jnp.take_along_axis(row_send[1, there], flip, axis=1)
            if 2 * LEVELS <= tile * 8 < 4 * LEVELS:
                turned = -turned
            row_send[1, there] = turned

    to_north = pltpu.make_async_remote_copy(
        src_ref=row_send.at[1],
        dst_ref=row_recv.at[jnp.where(is_north, 1, 0)],
        send_sem=send_sem.at[1],
        recv_sem=recv_sem.at[jnp.where(is_north, 1, 0)],
        device_id=north,
        device_id_type=MESH,
    )
    to_south = pltpu.make_async_remote_copy(
        src_ref=row_send.at[0],
        dst_ref=row_recv.at[1],
        send_sem=send_sem.at[0],
        recv_sem=recv_sem.at[1],
        device_id=south,
        device_id_type=MESH,
    )
    to_east = pltpu.make_async_remote_copy(
        src_ref=col_send.at[1],
        dst_ref=col_recv.at[0],
        send_sem=send_sem.at[3],
        recv_sem=recv_sem.at[2],
        device_id=east,
        device_id_type=MESH,
    )
    to_west = pltpu.make_async_remote_copy(
        src_ref=col_send.at[0],
        dst_ref=col_recv.at[1],
        send_sem=send_sem.at[2],
        recv_sem=recv_sem.at[3],
        device_id=west,
        device_id_type=MESH,
    )
    pl.when(jnp.logical_not(meets_early))(meet)
    north_turn = 0
    for n, turn in enumerate(FOLD_TURNS):
        north_turn = jnp.where(jnp.logical_and(fold_late, place == span - 1 - n), turn, north_turn)
    to_east.start()
    pl.when(first_west)(to_west.start)
    pl.when(jnp.logical_and(first_north, north_turn == 0))(to_north.start)
    pl.when(lat > 0)(to_south.start)

    def levels_first(wests, easts):
        return jnp.concatenate([wests, easts, nothing, nothing], axis=0).T

    loads[6].wait()
    depth_here = bottom[...]
    not_east = lane < LANES - 1
    not_north = row < ROWS - 1
    depth_east = jnp.where(
        not_east, jnp.minimum(depth_here, pltpu.roll(depth_here, LANES - 1, axis=1)), 0
    )
    depth_north = jnp.where(
        not_north, jnp.minimum(depth_here, pltpu.roll(depth_here, ROWS - 1, axis=0)), 0
    )
    link[pl.ds(0, ROWS)] = nothing

    def level(k, masks, carried):
        above, g_above, pressure_sum = carried
        wet, wet_east, wet_north, wet_below = masks
        k_float = jnp.asarray(k, jnp.int32).astype(jnp.float32)
        start = k * ROWS
        here = pl.ds(start if isinstance(k, int) else pl.multiple_of(start, ROWS), ROWS)
        shifted = pl.ds(start + 1, ROWS)
        t, s, u, v = (field[here] for field in fields)
        t_n, s_n, u_n, v_n = (field[shifted] for field in fields)
        t_e, s_e, u_e, v_e = (pltpu.roll(x, LANES - 1, axis=1) for x in (t, s, u, v))

        half = half_density(t, s, wet, k_float)
        pressure = pressure_sum + half
        pressure_sum = pressure + half
        p_e = pltpu.roll(pressure, LANES - 1, axis=1)
        p_n = pltpu.roll(pressure, ROWS - 1, axis=0)

        a_e = FACE * (u + u_e)
        a_n = FACE * (v + v_n)
        ahead_e = jnp.where(wet_east, a_e - 1.0, 0.0)
        behind_e = jnp.where(wet_east, a_e + 1.0, 0.0)
        ahead_n = jnp.where(wet_north, a_n - 1.0, 0.0)
        behind_n = jnp.where(wet_north, a_n + 1.0, 0.0)

        def spread(f_e, f_n):
            return (f_e - pltpu.roll(f_e, 1, axis=1)) + (f_n - pltpu.roll(f_n, 1, axis=0))

        def tracer(q, q_e, q_n):
            f_e = ahead_e * q_e + behind_e * q
            f_n = ahead_n * q_n + behind_n * q
            return jnp.where(wet, q - DIFFUSE * spread(f_e, f_n), 0.0)

        warm_out[here] = tracer(t, t_e, t_n)
        salt_out[here] = tracer(s, s_e, s_n)

        du_e = jnp.where(wet_east, u_e - u, 0.0)
        dp_e = jnp.where(wet_east, p_e - pressure, 0.0)
        du_n = jnp.where(wet_north, u_n - u, 0.0)
        lap_u = ((du_e - dp_e) - pltpu.roll(du_e + dp_e, 1, axis=1)) + (
            du_n - pltpu.roll(du_n, 1, axis=0)
        )
        zonal_out[here] = jnp.where(wet, u + VISCOUS * lap_u + coriolis * v, 0.0)
        dv_n = jnp.where(wet_north, v_n - v, 0.0)
        dp_n = jnp.where(wet_north, p_n - pressure, 0.0)
        dv_e = jnp.where(wet_east, v_e - v, 0.0)
        lap_v = ((dv_n - dp_n) - pltpu.roll(dv_n + dp_n, 1, axis=0)) + (
            dv_e - pltpu.roll(dv_e, 1, axis=1)
        )
        merid_out[here] = jnp.where(wet, v + VISCOUS * lap_v - coriolis * u, 0.0)

        below = jnp.where(wet_below, mixing[here], 0.0)
        diagonal = (1.0 + below) + above * (1.0 - g_above)
        inv = inverse(diagonal)
        dragged = jnp.logical_and(depth_here == k + 1, wet)
        inv_m = inverse(diagonal + jnp.where(dragged, BOTTOM_DRAG, 0.0))
        link[pl.ds(start + ROWS, ROWS)] = below
        inv_tracer[here] = inv
        inv_momentum[here] = inv_m
        return below, below * inv, pressure_sum

    def open_pair(plane):
        wet = plane > 0.5
        wet_east = jnp.where(not_east, plane * pltpu.roll(plane, LANES - 1, axis=1), 0.0) > 0.5
        wet_north = jnp.where(not_north, plane * pltpu.roll(plane, ROWS - 1, axis=0), 0.0) > 0.5
        return wet, wet_east, wet_north

    carried = (nothing, nothing, nothing)
    carried = level(0, open_pair(open0) + (open0 * open1 > 0.5,), carried)
    carried = level(
        1,
        open_pair(open1) + (jnp.logical_and(open1 > 0.5, depth_here > 2),),
        carried,
    )

    def deeper(k, carried):
        masks = (depth_here > k, depth_east > k, depth_north > k, depth_here > k + 1)
        return level(k, masks, carried)

    def group(step, carried):
        pl.when(jnp.logical_and(first_north, north_turn == step + 1))(to_north.start)
        for n in range(UNROLL):
            carried = deeper(2 + UNROLL * step + n, carried)
        return carried

    lax.fori_loop(0, (LEVELS - 2) // UNROLL, group, carried)

    def forward(k, values):
        here = at_level(k)
        above = link[here]
        invs = (inv_tracer[here], inv_momentum[here])
        new = []
        for n in range(FIELDS):
            value = (outs[n][here] + above * values[n]) * invs[n // 2]
            outs[n][here] = value
            new.append(value)
        return tuple(new)

    values = lax.fori_loop(0, LEVELS, forward, (nothing,) * 4, unroll=2)

    def backward(step, values):
        k = LEVELS - 2 - step
        here = at_level(k)
        ratio = link[at_level(k + 1)] * inv_tracer[here]
        new = []
        for n in range(FIELDS):
            value = outs[n][here] + ratio * values[n]
            outs[n][here] = value
            new.append(value)
        return tuple(new)

    lax.fori_loop(0, LEVELS - 1, backward, values, unroll=2)

    for side, edge in ((0, 0), (1, ROWS - 1)):
        there = pl.ds(edge, LEVELS, stride=ROWS)
        above = link[there]
        below = link[pl.ds(ROWS + edge, LEVELS, stride=ROWS)]
        inv_t = inv_tracer[there]
        inv_m = inv_momentum[there]
        up = below * inv_t
        for n in range(FIELDS):
            to = pl.ds(side * FIELDS + n, LEVELS, stride=EDGE)
            edge_inv[to] = inv_m if n > 1 else inv_t
            edge_down[to] = above * (inv_m if n > 1 else inv_t)
            edge_up[to] = up
    packed = (nothing, nothing)
    packed = pack(lambda k: link[at_level(k)], 0, packed)
    packed = pack(lambda k: inv_tracer[at_level(k)], 1, packed)
    packed = pack(lambda k: inv_momentum[at_level(k)], 2, packed)
    packed = pack(lambda k: link[at_level(k + 1)], 3, packed)

    coefs = levels_first(pltpu.roll(packed[1], LANES - 1, axis=1), packed[0])
    above, inv_t, inv_m, below = (coefs[n * LEVELS : (n + 1) * LEVELS] for n in range(4))
    for n in range(FIELDS):
        to = pl.ds(2 * FIELDS + n, LEVELS, stride=EDGE)
        edge_inv[to] = inv_m if n > 1 else inv_t
        edge_down[to] = above * (inv_m if n > 1 else inv_t)
        edge_up[to] = below * inv_t
        spare = pl.ds(3 * FIELDS + n, LEVELS, stride=EDGE)
        edge_down[spare] = nothing
        edge_up[spare] = nothing
        edge_value[spare] = nothing
    edge_half[...] = jnp.zeros_like(edge_half)
    edge_weight[...] = jnp.zeros_like(edge_weight)

    def edge_level(k):
        return pl.ds(k * EDGE, EDGE)

    for start in range(0, LEVELS, BLOCK):
        down = up = None
        for n in range(BLOCK):
            k = start + n
            down = edge_down[edge_level(k)] if n == 0 else down * edge_down[edge_level(k)]
            edge_down_block[edge_level(k)] = down
            k = start + BLOCK - 1 - n
            up = edge_up[edge_level(k)] if n == 0 else up * edge_up[edge_level(k)]
            edge_up_block[edge_level(k)] = up

    def wet_levels(level_index, depth, first, second):
        return jnp.where(
            level_index == 0,
            first,
            jnp.where(
                level_index == 1,
                second,
                jnp.where(level_index.astype(jnp.float32) < depth, 1.0, 0.0),
            ),
        )

    def arrival(source, target, slot, sem):
        return pltpu.make_async_remote_copy(
            src_ref=source.at[slot],
            dst_ref=target.at[slot],
            send_sem=send_sem.at[sem],
            recv_sem=recv_sem.at[sem],
            device_id=east,
            device_id_type=MESH,
        )

    from_south = arrival(row_send, row_recv, 0, 0)
    from_north = arrival(row_send, row_recv, 1, 1)
    from_west = arrival(col_send, col_recv, 0, 2)
    from_east = arrival(col_send, col_recv, 1, 3)

    row_float = row.astype(jnp.float32)
    column_lane = lane < 2 * ROWS
    column_sign = jnp.where(lane < ROWS, -1.0, 1.0)

    def row_edge(fields_there, planes):
        wet = wet_levels(row, *planes)
        half = half_density(fields_there[0], fields_there[1], wet > 0.5, row_float)
        return fields_there, wet, half

    def column_edge(buffer, planes):
        turned = levels_first(*(buffer[side, pl.ds(0, ROWS)] for side in (0, 1)))
        return row_edge(
            [turned[n * LEVELS : (n + 1) * LEVELS] for n in range(FIELDS)],
            [planes[n : n + 1] for n in range(3)],
        )

    def edge_terms(group, here, there, sign, across, extent=None):
        own, own_wet, own_half = here
        other, other_wet, other_half = there
        face = own_wet * other_wet > 0.5
        if extent is not None:
            face = jnp.logical_and(face, extent)
        a = (sign * FACE) * (own[across] + other[across])
        for n in range(FIELDS):
            to = pl.ds(group * FIELDS + n, LEVELS, stride=EDGE)
            if n < 2:
                fix = -DIFFUSE * ((a - 1.0) * other[n] + (a + 1.0) * own[n])
            else:
                fix = VISCOUS * (other[n] - own[n])
            edge_value[to] = jnp.where(face, fix * edge_inv[to], 0.0)
        to = pl.ds(group * FIELDS + across, LEVELS, stride=EDGE)
        edge_half[to] = other_half - own_half
        edge_weight[to] = jnp.where(face, (-VISCOUS * sign) * edge_inv[to], 0.0)

    own_rows = [
        row_edge(
            [field[pl.ds(edge, LEVELS, stride=ROWS)] for field in fields],
            [plane[edge : edge + 1] for plane in mask_planes],
        )
        for edge in (0, ROWS - 1)
    ]
    own_columns = column_edge(col_send, own_planes)

    @pl.when(answers_west)
    def _():
        pl.semaphore_wait(go_west, 1)
        to_west.start()

    @pl.when(answers_north)
    def _():
        pl.semaphore_wait(go_north, 1)
        to_north.start()

    from_north.wait_recv()
    pl.when(lat > 0)(from_south.wait_recv)
    for side in (0, 1):
        there = row_edge(
            [row_recv[side, pl.ds(n * LEVELS, LEVELS)] for n in range(FIELDS)],
            [row_recv[side, pl.ds(MASK_ROW + n, 1)] for n in range(3)],
        )
        edge_terms(side, own_rows[side], there, 1.0 if side else -1.0, 3)

    from_east.wait_recv()
    from_west.wait_recv()
    planes = jnp.where(
        lane[:8] < ROWS, col_recv[0, pl.ds(ROWS, 8)], col_recv[1, pl.ds(ROWS, 8)]
    )
    edge_terms(2, own_columns, column_edge(col_recv, planes), column_sign, 2, column_lane)

    total = jnp.zeros((EDGE, LANES), jnp.float32)
    values = []
    for k in range(LEVELS):
        half = edge_half[edge_level(k)]
        total = total + half
        value = edge_value[edge_level(k)] + edge_weight[edge_level(k)] * total
        total = total + half
        if k % BLOCK:
            value = value + edge_down[edge_level(k)] * values[-1]
        values.append(value)
    for start in range(BLOCK, LEVELS, BLOCK):
        for k in range(start, start + BLOCK):
            values[k] = values[k] + edge_down_block[edge_level(k)] * values[start - 1]
    for k in range(LEVELS - 2, -1, -1):
        if (k + 1) % BLOCK:
            values[k] = values[k] + edge_up[edge_level(k)] * values[k + 1]
    for end in range(LEVELS - BLOCK, 0, -BLOCK):
        for k in range(end - BLOCK, end):
            values[k] = values[k] + edge_up_block[edge_level(k)] * values[end]
    for k in range(LEVELS):
        edge_value[edge_level(k)] = values[k]

    turned = jnp.concatenate(
        [edge_value[pl.ds(2 * FIELDS + n, LEVELS, stride=EDGE)] for n in range(FIELDS)], axis=0
    ).T
    west_fix = pltpu.roll(turned[:ROWS], 1, axis=1)
    east_fix = turned[ROWS : 2 * ROWS]
    even_lane = lax.rem(lane, 2) == 0
    col_out[pl.ds(0, ROWS)] = jnp.where(even_lane, east_fix, west_fix)
    col_out[pl.ds(ROWS, ROWS)] = jnp.where(even_lane, west_fix, east_fix)

    to_north.wait_send()
    to_east.wait_send()
    to_west.wait_send()

    @pl.when(lat > 0)
    def _():
        to_south.wait_send()


def finish(
    warm, salt, zonal, merid, col_fix, edge_value, warm_hbm, salt_hbm, zonal_hbm, merid_hbm, done, sem
):
    lane = iota(1)
    edge_lane = jnp.logical_or(lane == 0, lane == LANES - 1)
    sources = (warm, salt, zonal, merid)
    targets = (warm_hbm, salt_hbm, zonal_hbm, merid_hbm)
    stores = []
    for n in range(FIELDS):

        for k in range(LEVELS):
            here = pl.ds(k * ROWS, ROWS)
            fix = col_fix[pl.ds(k % 2 * ROWS, ROWS)]
            turned = pltpu.roll(fix, LANES - 1 - n * LEVELS - k, axis=1)
            done[n, here] = sources[n][here] + jnp.where(edge_lane, turned, 0.0)
        for side, edge in ((0, 0), (1, ROWS - 1)):
            there = pl.ds(edge, LEVELS, stride=ROWS)
            done[n, there] += edge_value[pl.ds(side * FIELDS + n, LEVELS, stride=EDGE)]
        store = pltpu.make_async_copy(done.at[n], targets[n], sem.at[n])
        store.start()
        stores.append(store)
    for store in stores:
        store.wait()


def result(space, rows):
    return space((rows, LANES), jnp.float32)


def keep_in(x, space):
    return pltpu.with_memory_space_constraint(x, space)


def solution(mesh):
    lat_count = mesh.shape["lat"]
    lon_count = mesh.shape["lon"]

    def step(warm, salt, zonal, merid, mixing, open_water, bottom):
        flat = [x.reshape(CELLS, LANES) for x in (warm, salt, zonal, merid, mixing, open_water)]
        f32 = jnp.float32
        solved = pl.pallas_call(
            functools.partial(kernel, lat_count, lon_count),
            out_shape=[
                *[result(pltpu.VMEM, CELLS)] * FIELDS,
                result(pltpu.VMEM, 2 * ROWS),
                result(pltpu.VMEM, LEVELS * EDGE),
            ],
            in_specs=[pl.BlockSpec(memory_space=pl.ANY)] * 7,
            out_specs=[pl.BlockSpec(memory_space=pltpu.VMEM)] * (FIELDS + 2),
            scratch_shapes=[
                *[pltpu.VMEM((CELLS + 8, LANES), f32)] * FIELDS,
                pltpu.VMEM((CELLS, LANES), f32),
                pltpu.VMEM((2 * ROWS, LANES), jnp.int32),
                pltpu.VMEM((ROWS, LANES), jnp.int32),
                pltpu.VMEM((CELLS + ROWS, LANES), f32),
                pltpu.VMEM((CELLS, LANES), f32),
                pltpu.VMEM((CELLS, LANES), f32),
                pltpu.VMEM((2, MASK_ROW + 8, LANES), f32),
                pltpu.VMEM((2, MASK_ROW + 8, LANES), f32),
                pltpu.VMEM((2, ROWS + 8, LANES), f32),
                pltpu.VMEM((2, ROWS + 8, LANES), f32),
                *[pltpu.VMEM((LEVELS * EDGE, LANES), f32)] * 7,
                pltpu.SemaphoreType.DMA((7,)),
                pltpu.SemaphoreType.DMA((4,)),
                pltpu.SemaphoreType.DMA((4,)),
                pltpu.SemaphoreType.REGULAR,
                pltpu.SemaphoreType.REGULAR,
            ],
            compiler_params=pltpu.CompilerParams(
                collective_id=0, has_side_effects=True, vmem_limit_bytes=16 * 1024 * 1024
            ),
        )(*[keep_in(x, pltpu.HBM) for x in (*flat, bottom)])
        outs = pl.pallas_call(
            finish,
            out_shape=[result(pltpu.HBM, CELLS)] * FIELDS,
            in_specs=[pl.BlockSpec(memory_space=pltpu.VMEM)] * (FIELDS + 2),
            out_specs=[pl.BlockSpec(memory_space=pltpu.HBM)] * FIELDS,
            scratch_shapes=[
                pltpu.VMEM((FIELDS, CELLS, LANES), f32),
                pltpu.SemaphoreType.DMA((FIELDS,)),
            ],
            compiler_params=pltpu.CompilerParams(vmem_limit_bytes=8 * 1024 * 1024),
        )(*[keep_in(x, pltpu.VMEM) for x in solved])
        return tuple(x.reshape(LEVELS, ROWS, LANES) for x in outs)

    tile = P(None, "lat", "lon")
    return jax.shard_map(
        step,
        mesh=mesh,
        in_specs=(tile,) * 6 + (P("lat", "lon"),),
        out_specs=(tile,) * 4,
        check_vma=False,
    )
```

```python
import functools
import math

import jax
import jax.numpy as jnp
from jax import lax
from jax.experimental import pallas as pl
from jax.experimental.pallas import tpu as pltpu
from jax.sharding import PartitionSpec as P

THERMAL_EXPAND = 0.1655
HALINE_CONTRACT = 0.76554
THERMAL_CABBELING = 0.05952
HALINE_CABBELING = 0.00074914
THERMAL_PRESSURE = 0.0001497
HALINE_PRESSURE = 1.109e-05
MIXED_CABBELING = 0.0024341
ADVECT = 0.2
DIFFUSE = 0.08
VISCOUS = 0.08
GRADIENT = 0.1
ROTATION = 0.25
BOTTOM_DRAG = 1.0
OCEAN_DEPTH = 4000.0

MESH = pl.DeviceIdType.MESH
LEVELS = 32
ROWS = 32
LANES = 128
CELLS = LEVELS * ROWS
FIELDS = 4
MASK_ROW = FIELDS * LEVELS
EDGE = 16
UNROLL = 3
BLOCK = 4
PARTS = 2
FOLD_TURNS = (0, 1, 3, 5, 0, 0, 0, 0)
PRESSURE_SCALE = 0.5 / LEVELS * (0.5 * GRADIENT / VISCOUS)
FACE = 0.25 * ADVECT / DIFFUSE


def half_density(warm, salt, wet, level):
    thermal = warm - 10.0
    haline = salt - 35.0
    depth = (level + 0.5) * (OCEAN_DEPTH / LEVELS)
    s = PRESSURE_SCALE
    by_thermal = -THERMAL_EXPAND * s - (THERMAL_EXPAND * THERMAL_PRESSURE * s) * depth
    by_haline = HALINE_CONTRACT * s - (HALINE_CONTRACT * HALINE_PRESSURE * s) * depth
    value = thermal * (
        by_thermal
        - (0.5 * THERMAL_EXPAND * THERMAL_CABBELING * s) * thermal
        - (MIXED_CABBELING * s) * haline
    ) + haline * (by_haline - (0.5 * HALINE_CONTRACT * HALINE_CABBELING * s) * haline)
    return jnp.where(wet, value, 0.0)


def inverse(x):
    r = pl.reciprocal(x, approx=True)
    return r * (2.0 - x * r)


def iota(axis):
    return lax.broadcasted_iota(jnp.int32, (ROWS, LANES), axis)


def kernel(
    lat_count,
    lon_count,
    warm_hbm,
    salt_hbm,
    zonal_hbm,
    merid_hbm,
    mixing_hbm,
    open_hbm,
    bottom_hbm,
    warm_out,
    salt_out,
    zonal_out,
    merid_out,
    col_out,
    edge_value,
    warm,
    salt,
    zonal,
    merid,
    mixing,
    top_open,
    bottom,
    link,
    inv_tracer,
    inv_momentum,
    row_send,
    row_recv,
    col_send,
    col_recv,
    edge_inv,
    edge_down,
    edge_up,
    edge_down_block,
    edge_up_block,
    edge_half,
    edge_weight,
    load_sem,
    send_sem,
    recv_sem,
    go_west,
    go_north,
):
    lat = lax.axis_index("lat")
    lon = lax.axis_index("lon")
    is_south = lat == 0
    is_north = lat == lat_count - 1
    east = {"lon": lax.rem(lon + 1, lon_count)}
    west = {"lon": lax.rem(lon + lon_count - 1, lon_count)}
    south = {"lat": jnp.maximum(lat - 1, 0)}
    north_lat = jnp.minimum(lat + 1, lat_count - 1)
    north_lon = jnp.where(is_north, lon_count - 1 - lon, lon)
    north = {"lat": north_lat, "lon": north_lon}
    fields = (warm, salt, zonal, merid)
    outs = (warm_out, salt_out, zonal_out, merid_out)

    span = lon_count // 2
    place = lax.rem(lon, span)
    is_last = place == span - 1
    lat_odd = lax.rem(lat, 2) == 1
    answers_west = jnp.logical_or(place == 0, is_last)
    fold_late = jnp.logical_and(is_north, place >= span // 2)
    answers_north = jnp.logical_and(lat_odd, jnp.logical_not(fold_late))
    first_west = jnp.logical_not(answers_west)
    first_north = jnp.logical_not(answers_north)

    barrier = pltpu.get_barrier_semaphore()

    def greet(target):
        pl.semaphore_signal(barrier, inc=1, device_id=target, device_id_type=MESH)

    pl.when(jnp.logical_not(fold_late))(lambda: greet(north))
    pl.when(lat_odd)(lambda: greet(south))
    pl.when(place < span - 2)(lambda: greet(east))
    greet(west)
    greetings = (
        1
        + jnp.where(first_west, 1, 0)
        + jnp.where(first_north, 1, 0)
        + jnp.where(is_south, 0, 1)
    )

    meets_early = jnp.logical_and(is_last, lax.rem(lat, 4) != 0)

    def meet():
        pl.semaphore_wait(barrier, greetings)

        def go(sem, target):
            pl.semaphore_signal(sem, inc=1, device_id=target, device_id_type=MESH)

        pl.when(place >= span - 2)(lambda: go(go_west, east))
        pl.when(jnp.logical_and(jnp.logical_not(lat_odd), lat > 0))(lambda: go(go_north, south))
        pl.when(fold_late)(lambda: go(go_north, north))

    loads = [
        pltpu.make_async_copy(src, dst, load_sem.at[n])
        for n, (src, dst) in enumerate(
            (
                (bottom_hbm, bottom),
                (open_hbm.at[pl.ds(0, 2 * ROWS)], top_open),
                (warm_hbm, warm.at[pl.ds(0, CELLS)]),
                (salt_hbm, salt.at[pl.ds(0, CELLS)]),
                (zonal_hbm, zonal.at[pl.ds(0, CELLS)]),
                (merid_hbm, merid.at[pl.ds(0, CELLS)]),
                (mixing_hbm, mixing),
            )
        )
    ]
    for load in loads[:6]:
        load.start()

    lane = iota(1)
    row = iota(0)
    nothing = jnp.zeros((ROWS, LANES), jnp.float32)
    for field in fields:
        field[pl.ds(CELLS, 8)] = jnp.zeros((8, LANES), jnp.float32)

    @pl.when(is_south)
    def _():
        row_recv[0] = jnp.zeros((MASK_ROW + 8, LANES), jnp.float32)

    row_global = (lat * ROWS + row).astype(jnp.float32)
    coriolis = ROTATION * jnp.sin(
        math.pi / 180.0 * (-80.0 + 170.0 * (row_global + 0.5) / (ROWS * lat_count))
    )

    def at_level(k):
        return pl.ds(k * ROWS if isinstance(k, int) else pl.multiple_of(k * ROWS, ROWS), ROWS)

    def pack(source, n, sums):
        easts, wests = sums
        for k in range(LEVELS):
            at = n * LEVELS + k
            turned = pltpu.roll(source(k), (at + 1) % LANES, axis=1)
            easts = jnp.where(lane == at, turned, easts)
            wests = jnp.where(lane == (at + 1) % LANES, turned, wests)
        return easts, wests

    pl.when(meets_early)(meet)
    loads[0].wait()
    loads[1].wait()
    deep = bottom[...].astype(jnp.float32)
    open0 = top_open[pl.ds(0, ROWS)].astype(jnp.float32)
    open1 = top_open[pl.ds(ROWS, ROWS)].astype(jnp.float32)
    mask_planes = (deep, open0, open1)
    for side, edge in ((0, 0), (1, ROWS - 1)):
        for n, plane in enumerate(mask_planes):
            row_send[side, pl.ds(MASK_ROW + n, 1)] = plane[edge : edge + 1]
        row_send[side, pl.ds(MASK_ROW + 3, 5)] = jnp.zeros((5, LANES), jnp.float32)
    east_masks = nothing
    west_masks = nothing
    for n, plane in enumerate(mask_planes):
        turned = pltpu.roll(plane, n + 1, axis=1)
        east_masks = jnp.where(lane == n, turned, east_masks)
        west_masks = jnp.where(lane == n + 1, turned, west_masks)
    west_masks = pltpu.roll(west_masks, LANES - 1, axis=1)
    turned = jnp.concatenate([east_masks, west_masks, west_masks, east_masks], axis=0).T[:8]
    col_send[1, pl.ds(ROWS, 8)] = turned
    col_send[0, pl.ds(ROWS, 8)] = turned
    own_planes = pltpu.roll(turned, LANES - 2 * ROWS, axis=1)
    packed = (nothing, nothing)
    for n, field in enumerate(fields):
        loads[2 + n].wait()
        if n == 1:
            loads[6].start()
        for side, edge in ((0, 0), (1, ROWS - 1)):
            row_send[side, pl.ds(n * LEVELS, LEVELS)] = field[pl.ds(edge, LEVELS, stride=ROWS)]
        packed = pack(lambda k, field=field: field[at_level(k)], n, packed)
    col_send[1, pl.ds(0, ROWS)] = packed[0]
    col_send[0, pl.ds(0, ROWS)] = pltpu.roll(packed[1], LANES - 1, axis=1)

    @pl.when(is_north)
    def _():
        flip = (LANES - 1) - lax.broadcasted_iota(jnp.int32, (8, LANES), 1)
        for tile in range((MASK_ROW + 8) // 8):
            there = pl.ds(tile * 8, 8)
            turned = jnp.take_along_axis(row_send[1, there], flip, axis=1)
            if 2 * LEVELS <= tile * 8 < 4 * LEVELS:
                turned = -turned
            row_send[1, there] = turned

    to_north = pltpu.make_async_remote_copy(
        src_ref=row_send.at[1],
        dst_ref=row_recv.at[jnp.where(is_north, 1, 0)],
        send_sem=send_sem.at[1],
        recv_sem=recv_sem.at[jnp.where(is_north, 1, 0)],
        device_id=north,
        device_id_type=MESH,
    )
    to_south = pltpu.make_async_remote_copy(
        src_ref=row_send.at[0],
        dst_ref=row_recv.at[1],
        send_sem=send_sem.at[0],
        recv_sem=recv_sem.at[1],
        device_id=south,
        device_id_type=MESH,
    )
    to_east = pltpu.make_async_remote_copy(
        src_ref=col_send.at[1],
        dst_ref=col_recv.at[0],
        send_sem=send_sem.at[3],
        recv_sem=recv_sem.at[2],
        device_id=east,
        device_id_type=MESH,
    )
    to_west = pltpu.make_async_remote_copy(
        src_ref=col_send.at[0],
        dst_ref=col_recv.at[1],
        send_sem=send_sem.at[2],
        recv_sem=recv_sem.at[3],
        device_id=west,
        device_id_type=MESH,
    )
    pl.when(jnp.logical_not(meets_early))(meet)
    north_turn = 0
    for n, turn in enumerate(FOLD_TURNS):
        north_turn = jnp.where(jnp.logical_and(fold_late, place == span - 1 - n), turn, north_turn)
    to_east.start()
    pl.when(first_west)(to_west.start)
    pl.when(jnp.logical_and(first_north, north_turn == 0))(to_north.start)
    pl.when(lat > 0)(to_south.start)

    def levels_first(wests, easts):
        return jnp.concatenate([wests, easts, nothing, nothing], axis=0).T

    loads[6].wait()
    depth_here = bottom[...]
    not_east = lane < LANES - 1
    not_north = row < ROWS - 1
    depth_east = jnp.where(
        not_east, jnp.minimum(depth_here, pltpu.roll(depth_here, LANES - 1, axis=1)), 0
    )
    depth_north = jnp.where(
        not_north, jnp.minimum(depth_here, pltpu.roll(depth_here, ROWS - 1, axis=0)), 0
    )
    link[pl.ds(0, ROWS)] = nothing

    def level(k, masks, carried):
        above, g_above, pressure_sum = carried
        wet, wet_east, wet_north, wet_below = masks
        k_float = jnp.asarray(k, jnp.int32).astype(jnp.float32)
        start = k * ROWS
        here = pl.ds(start if isinstance(k, int) else pl.multiple_of(start, ROWS), ROWS)
        shifted = pl.ds(start + 1, ROWS)
        t, s, u, v = (field[here] for field in fields)
        t_n, s_n, u_n, v_n = (field[shifted] for field in fields)
        t_e, s_e, u_e, v_e = (pltpu.roll(x, LANES - 1, axis=1) for x in (t, s, u, v))

        half = half_density(t, s, wet, k_float)
        pressure = pressure_sum + half
        pressure_sum = pressure + half
        p_e = pltpu.roll(pressure, LANES - 1, axis=1)
        p_n = pltpu.roll(pressure, ROWS - 1, axis=0)

        a_e = FACE * (u + u_e)
        a_n = FACE * (v + v_n)
        ahead_e = jnp.where(wet_east, a_e - 1.0, 0.0)
        behind_e = jnp.where(wet_east, a_e + 1.0, 0.0)
        ahead_n = jnp.where(wet_north, a_n - 1.0, 0.0)
        behind_n = jnp.where(wet_north, a_n + 1.0, 0.0)

        def spread(f_e, f_n):
            return (f_e - pltpu.roll(f_e, 1, axis=1)) + (f_n - pltpu.roll(f_n, 1, axis=0))

        def tracer(q, q_e, q_n):
            f_e = ahead_e * q_e + behind_e * q
            f_n = ahead_n * q_n + behind_n * q
            return jnp.where(wet, q - DIFFUSE * spread(f_e, f_n), 0.0)

        warm_out[here] = tracer(t, t_e, t_n)
        salt_out[here] = tracer(s, s_e, s_n)

        du_e = jnp.where(wet_east, u_e - u, 0.0)
        dp_e = jnp.where(wet_east, p_e - pressure, 0.0)
        du_n = jnp.where(wet_north, u_n - u, 0.0)
        lap_u = ((du_e - dp_e) - pltpu.roll(du_e + dp_e, 1, axis=1)) + (
            du_n - pltpu.roll(du_n, 1, axis=0)
        )
        zonal_out[here] = jnp.where(wet, u + VISCOUS * lap_u + coriolis * v, 0.0)
        dv_n = jnp.where(wet_north, v_n - v, 0.0)
        dp_n = jnp.where(wet_north, p_n - pressure, 0.0)
        dv_e = jnp.where(wet_east, v_e - v, 0.0)
        lap_v = ((dv_n - dp_n) - pltpu.roll(dv_n + dp_n, 1, axis=0)) + (
            dv_e - pltpu.roll(dv_e, 1, axis=1)
        )
        merid_out[here] = jnp.where(wet, v + VISCOUS * lap_v - coriolis * u, 0.0)

        below = jnp.where(wet_below, mixing[here], 0.0)
        diagonal = (1.0 + below) + above * (1.0 - g_above)
        inv = inverse(diagonal)
        dragged = jnp.logical_and(depth_here == k + 1, wet)
        inv_m = inverse(diagonal + jnp.where(dragged, BOTTOM_DRAG, 0.0))
        link[pl.ds(start + ROWS, ROWS)] = below
        inv_tracer[here] = inv
        inv_momentum[here] = inv_m
        return below, below * inv, pressure_sum

    def open_pair(plane):
        wet = plane > 0.5
        wet_east = jnp.where(not_east, plane * pltpu.roll(plane, LANES - 1, axis=1), 0.0) > 0.5
        wet_north = jnp.where(not_north, plane * pltpu.roll(plane, ROWS - 1, axis=0), 0.0) > 0.5
        return wet, wet_east, wet_north

    carried = (nothing, nothing, nothing)
    carried = level(0, open_pair(open0) + (open0 * open1 > 0.5,), carried)
    carried = level(
        1,
        open_pair(open1) + (jnp.logical_and(open1 > 0.5, depth_here > 2),),
        carried,
    )

    def deeper(k, carried):
        masks = (depth_here > k, depth_east > k, depth_north > k, depth_here > k + 1)
        return level(k, masks, carried)

    def group(step, carried):
        pl.when(jnp.logical_and(first_north, north_turn == step + 1))(to_north.start)
        for n in range(UNROLL):
            carried = deeper(2 + UNROLL * step + n, carried)
        return carried

    lax.fori_loop(0, (LEVELS - 2) // UNROLL, group, carried)

    def forward(k, values):
        here = at_level(k)
        above = link[here]
        invs = (inv_tracer[here], inv_momentum[here])
        new = []
        for n in range(FIELDS):
            value = (outs[n][here] + above * values[n]) * invs[n // 2]
            outs[n][here] = value
            new.append(value)
        return tuple(new)

    values = lax.fori_loop(0, LEVELS, forward, (nothing,) * 4, unroll=2)

    def backward(step, values):
        k = LEVELS - 2 - step
        here = at_level(k)
        ratio = link[at_level(k + 1)] * inv_tracer[here]
        new = []
        for n in range(FIELDS):
            value = outs[n][here] + ratio * values[n]
            outs[n][here] = value
            new.append(value)
        return tuple(new)

    lax.fori_loop(0, LEVELS - 1, backward, values, unroll=2)

    for side, edge in ((0, 0), (1, ROWS - 1)):
        there = pl.ds(edge, LEVELS, stride=ROWS)
        above = link[there]
        below = link[pl.ds(ROWS + edge, LEVELS, stride=ROWS)]
        inv_t = inv_tracer[there]
        inv_m = inv_momentum[there]
        up = below * inv_t
        for n in range(FIELDS):
            to = pl.ds(side * FIELDS + n, LEVELS, stride=EDGE)
            edge_inv[to] = inv_m if n > 1 else inv_t
            edge_down[to] = above * (inv_m if n > 1 else inv_t)
            edge_up[to] = up
    packed = (nothing, nothing)
    packed = pack(lambda k: link[at_level(k)], 0, packed)
    packed = pack(lambda k: inv_tracer[at_level(k)], 1, packed)
    packed = pack(lambda k: inv_momentum[at_level(k)], 2, packed)
    packed = pack(lambda k: link[at_level(k + 1)], 3, packed)

    coefs = levels_first(pltpu.roll(packed[1], LANES - 1, axis=1), packed[0])
    above, inv_t, inv_m, below = (coefs[n * LEVELS : (n + 1) * LEVELS] for n in range(4))
    for n in range(FIELDS):
        to = pl.ds(2 * FIELDS + n, LEVELS, stride=EDGE)
        edge_inv[to] = inv_m if n > 1 else inv_t
        edge_down[to] = above * (inv_m if n > 1 else inv_t)
        edge_up[to] = below * inv_t
        spare = pl.ds(3 * FIELDS + n, LEVELS, stride=EDGE)
        edge_down[spare] = nothing
        edge_up[spare] = nothing
        edge_value[spare] = nothing
    edge_half[...] = jnp.zeros_like(edge_half)
    edge_weight[...] = jnp.zeros_like(edge_weight)

    def edge_level(k):
        return pl.ds(k * EDGE, EDGE)

    for start in range(0, LEVELS, BLOCK):
        down = up = None
        for n in range(BLOCK):
            k = start + n
            down = edge_down[edge_level(k)] if n == 0 else down * edge_down[edge_level(k)]
            edge_down_block[edge_level(k)] = down
            k = start + BLOCK - 1 - n
            up = edge_up[edge_level(k)] if n == 0 else up * edge_up[edge_level(k)]
            edge_up_block[edge_level(k)] = up

    def wet_levels(level_index, depth, first, second):
        return jnp.where(
            level_index == 0,
            first,
            jnp.where(
                level_index == 1,
                second,
                jnp.where(level_index.astype(jnp.float32) < depth, 1.0, 0.0),
            ),
        )

    def arrival(source, target, slot, sem):
        return pltpu.make_async_remote_copy(
            src_ref=source.at[slot],
            dst_ref=target.at[slot],
            send_sem=send_sem.at[sem],
            recv_sem=recv_sem.at[sem],
            device_id=east,
            device_id_type=MESH,
        )

    from_south = arrival(row_send, row_recv, 0, 0)
    from_north = arrival(row_send, row_recv, 1, 1)
    from_west = arrival(col_send, col_recv, 0, 2)
    from_east = arrival(col_send, col_recv, 1, 3)

    row_float = row.astype(jnp.float32)
    column_lane = lane < 2 * ROWS
    column_sign = jnp.where(lane < ROWS, -1.0, 1.0)

    def row_edge(fields_there, planes):
        wet = wet_levels(row, *planes)
        half = half_density(fields_there[0], fields_there[1], wet > 0.5, row_float)
        return fields_there, wet, half

    def column_edge(buffer, planes):
        turned = levels_first(*(buffer[side, pl.ds(0, ROWS)] for side in (0, 1)))
        return row_edge(
            [turned[n * LEVELS : (n + 1) * LEVELS] for n in range(FIELDS)],
            [planes[n : n + 1] for n in range(3)],
        )

    def edge_terms(group, here, there, sign, across, extent=None):
        own, own_wet, own_half = here
        other, other_wet, other_half = there
        face = own_wet * other_wet > 0.5
        if extent is not None:
            face = jnp.logical_and(face, extent)
        a = (sign * FACE) * (own[across] + other[across])
        for n in range(FIELDS):
            to = pl.ds(group * FIELDS + n, LEVELS, stride=EDGE)
            if n < 2:
                fix = -DIFFUSE * ((a - 1.0) * other[n] + (a + 1.0) * own[n])
            else:
                fix = VISCOUS * (other[n] - own[n])
            edge_value[to] = jnp.where(face, fix * edge_inv[to], 0.0)
        to = pl.ds(group * FIELDS + across, LEVELS, stride=EDGE)
        edge_half[to] = other_half - own_half
        edge_weight[to] = jnp.where(face, (-VISCOUS * sign) * edge_inv[to], 0.0)

    own_rows = [
        row_edge(
            [field[pl.ds(edge, LEVELS, stride=ROWS)] for field in fields],
            [plane[edge : edge + 1] for plane in mask_planes],
        )
        for edge in (0, ROWS - 1)
    ]
    own_columns = column_edge(col_send, own_planes)

    @pl.when(answers_west)
    def _():
        pl.semaphore_wait(go_west, 1)
        to_west.start()

    @pl.when(answers_north)
    def _():
        pl.semaphore_wait(go_north, 1)
        to_north.start()

    from_north.wait_recv()
    pl.when(lat > 0)(from_south.wait_recv)
    for side in (0, 1):
        there = row_edge(
            [row_recv[side, pl.ds(n * LEVELS, LEVELS)] for n in range(FIELDS)],
            [row_recv[side, pl.ds(MASK_ROW + n, 1)] for n in range(3)],
        )
        edge_terms(side, own_rows[side], there, 1.0 if side else -1.0, 3)

    from_east.wait_recv()
    from_west.wait_recv()
    planes = jnp.where(
        lane[:8] < ROWS, col_recv[0, pl.ds(ROWS, 8)], col_recv[1, pl.ds(ROWS, 8)]
    )
    edge_terms(2, own_columns, column_edge(col_recv, planes), column_sign, 2, column_lane)

    total = jnp.zeros((EDGE, LANES), jnp.float32)
    values = []
    for k in range(LEVELS):
        half = edge_half[edge_level(k)]
        total = total + half
        value = edge_value[edge_level(k)] + edge_weight[edge_level(k)] * total
        total = total + half
        if k % BLOCK:
            value = value + edge_down[edge_level(k)] * values[-1]
        values.append(value)
    for start in range(BLOCK, LEVELS, BLOCK):
        for k in range(start, start + BLOCK):
            values[k] = values[k] + edge_down_block[edge_level(k)] * values[start - 1]
    for k in range(LEVELS - 2, -1, -1):
        if (k + 1) % BLOCK:
            values[k] = values[k] + edge_up[edge_level(k)] * values[k + 1]
    for end in range(LEVELS - BLOCK, 0, -BLOCK):
        for k in range(end - BLOCK, end):
            values[k] = values[k] + edge_up_block[edge_level(k)] * values[end]
    for k in range(LEVELS):
        edge_value[edge_level(k)] = values[k]

    turned = jnp.concatenate(
        [edge_value[pl.ds(2 * FIELDS + n, LEVELS, stride=EDGE)] for n in range(FIELDS)], axis=0
    ).T
    west_fix = pltpu.roll(turned[:ROWS], 1, axis=1)
    east_fix = turned[ROWS : 2 * ROWS]
    even_lane = lax.rem(lane, 2) == 0
    col_out[pl.ds(0, ROWS)] = jnp.where(even_lane, east_fix, west_fix)
    col_out[pl.ds(ROWS, ROWS)] = jnp.where(even_lane, west_fix, east_fix)

    to_north.wait_send()
    to_east.wait_send()
    to_west.wait_send()

    @pl.when(lat > 0)
    def _():
        to_south.wait_send()


def finish(
    warm, salt, zonal, merid, col_fix, edge_value, warm_hbm, salt_hbm, zonal_hbm, merid_hbm, done, sem
):
    lane = iota(1)
    edge_lane = jnp.logical_or(lane == 0, lane == LANES - 1)
    sources = (warm, salt, zonal, merid)
    targets = (warm_hbm, salt_hbm, zonal_hbm, merid_hbm)
    stores = []
    for n in range(FIELDS):
        for part in range(PARTS):
            levels = LEVELS // PARTS
            first = part * levels
            for k in range(first, first + levels):
                here = pl.ds(k * ROWS, ROWS)
                fix = col_fix[pl.ds(k % 2 * ROWS, ROWS)]
                turned = pltpu.roll(fix, LANES - 1 - n * LEVELS - k, axis=1)
                done[n, here] = sources[n][here] + jnp.where(edge_lane, turned, 0.0)
            for side, edge in ((0, 0), (1, ROWS - 1)):
                there = pl.ds(first * ROWS + edge, levels, stride=ROWS)
                done[n, there] += edge_value[pl.ds(first * EDGE + side * FIELDS + n, levels, stride=EDGE)]
            cells = pl.ds(first * ROWS, levels * ROWS)
            store = pltpu.make_async_copy(done.at[n, cells], targets[n].at[cells], sem.at[n, part])
            store.start()
            stores.append(store)
    for store in stores:
        store.wait()


def result(space, rows):
    return space((rows, LANES), jnp.float32)


def keep_in(x, space):
    return pltpu.with_memory_space_constraint(x, space)


def solution(mesh):
    lat_count = mesh.shape["lat"]
    lon_count = mesh.shape["lon"]

    def step(warm, salt, zonal, merid, mixing, open_water, bottom):
        flat = [x.reshape(CELLS, LANES) for x in (warm, salt, zonal, merid, mixing, open_water)]
        f32 = jnp.float32
        solved = pl.pallas_call(
            functools.partial(kernel, lat_count, lon_count),
            out_shape=[
                *[result(pltpu.VMEM, CELLS)] * FIELDS,
                result(pltpu.VMEM, 2 * ROWS),
                result(pltpu.VMEM, (LEVELS + 1) * EDGE),
            ],
            in_specs=[pl.BlockSpec(memory_space=pl.ANY)] * 7,
            out_specs=[pl.BlockSpec(memory_space=pltpu.VMEM)] * (FIELDS + 2),
            scratch_shapes=[
                *[pltpu.VMEM((CELLS + ROWS, LANES), f32)] * FIELDS,
                pltpu.VMEM((CELLS, LANES), f32),
                pltpu.VMEM((2 * ROWS, LANES), jnp.int32),
                pltpu.VMEM((ROWS, LANES), jnp.int32),
                pltpu.VMEM((CELLS + 2 * ROWS, LANES), f32),
                pltpu.VMEM((CELLS + ROWS, LANES), f32),
                pltpu.VMEM((CELLS + ROWS, LANES), f32),
                pltpu.VMEM((2, MASK_ROW + 8, LANES), f32),
                pltpu.VMEM((2, MASK_ROW + 8, LANES), f32),
                pltpu.VMEM((2, ROWS + 8, LANES), f32),
                pltpu.VMEM((2, ROWS + 8, LANES), f32),
                *[pltpu.VMEM(((LEVELS + 1) * EDGE, LANES), f32)] * 7,
                pltpu.SemaphoreType.DMA((7,)),
                pltpu.SemaphoreType.DMA((4,)),
                pltpu.SemaphoreType.DMA((4,)),
                pltpu.SemaphoreType.REGULAR,
                pltpu.SemaphoreType.REGULAR,
            ],
            compiler_params=pltpu.CompilerParams(
                collective_id=0, has_side_effects=True, vmem_limit_bytes=16 * 1024 * 1024
            ),
        )(*[keep_in(x, pltpu.HBM) for x in (*flat, bottom)])
        outs = pl.pallas_call(
            finish,
            out_shape=[result(pltpu.HBM, CELLS)] * FIELDS,
            in_specs=[pl.BlockSpec(memory_space=pltpu.VMEM)] * (FIELDS + 2),
            out_specs=[pl.BlockSpec(memory_space=pltpu.HBM)] * FIELDS,
            scratch_shapes=[
                pltpu.VMEM((FIELDS, CELLS + ROWS, LANES), f32),
                pltpu.SemaphoreType.DMA((FIELDS, PARTS)),
            ],
            compiler_params=pltpu.CompilerParams(vmem_limit_bytes=8 * 1024 * 1024),
        )(*[keep_in(x, pltpu.VMEM) for x in solved])
        return tuple(x.reshape(LEVELS, ROWS, LANES) for x in outs)

    tile = P(None, "lat", "lon")
    return jax.shard_map(
        step,
        mesh=mesh,
        in_specs=(tile,) * 6 + (P("lat", "lon"),),
        out_specs=(tile,) * 4,
        check_vma=False,
    )
```

```python
import functools
import math

import jax
import jax.numpy as jnp
from jax import lax
from jax.experimental import pallas as pl
from jax.experimental.pallas import tpu as pltpu
from jax.sharding import PartitionSpec as P

THERMAL_EXPAND = 0.1655
HALINE_CONTRACT = 0.76554
THERMAL_CABBELING = 0.05952
HALINE_CABBELING = 0.00074914
THERMAL_PRESSURE = 0.0001497
HALINE_PRESSURE = 1.109e-05
MIXED_CABBELING = 0.0024341
ADVECT = 0.2
DIFFUSE = 0.08
VISCOUS = 0.08
GRADIENT = 0.1
ROTATION = 0.25
BOTTOM_DRAG = 1.0
OCEAN_DEPTH = 4000.0

MESH = pl.DeviceIdType.MESH
LEVELS = 32
ROWS = 32
LANES = 128
CELLS = LEVELS * ROWS
FIELDS = 4
MASK_ROW = FIELDS * LEVELS
EDGE = 16
UNROLL = 3
BLOCK = 4
PARTS = 2
FOLD_TURNS = (0, 1, 3, 5, 0, 0, 0, 0)
PRESSURE_SCALE = 0.5 / LEVELS * (0.5 * GRADIENT / VISCOUS)
FACE = 0.25 * ADVECT / DIFFUSE


def half_density(warm, salt, wet, level):
    thermal = warm - 10.0
    haline = salt - 35.0
    depth = (level + 0.5) * (OCEAN_DEPTH / LEVELS)
    s = PRESSURE_SCALE
    by_thermal = -THERMAL_EXPAND * s - (THERMAL_EXPAND * THERMAL_PRESSURE * s) * depth
    by_haline = HALINE_CONTRACT * s - (HALINE_CONTRACT * HALINE_PRESSURE * s) * depth
    value = thermal * (
        by_thermal
        - (0.5 * THERMAL_EXPAND * THERMAL_CABBELING * s) * thermal
        - (MIXED_CABBELING * s) * haline
    ) + haline * (by_haline - (0.5 * HALINE_CONTRACT * HALINE_CABBELING * s) * haline)
    return jnp.where(wet, value, 0.0)


def inverse(x):
    r = pl.reciprocal(x, approx=True)
    return r * (2.0 - x * r)


def iota(axis):
    return lax.broadcasted_iota(jnp.int32, (ROWS, LANES), axis)


def kernel(
    lat_count,
    lon_count,
    warm_hbm,
    salt_hbm,
    zonal_hbm,
    merid_hbm,
    mixing_hbm,
    open_hbm,
    bottom_hbm,
    warm_out,
    salt_out,
    zonal_out,
    merid_out,
    col_out,
    edge_value,
    warm,
    salt,
    zonal,
    merid,
    mixing,
    top_open,
    bottom,
    link,
    inv_tracer,
    inv_momentum,
    row_send,
    row_recv,
    col_send,
    col_recv,
    edge_inv,
    edge_down,
    edge_up,
    edge_down_block,
    edge_up_block,
    edge_half,
    edge_weight,
    load_sem,
    send_sem,
    recv_sem,
    go_west,
    go_north,
):
    lat = lax.axis_index("lat")
    lon = lax.axis_index("lon")
    is_south = lat == 0
    is_north = lat == lat_count - 1
    east = {"lon": lax.rem(lon + 1, lon_count)}
    west = {"lon": lax.rem(lon + lon_count - 1, lon_count)}
    south = {"lat": jnp.maximum(lat - 1, 0)}
    north_lat = jnp.minimum(lat + 1, lat_count - 1)
    north_lon = jnp.where(is_north, lon_count - 1 - lon, lon)
    north = {"lat": north_lat, "lon": north_lon}
    fields = (warm, salt, zonal, merid)
    outs = (warm_out, salt_out, zonal_out, merid_out)

    span = lon_count // 2
    place = lax.rem(lon, span)
    is_last = place == span - 1
    lat_odd = lax.rem(lat, 2) == 1
    answers_west = jnp.logical_or(place == 0, is_last)
    fold_late = jnp.logical_and(is_north, place >= span // 2)
    answers_north = jnp.logical_and(lat_odd, jnp.logical_not(fold_late))
    first_west = jnp.logical_not(answers_west)
    first_north = jnp.logical_not(answers_north)

    barrier = pltpu.get_barrier_semaphore()

    def greet(target):
        pl.semaphore_signal(barrier, inc=1, device_id=target, device_id_type=MESH)

    pl.when(jnp.logical_not(fold_late))(lambda: greet(north))
    pl.when(lat_odd)(lambda: greet(south))
    pl.when(place < span - 2)(lambda: greet(east))
    greet(west)
    greetings = (
        1
        + jnp.where(first_west, 1, 0)
        + jnp.where(first_north, 1, 0)
        + jnp.where(is_south, 0, 1)
    )

    meets_early = jnp.logical_and(is_last, lax.rem(lat, 4) != 0)

    def meet():
        pl.semaphore_wait(barrier, greetings)

        def go(sem, target):
            pl.semaphore_signal(sem, inc=1, device_id=target, device_id_type=MESH)

        pl.when(place >= span - 2)(lambda: go(go_west, east))
        pl.when(jnp.logical_and(jnp.logical_not(lat_odd), lat > 0))(lambda: go(go_north, south))
        pl.when(fold_late)(lambda: go(go_north, north))

    loads = [
        pltpu.make_async_copy(src, dst, load_sem.at[n])
        for n, (src, dst) in enumerate(
            (
                (bottom_hbm, bottom),
                (open_hbm.at[pl.ds(0, 2 * ROWS)], top_open),
                (warm_hbm, warm.at[pl.ds(0, CELLS)]),
                (salt_hbm, salt.at[pl.ds(0, CELLS)]),
                (zonal_hbm, zonal.at[pl.ds(0, CELLS)]),
                (merid_hbm, merid.at[pl.ds(0, CELLS)]),
                (mixing_hbm, mixing),
            )
        )
    ]
    for load in loads[:6]:
        load.start()

    lane = iota(1)
    row = iota(0)
    nothing = jnp.zeros((ROWS, LANES), jnp.float32)
    for field in fields:
        field[pl.ds(CELLS, 8)] = jnp.zeros((8, LANES), jnp.float32)

    @pl.when(is_south)
    def _():
        row_recv[0] = jnp.zeros((MASK_ROW + 8, LANES), jnp.float32)

    row_global = (lat * ROWS + row).astype(jnp.float32)
    coriolis = ROTATION * jnp.sin(
        math.pi / 180.0 * (-80.0 + 170.0 * (row_global + 0.5) / (ROWS * lat_count))
    )

    def at_level(k):
        return pl.ds(k * ROWS if isinstance(k, int) else pl.multiple_of(k * ROWS, ROWS), ROWS)

    def pack(source, n, sums):
        easts, wests = sums
        for k in range(LEVELS):
            at = n * LEVELS + k
            turned = pltpu.roll(source(k), (at + 1) % LANES, axis=1)
            easts = jnp.where(lane == at, turned, easts)
            wests = jnp.where(lane == (at + 1) % LANES, turned, wests)
        return easts, wests

    pl.when(meets_early)(meet)
    loads[0].wait()
    loads[1].wait()
    deep = bottom[...].astype(jnp.float32)
    open0 = top_open[pl.ds(0, ROWS)].astype(jnp.float32)
    open1 = top_open[pl.ds(ROWS, ROWS)].astype(jnp.float32)
    mask_planes = (deep, open0, open1)
    for side, edge in ((0, 0), (1, ROWS - 1)):
        for n, plane in enumerate(mask_planes):
            row_send[side, pl.ds(MASK_ROW + n, 1)] = plane[edge : edge + 1]
        row_send[side, pl.ds(MASK_ROW + 3, 5)] = jnp.zeros((5, LANES), jnp.float32)
    east_masks = nothing
    west_masks = nothing
    for n, plane in enumerate(mask_planes):
        turned = pltpu.roll(plane, n + 1, axis=1)
        east_masks = jnp.where(lane == n, turned, east_masks)
        west_masks = jnp.where(lane == n + 1, turned, west_masks)
    west_masks = pltpu.roll(west_masks, LANES - 1, axis=1)
    turned = jnp.concatenate([east_masks, west_masks, west_masks, east_masks], axis=0).T[:8]
    col_send[1, pl.ds(ROWS, 8)] = turned
    col_send[0, pl.ds(ROWS, 8)] = turned
    own_planes = pltpu.roll(turned, LANES - 2 * ROWS, axis=1)
    packed = (nothing, nothing)
    for n, field in enumerate(fields):
        loads[2 + n].wait()
        if n == 1:
            loads[6].start()
        for side, edge in ((0, 0), (1, ROWS - 1)):
            row_send[side, pl.ds(n * LEVELS, LEVELS)] = field[pl.ds(edge, LEVELS, stride=ROWS)]
        packed = pack(lambda k, field=field: field[at_level(k)], n, packed)
    col_send[1, pl.ds(0, ROWS)] = packed[0]
    col_send[0, pl.ds(0, ROWS)] = pltpu.roll(packed[1], LANES - 1, axis=1)

    @pl.when(is_north)
    def _():
        flip = (LANES - 1) - lax.broadcasted_iota(jnp.int32, (8, LANES), 1)
        for tile in range((MASK_ROW + 8) // 8):
            there = pl.ds(tile * 8, 8)
            turned = jnp.take_along_axis(row_send[1, there], flip, axis=1)
            if 2 * LEVELS <= tile * 8 < 4 * LEVELS:
                turned = -turned
            row_send[1, there] = turned

    to_north = pltpu.make_async_remote_copy(
        src_ref=row_send.at[1],
        dst_ref=row_recv.at[jnp.where(is_north, 1, 0)],
        send_sem=send_sem.at[1],
        recv_sem=recv_sem.at[jnp.where(is_north, 1, 0)],
        device_id=north,
        device_id_type=MESH,
    )
    to_south = pltpu.make_async_remote_copy(
        src_ref=row_send.at[0],
        dst_ref=row_recv.at[1],
        send_sem=send_sem.at[0],
        recv_sem=recv_sem.at[1],
        device_id=south,
        device_id_type=MESH,
    )
    to_east = pltpu.make_async_remote_copy(
        src_ref=col_send.at[1],
        dst_ref=col_recv.at[0],
        send_sem=send_sem.at[3],
        recv_sem=recv_sem.at[2],
        device_id=east,
        device_id_type=MESH,
    )
    to_west = pltpu.make_async_remote_copy(
        src_ref=col_send.at[0],
        dst_ref=col_recv.at[1],
        send_sem=send_sem.at[2],
        recv_sem=recv_sem.at[3],
        device_id=west,
        device_id_type=MESH,
    )
    pl.when(jnp.logical_not(meets_early))(meet)
    north_turn = 0
    for n, turn in enumerate(FOLD_TURNS):
        north_turn = jnp.where(jnp.logical_and(fold_late, place == span - 1 - n), turn, north_turn)
    to_east.start()
    pl.when(first_west)(to_west.start)
    pl.when(jnp.logical_and(first_north, north_turn == 0))(to_north.start)
    pl.when(lat > 0)(to_south.start)

    def levels_first(wests, easts):
        return jnp.concatenate([wests, easts, nothing, nothing], axis=0).T

    loads[6].wait()
    depth_here = bottom[...]
    not_east = lane < LANES - 1
    not_north = row < ROWS - 1
    depth_east = jnp.where(
        not_east, jnp.minimum(depth_here, pltpu.roll(depth_here, LANES - 1, axis=1)), 0
    )
    depth_north = jnp.where(
        not_north, jnp.minimum(depth_here, pltpu.roll(depth_here, ROWS - 1, axis=0)), 0
    )
    link[pl.ds(0, ROWS)] = nothing

    def level(k, masks, carried):
        above, g_above, pressure_sum = carried
        wet, wet_east, wet_north, wet_below = masks
        k_float = jnp.asarray(k, jnp.int32).astype(jnp.float32)
        start = k * ROWS
        here = pl.ds(start if isinstance(k, int) else pl.multiple_of(start, ROWS), ROWS)
        shifted = pl.ds(start + 1, ROWS)
        t, s, u, v = (field[here] for field in fields)
        t_n, s_n, u_n, v_n = (field[shifted] for field in fields)
        t_e, s_e, u_e, v_e = (pltpu.roll(x, LANES - 1, axis=1) for x in (t, s, u, v))

        half = half_density(t, s, wet, k_float)
        pressure = pressure_sum + half
        pressure_sum = pressure + half
        p_e = pltpu.roll(pressure, LANES - 1, axis=1)
        p_n = pltpu.roll(pressure, ROWS - 1, axis=0)

        a_e = FACE * (u + u_e)
        a_n = FACE * (v + v_n)
        ahead_e = jnp.where(wet_east, a_e - 1.0, 0.0)
        behind_e = jnp.where(wet_east, a_e + 1.0, 0.0)
        ahead_n = jnp.where(wet_north, a_n - 1.0, 0.0)
        behind_n = jnp.where(wet_north, a_n + 1.0, 0.0)

        def spread(f_e, f_n):
            return (f_e - pltpu.roll(f_e, 1, axis=1)) + (f_n - pltpu.roll(f_n, 1, axis=0))

        def tracer(q, q_e, q_n):
            f_e = ahead_e * q_e + behind_e * q
            f_n = ahead_n * q_n + behind_n * q
            return jnp.where(wet, q - DIFFUSE * spread(f_e, f_n), 0.0)

        warm_out[here] = tracer(t, t_e, t_n)
        salt_out[here] = tracer(s, s_e, s_n)

        du_e = jnp.where(wet_east, u_e - u, 0.0)
        dp_e = jnp.where(wet_east, p_e - pressure, 0.0)
        du_n = jnp.where(wet_north, u_n - u, 0.0)
        lap_u = ((du_e - dp_e) - pltpu.roll(du_e + dp_e, 1, axis=1)) + (
            du_n - pltpu.roll(du_n, 1, axis=0)
        )
        zonal_out[here] = jnp.where(wet, u + VISCOUS * lap_u + coriolis * v, 0.0)
        dv_n = jnp.where(wet_north, v_n - v, 0.0)
        dp_n = jnp.where(wet_north, p_n - pressure, 0.0)
        dv_e = jnp.where(wet_east, v_e - v, 0.0)
        lap_v = ((dv_n - dp_n) - pltpu.roll(dv_n + dp_n, 1, axis=0)) + (
            dv_e - pltpu.roll(dv_e, 1, axis=1)
        )
        merid_out[here] = jnp.where(wet, v + VISCOUS * lap_v - coriolis * u, 0.0)

        below = jnp.where(wet_below, mixing[here], 0.0)
        diagonal = (1.0 + below) + above * (1.0 - g_above)
        inv = inverse(diagonal)
        dragged = jnp.logical_and(depth_here == k + 1, wet)
        inv_m = inverse(diagonal + jnp.where(dragged, BOTTOM_DRAG, 0.0))
        link[pl.ds(start + ROWS, ROWS)] = below
        inv_tracer[here] = inv
        inv_momentum[here] = inv_m
        return below, below * inv, pressure_sum

    def open_pair(plane):
        wet = plane > 0.5
        wet_east = jnp.where(not_east, plane * pltpu.roll(plane, LANES - 1, axis=1), 0.0) > 0.5
        wet_north = jnp.where(not_north, plane * pltpu.roll(plane, ROWS - 1, axis=0), 0.0) > 0.5
        return wet, wet_east, wet_north

    carried = (nothing, nothing, nothing)
    carried = level(0, open_pair(open0) + (open0 * open1 > 0.5,), carried)
    carried = level(
        1,
        open_pair(open1) + (jnp.logical_and(open1 > 0.5, depth_here > 2),),
        carried,
    )

    def deeper(k, carried):
        masks = (depth_here > k, depth_east > k, depth_north > k, depth_here > k + 1)
        return level(k, masks, carried)

    def group(step, carried):
        pl.when(jnp.logical_and(first_north, north_turn == step + 1))(to_north.start)
        for n in range(UNROLL):
            carried = deeper(2 + UNROLL * step + n, carried)
        return carried

    lax.fori_loop(0, (LEVELS - 2) // UNROLL, group, carried)

    def forward(k, values):
        here = at_level(k)
        above = link[here]
        invs = (inv_tracer[here], inv_momentum[here])
        new = []
        for n in range(FIELDS):
            value = (outs[n][here] + above * values[n]) * invs[n // 2]
            outs[n][here] = value
            new.append(value)
        return tuple(new)

    values = lax.fori_loop(0, LEVELS, forward, (nothing,) * 4, unroll=2)

    def backward(step, values):
        k = LEVELS - 2 - step
        here = at_level(k)
        ratio = link[at_level(k + 1)] * inv_tracer[here]
        new = []
        for n in range(FIELDS):
            value = outs[n][here] + ratio * values[n]
            outs[n][here] = value
            new.append(value)
        return tuple(new)

    lax.fori_loop(0, LEVELS - 1, backward, values, unroll=2)

    for side, edge in ((0, 0), (1, ROWS - 1)):
        there = pl.ds(edge, LEVELS, stride=ROWS)
        above = link[there]
        below = link[pl.ds(ROWS + edge, LEVELS, stride=ROWS)]
        inv_t = inv_tracer[there]
        inv_m = inv_momentum[there]
        up = below * inv_t
        for n in range(FIELDS):
            to = pl.ds(side * FIELDS + n, LEVELS, stride=EDGE)
            edge_inv[to] = inv_m if n > 1 else inv_t
            edge_down[to] = above * (inv_m if n > 1 else inv_t)
            edge_up[to] = up
    packed = (nothing, nothing)
    packed = pack(lambda k: link[at_level(k)], 0, packed)
    packed = pack(lambda k: inv_tracer[at_level(k)], 1, packed)
    packed = pack(lambda k: inv_momentum[at_level(k)], 2, packed)
    packed = pack(lambda k: link[at_level(k + 1)], 3, packed)

    coefs = levels_first(pltpu.roll(packed[1], LANES - 1, axis=1), packed[0])
    above, inv_t, inv_m, below = (coefs[n * LEVELS : (n + 1) * LEVELS] for n in range(4))
    for n in range(FIELDS):
        to = pl.ds(2 * FIELDS + n, LEVELS, stride=EDGE)
        edge_inv[to] = inv_m if n > 1 else inv_t
        edge_down[to] = above * (inv_m if n > 1 else inv_t)
        edge_up[to] = below * inv_t
        spare = pl.ds(3 * FIELDS + n, LEVELS, stride=EDGE)
        edge_down[spare] = nothing
        edge_up[spare] = nothing
        edge_value[spare] = nothing
    edge_half[...] = jnp.zeros_like(edge_half)
    edge_weight[...] = jnp.zeros_like(edge_weight)

    def edge_level(k):
        return pl.ds(k * EDGE, EDGE)

    for start in range(0, LEVELS, BLOCK):
        down = up = None
        for n in range(BLOCK):
            k = start + n
            down = edge_down[edge_level(k)] if n == 0 else down * edge_down[edge_level(k)]
            edge_down_block[edge_level(k)] = down
            k = start + BLOCK - 1 - n
            up = edge_up[edge_level(k)] if n == 0 else up * edge_up[edge_level(k)]
            edge_up_block[edge_level(k)] = up

    def wet_levels(level_index, depth, first, second):
        return jnp.where(
            level_index == 0,
            first,
            jnp.where(
                level_index == 1,
                second,
                jnp.where(level_index.astype(jnp.float32) < depth, 1.0, 0.0),
            ),
        )

    def arrival(source, target, slot, sem):
        return pltpu.make_async_remote_copy(
            src_ref=source.at[slot],
            dst_ref=target.at[slot],
            send_sem=send_sem.at[sem],
            recv_sem=recv_sem.at[sem],
            device_id=east,
            device_id_type=MESH,
        )

    from_south = arrival(row_send, row_recv, 0, 0)
    from_north = arrival(row_send, row_recv, 1, 1)
    from_west = arrival(col_send, col_recv, 0, 2)
    from_east = arrival(col_send, col_recv, 1, 3)

    row_float = row.astype(jnp.float32)
    column_lane = lane < 2 * ROWS
    column_sign = jnp.where(lane < ROWS, -1.0, 1.0)

    def row_edge(fields_there, planes):
        wet = wet_levels(row, *planes)
        half = half_density(fields_there[0], fields_there[1], wet > 0.5, row_float)
        return fields_there, wet, half

    def column_edge(buffer, planes):
        turned = levels_first(*(buffer[side, pl.ds(0, ROWS)] for side in (0, 1)))
        return row_edge(
            [turned[n * LEVELS : (n + 1) * LEVELS] for n in range(FIELDS)],
            [planes[n : n + 1] for n in range(3)],
        )

    def edge_terms(group, here, there, sign, across, extent=None):
        own, own_wet, own_half = here
        other, other_wet, other_half = there
        face = own_wet * other_wet > 0.5
        if extent is not None:
            face = jnp.logical_and(face, extent)
        a = (sign * FACE) * (own[across] + other[across])
        for n in range(FIELDS):
            to = pl.ds(group * FIELDS + n, LEVELS, stride=EDGE)
            if n < 2:
                fix = -DIFFUSE * ((a - 1.0) * other[n] + (a + 1.0) * own[n])
            else:
                fix = VISCOUS * (other[n] - own[n])
            edge_value[to] = jnp.where(face, fix * edge_inv[to], 0.0)
        to = pl.ds(group * FIELDS + across, LEVELS, stride=EDGE)
        edge_half[to] = other_half - own_half
        edge_weight[to] = jnp.where(face, (-VISCOUS * sign) * edge_inv[to], 0.0)

    own_rows = [
        row_edge(
            [field[pl.ds(edge, LEVELS, stride=ROWS)] for field in fields],
            [plane[edge : edge + 1] for plane in mask_planes],
        )
        for edge in (0, ROWS - 1)
    ]
    own_columns = column_edge(col_send, own_planes)

    @pl.when(answers_north)
    def _():
        pl.semaphore_wait(go_north, 1)
        to_north.start()

    @pl.when(answers_west)
    def _():
        pl.semaphore_wait(go_west, 1)
        to_west.start()

    from_north.wait_recv()
    pl.when(lat > 0)(from_south.wait_recv)
    for side in (0, 1):
        there = row_edge(
            [row_recv[side, pl.ds(n * LEVELS, LEVELS)] for n in range(FIELDS)],
            [row_recv[side, pl.ds(MASK_ROW + n, 1)] for n in range(3)],
        )
        edge_terms(side, own_rows[side], there, 1.0 if side else -1.0, 3)

    from_east.wait_recv()
    from_west.wait_recv()
    planes = jnp.where(
        lane[:8] < ROWS, col_recv[0, pl.ds(ROWS, 8)], col_recv[1, pl.ds(ROWS, 8)]
    )
    edge_terms(2, own_columns, column_edge(col_recv, planes), column_sign, 2, column_lane)

    total = jnp.zeros((EDGE, LANES), jnp.float32)
    values = []
    for k in range(LEVELS):
        half = edge_half[edge_level(k)]
        total = total + half
        value = edge_value[edge_level(k)] + edge_weight[edge_level(k)] * total
        total = total + half
        if k % BLOCK:
            value = value + edge_down[edge_level(k)] * values[-1]
        values.append(value)
    for start in range(BLOCK, LEVELS, BLOCK):
        for k in range(start, start + BLOCK):
            values[k] = values[k] + edge_down_block[edge_level(k)] * values[start - 1]
    for k in range(LEVELS - 2, -1, -1):
        if (k + 1) % BLOCK:
            values[k] = values[k] + edge_up[edge_level(k)] * values[k + 1]
    for end in range(LEVELS - BLOCK, 0, -BLOCK):
        for k in range(end - BLOCK, end):
            values[k] = values[k] + edge_up_block[edge_level(k)] * values[end]
    for k in range(LEVELS):
        edge_value[edge_level(k)] = values[k]

    turned = jnp.concatenate(
        [edge_value[pl.ds(2 * FIELDS + n, LEVELS, stride=EDGE)] for n in range(FIELDS)], axis=0
    ).T
    west_fix = pltpu.roll(turned[:ROWS], 1, axis=1)
    east_fix = turned[ROWS : 2 * ROWS]
    even_lane = lax.rem(lane, 2) == 0
    col_out[pl.ds(0, ROWS)] = jnp.where(even_lane, east_fix, west_fix)
    col_out[pl.ds(ROWS, ROWS)] = jnp.where(even_lane, west_fix, east_fix)

    to_north.wait_send()
    to_east.wait_send()
    to_west.wait_send()

    @pl.when(lat > 0)
    def _():
        to_south.wait_send()


def finish(
    warm, salt, zonal, merid, col_fix, edge_value, warm_hbm, salt_hbm, zonal_hbm, merid_hbm, done, sem
):
    lane = iota(1)
    edge_lane = jnp.logical_or(lane == 0, lane == LANES - 1)
    sources = (warm, salt, zonal, merid)
    targets = (warm_hbm, salt_hbm, zonal_hbm, merid_hbm)
    stores = []
    for n in range(FIELDS):
        for part in range(PARTS):
            levels = LEVELS // PARTS
            first = part * levels
            for k in range(first, first + levels):
                here = pl.ds(k * ROWS, ROWS)
                fix = col_fix[pl.ds(k % 2 * ROWS, ROWS)]
                turned = pltpu.roll(fix, LANES - 1 - n * LEVELS - k, axis=1)
                done[n, here] = sources[n][here] + jnp.where(edge_lane, turned, 0.0)
            for side, edge in ((0, 0), (1, ROWS - 1)):
                there = pl.ds(first * ROWS + edge, levels, stride=ROWS)
                done[n, there] += edge_value[pl.ds(first * EDGE + side * FIELDS + n, levels, stride=EDGE)]
            cells = pl.ds(first * ROWS, levels * ROWS)
            store = pltpu.make_async_copy(done.at[n, cells], targets[n].at[cells], sem.at[n, part])
            store.start()
            stores.append(store)
    for store in stores:
        store.wait()


def result(space, rows):
    return space((rows, LANES), jnp.float32)


def keep_in(x, space):
    return pltpu.with_memory_space_constraint(x, space)


def solution(mesh):
    lat_count = mesh.shape["lat"]
    lon_count = mesh.shape["lon"]

    def step(warm, salt, zonal, merid, mixing, open_water, bottom):
        flat = [x.reshape(CELLS, LANES) for x in (warm, salt, zonal, merid, mixing, open_water)]
        f32 = jnp.float32
        solved = pl.pallas_call(
            functools.partial(kernel, lat_count, lon_count),
            out_shape=[
                *[result(pltpu.VMEM, CELLS)] * FIELDS,
                result(pltpu.VMEM, 2 * ROWS),
                result(pltpu.VMEM, (LEVELS + 1) * EDGE),
            ],
            in_specs=[pl.BlockSpec(memory_space=pl.ANY)] * 7,
            out_specs=[pl.BlockSpec(memory_space=pltpu.VMEM)] * (FIELDS + 2),
            scratch_shapes=[
                *[pltpu.VMEM((CELLS + ROWS, LANES), f32)] * FIELDS,
                pltpu.VMEM((CELLS, LANES), f32),
                pltpu.VMEM((2 * ROWS, LANES), jnp.int32),
                pltpu.VMEM((ROWS, LANES), jnp.int32),
                pltpu.VMEM((CELLS + 2 * ROWS, LANES), f32),
                pltpu.VMEM((CELLS + ROWS, LANES), f32),
                pltpu.VMEM((CELLS + ROWS, LANES), f32),
                pltpu.VMEM((2, MASK_ROW + 8, LANES), f32),
                pltpu.VMEM((2, MASK_ROW + 8, LANES), f32),
                pltpu.VMEM((2, ROWS + 8, LANES), f32),
                pltpu.VMEM((2, ROWS + 8, LANES), f32),
                *[pltpu.VMEM(((LEVELS + 1) * EDGE, LANES), f32)] * 7,
                pltpu.SemaphoreType.DMA((7,)),
                pltpu.SemaphoreType.DMA((4,)),
                pltpu.SemaphoreType.DMA((4,)),
                pltpu.SemaphoreType.REGULAR,
                pltpu.SemaphoreType.REGULAR,
            ],
            compiler_params=pltpu.CompilerParams(
                collective_id=0, has_side_effects=True, vmem_limit_bytes=16 * 1024 * 1024
            ),
        )(*[keep_in(x, pltpu.HBM) for x in (*flat, bottom)])
        outs = pl.pallas_call(
            finish,
            out_shape=[result(pltpu.HBM, CELLS)] * FIELDS,
            in_specs=[pl.BlockSpec(memory_space=pltpu.VMEM)] * (FIELDS + 2),
            out_specs=[pl.BlockSpec(memory_space=pltpu.HBM)] * FIELDS,
            scratch_shapes=[
                pltpu.VMEM((FIELDS, CELLS + ROWS, LANES), f32),
                pltpu.SemaphoreType.DMA((FIELDS, PARTS)),
            ],
            compiler_params=pltpu.CompilerParams(vmem_limit_bytes=8 * 1024 * 1024),
        )(*[keep_in(x, pltpu.VMEM) for x in solved])
        return tuple(x.reshape(LEVELS, ROWS, LANES) for x in outs)

    tile = P(None, "lat", "lon")
    return jax.shard_map(
        step,
        mesh=mesh,
        in_specs=(tile,) * 6 + (P("lat", "lon"),),
        out_specs=(tile,) * 4,
        check_vma=False,
    )
```

```python
import functools
import math

import jax
import jax.numpy as jnp
from jax import lax
from jax.experimental import pallas as pl
from jax.experimental.pallas import tpu as pltpu
from jax.sharding import PartitionSpec as P

THERMAL_EXPAND = 0.1655
HALINE_CONTRACT = 0.76554
THERMAL_CABBELING = 0.05952
HALINE_CABBELING = 0.00074914
THERMAL_PRESSURE = 0.0001497
HALINE_PRESSURE = 1.109e-05
MIXED_CABBELING = 0.0024341
ADVECT = 0.2
DIFFUSE = 0.08
VISCOUS = 0.08
GRADIENT = 0.1
ROTATION = 0.25
BOTTOM_DRAG = 1.0
OCEAN_DEPTH = 4000.0

MESH = pl.DeviceIdType.MESH
LEVELS = 32
ROWS = 32
LANES = 128
CELLS = LEVELS * ROWS
FIELDS = 4
MASK_ROW = FIELDS * LEVELS
EDGE = 16
UNROLL = 3
BLOCK = 4
PARTS = 2
FOLD_TURNS = (0, 1, 3, 4, 0, 0, 0, 0)
PRESSURE_SCALE = 0.5 / LEVELS * (0.5 * GRADIENT / VISCOUS)
FACE = 0.25 * ADVECT / DIFFUSE


def half_density(warm, salt, wet, level):
    thermal = warm - 10.0
    haline = salt - 35.0
    depth = (level + 0.5) * (OCEAN_DEPTH / LEVELS)
    s = PRESSURE_SCALE
    by_thermal = -THERMAL_EXPAND * s - (THERMAL_EXPAND * THERMAL_PRESSURE * s) * depth
    by_haline = HALINE_CONTRACT * s - (HALINE_CONTRACT * HALINE_PRESSURE * s) * depth
    value = thermal * (
        by_thermal
        - (0.5 * THERMAL_EXPAND * THERMAL_CABBELING * s) * thermal
        - (MIXED_CABBELING * s) * haline
    ) + haline * (by_haline - (0.5 * HALINE_CONTRACT * HALINE_CABBELING * s) * haline)
    return jnp.where(wet, value, 0.0)


def inverse(x):
    r = pl.reciprocal(x, approx=True)
    return r * (2.0 - x * r)


def iota(axis):
    return lax.broadcasted_iota(jnp.int32, (ROWS, LANES), axis)


def kernel(
    lat_count,
    lon_count,
    warm_hbm,
    salt_hbm,
    zonal_hbm,
    merid_hbm,
    mixing_hbm,
    open_hbm,
    bottom_hbm,
    warm_out,
    salt_out,
    zonal_out,
    merid_out,
    col_out,
    edge_value,
    warm,
    salt,
    zonal,
    merid,
    mixing,
    top_open,
    bottom,
    link,
    inv_tracer,
    inv_momentum,
    row_send,
    row_recv,
    col_send,
    col_recv,
    edge_inv,
    edge_down,
    edge_up,
    edge_down_block,
    edge_up_block,
    edge_half,
    edge_weight,
    load_sem,
    send_sem,
    recv_sem,
    go_west,
    go_east,
    go_north,
):
    lat = lax.axis_index("lat")
    lon = lax.axis_index("lon")
    is_south = lat == 0
    is_north = lat == lat_count - 1
    east = {"lon": lax.rem(lon + 1, lon_count)}
    west = {"lon": lax.rem(lon + lon_count - 1, lon_count)}
    south = {"lat": jnp.maximum(lat - 1, 0)}
    north_lat = jnp.minimum(lat + 1, lat_count - 1)
    north_lon = jnp.where(is_north, lon_count - 1 - lon, lon)
    north = {"lat": north_lat, "lon": north_lon}
    fields = (warm, salt, zonal, merid)
    outs = (warm_out, salt_out, zonal_out, merid_out)

    span = lon_count // 2
    place = lax.rem(lon, span)
    is_last = place == span - 1
    lat_odd = lax.rem(lat, 2) == 1
    answers_east = jnp.logical_and(is_north, place == span - 4)
    answers_west = jnp.logical_or(jnp.logical_or(place == 0, is_last), answers_east)
    before_far = jnp.logical_and(is_north, place == span - 5)
    after_far = jnp.logical_and(is_north, place == span - 3)
    first_east = jnp.logical_not(answers_east)
    fold_late = jnp.logical_and(is_north, place >= span // 2)
    answers_north = jnp.logical_and(lat_odd, jnp.logical_not(fold_late))
    first_west = jnp.logical_not(answers_west)
    first_north = jnp.logical_not(answers_north)

    barrier = pltpu.get_barrier_semaphore()

    def greet(target):
        pl.semaphore_signal(barrier, inc=1, device_id=target, device_id_type=MESH)

    pl.when(jnp.logical_not(fold_late))(lambda: greet(north))
    pl.when(lat_odd)(lambda: greet(south))
    pl.when(jnp.logical_and(place < span - 2, jnp.logical_not(before_far)))(lambda: greet(east))
    pl.when(jnp.logical_not(after_far))(lambda: greet(west))
    greetings = (
        jnp.where(first_east, 1, 0)
        + jnp.where(first_west, 1, 0)
        + jnp.where(first_north, 1, 0)
        + jnp.where(is_south, 0, 1)
    )

    meets_early = jnp.logical_and(is_last, lax.rem(lat, 4) != 0)

    def meet():
        pl.semaphore_wait(barrier, greetings)

        def go(sem, target):
            pl.semaphore_signal(sem, inc=1, device_id=target, device_id_type=MESH)

        pl.when(jnp.logical_or(place >= span - 2, before_far))(lambda: go(go_west, east))
        pl.when(after_far)(lambda: go(go_east, west))
        pl.when(jnp.logical_and(jnp.logical_not(lat_odd), lat > 0))(lambda: go(go_north, south))
        pl.when(fold_late)(lambda: go(go_north, north))

    loads = [
        pltpu.make_async_copy(src, dst, load_sem.at[n])
        for n, (src, dst) in enumerate(
            (
                (bottom_hbm, bottom),
                (open_hbm.at[pl.ds(0, 2 * ROWS)], top_open),
                (warm_hbm, warm.at[pl.ds(0, CELLS)]),
                (salt_hbm, salt.at[pl.ds(0, CELLS)]),
                (zonal_hbm, zonal.at[pl.ds(0, CELLS)]),
                (merid_hbm, merid.at[pl.ds(0, CELLS)]),
                (mixing_hbm, mixing),
            )
        )
    ]
    for load in loads[:6]:
        load.start()

    lane = iota(1)
    row = iota(0)
    nothing = jnp.zeros((ROWS, LANES), jnp.float32)
    for field in fields:
        field[pl.ds(CELLS, 8)] = jnp.zeros((8, LANES), jnp.float32)

    @pl.when(is_south)
    def _():
        row_recv[0] = jnp.zeros((MASK_ROW + 8, LANES), jnp.float32)

    row_global = (lat * ROWS + row).astype(jnp.float32)
    coriolis = ROTATION * jnp.sin(
        math.pi / 180.0 * (-80.0 + 170.0 * (row_global + 0.5) / (ROWS * lat_count))
    )

    def at_level(k):
        return pl.ds(k * ROWS if isinstance(k, int) else pl.multiple_of(k * ROWS, ROWS), ROWS)

    def pack(source, n, sums):
        easts, wests = sums
        for k in range(LEVELS):
            at = n * LEVELS + k
            turned = pltpu.roll(source(k), (at + 1) % LANES, axis=1)
            easts = jnp.where(lane == at, turned, easts)
            wests = jnp.where(lane == (at + 1) % LANES, turned, wests)
        return easts, wests

    pl.when(meets_early)(meet)
    loads[0].wait()
    loads[1].wait()
    deep = bottom[...].astype(jnp.float32)
    open0 = top_open[pl.ds(0, ROWS)].astype(jnp.float32)
    open1 = top_open[pl.ds(ROWS, ROWS)].astype(jnp.float32)
    mask_planes = (deep, open0, open1)
    for side, edge in ((0, 0), (1, ROWS - 1)):
        for n, plane in enumerate(mask_planes):
            row_send[side, pl.ds(MASK_ROW + n, 1)] = plane[edge : edge + 1]
        row_send[side, pl.ds(MASK_ROW + 3, 5)] = jnp.zeros((5, LANES), jnp.float32)
    east_masks = nothing
    west_masks = nothing
    for n, plane in enumerate(mask_planes):
        turned = pltpu.roll(plane, n + 1, axis=1)
        east_masks = jnp.where(lane == n, turned, east_masks)
        west_masks = jnp.where(lane == n + 1, turned, west_masks)
    west_masks = pltpu.roll(west_masks, LANES - 1, axis=1)
    turned = jnp.concatenate([east_masks, west_masks, west_masks, east_masks], axis=0).T[:8]
    col_send[1, pl.ds(ROWS, 8)] = turned
    col_send[0, pl.ds(ROWS, 8)] = turned
    own_planes = pltpu.roll(turned, LANES - 2 * ROWS, axis=1)
    packed = (nothing, nothing)
    for n, field in enumerate(fields):
        loads[2 + n].wait()
        if n == 1:
            loads[6].start()
        for side, edge in ((0, 0), (1, ROWS - 1)):
            row_send[side, pl.ds(n * LEVELS, LEVELS)] = field[pl.ds(edge, LEVELS, stride=ROWS)]
        packed = pack(lambda k, field=field: field[at_level(k)], n, packed)
    col_send[1, pl.ds(0, ROWS)] = packed[0]
    col_send[0, pl.ds(0, ROWS)] = pltpu.roll(packed[1], LANES - 1, axis=1)

    @pl.when(is_north)
    def _():
        flip = (LANES - 1) - lax.broadcasted_iota(jnp.int32, (8, LANES), 1)
        for tile in range((MASK_ROW + 8) // 8):
            there = pl.ds(tile * 8, 8)
            turned = jnp.take_along_axis(row_send[1, there], flip, axis=1)
            if 2 * LEVELS <= tile * 8 < 4 * LEVELS:
                turned = -turned
            row_send[1, there] = turned

    to_north = pltpu.make_async_remote_copy(
        src_ref=row_send.at[1],
        dst_ref=row_recv.at[jnp.where(is_north, 1, 0)],
        send_sem=send_sem.at[1],
        recv_sem=recv_sem.at[jnp.where(is_north, 1, 0)],
        device_id=north,
        device_id_type=MESH,
    )
    to_south = pltpu.make_async_remote_copy(
        src_ref=row_send.at[0],
        dst_ref=row_recv.at[1],
        send_sem=send_sem.at[0],
        recv_sem=recv_sem.at[1],
        device_id=south,
        device_id_type=MESH,
    )
    to_east = pltpu.make_async_remote_copy(
        src_ref=col_send.at[1],
        dst_ref=col_recv.at[0],
        send_sem=send_sem.at[3],
        recv_sem=recv_sem.at[2],
        device_id=east,
        device_id_type=MESH,
    )
    to_west = pltpu.make_async_remote_copy(
        src_ref=col_send.at[0],
        dst_ref=col_recv.at[1],
        send_sem=send_sem.at[2],
        recv_sem=recv_sem.at[3],
        device_id=west,
        device_id_type=MESH,
    )
    pl.when(jnp.logical_not(meets_early))(meet)
    north_turn = 0
    for n, turn in enumerate(FOLD_TURNS):
        north_turn = jnp.where(jnp.logical_and(fold_late, place == span - 1 - n), turn, north_turn)
    pl.when(first_east)(to_east.start)
    pl.when(first_west)(to_west.start)
    pl.when(jnp.logical_and(first_north, north_turn == 0))(to_north.start)
    pl.when(lat > 0)(to_south.start)

    def levels_first(wests, easts):
        return jnp.concatenate([wests, easts, nothing, nothing], axis=0).T

    loads[6].wait()
    depth_here = bottom[...]
    not_east = lane < LANES - 1
    not_north = row < ROWS - 1
    depth_east = jnp.where(
        not_east, jnp.minimum(depth_here, pltpu.roll(depth_here, LANES - 1, axis=1)), 0
    )
    depth_north = jnp.where(
        not_north, jnp.minimum(depth_here, pltpu.roll(depth_here, ROWS - 1, axis=0)), 0
    )
    link[pl.ds(0, ROWS)] = nothing

    def level(k, masks, carried):
        above, g_above, pressure_sum = carried
        wet, wet_east, wet_north, wet_below = masks
        k_float = jnp.asarray(k, jnp.int32).astype(jnp.float32)
        start = k * ROWS
        here = pl.ds(start if isinstance(k, int) else pl.multiple_of(start, ROWS), ROWS)
        shifted = pl.ds(start + 1, ROWS)
        t, s, u, v = (field[here] for field in fields)
        t_n, s_n, u_n, v_n = (field[shifted] for field in fields)
        t_e, s_e, u_e, v_e = (pltpu.roll(x, LANES - 1, axis=1) for x in (t, s, u, v))

        half = half_density(t, s, wet, k_float)
        pressure = pressure_sum + half
        pressure_sum = pressure + half
        p_e = pltpu.roll(pressure, LANES - 1, axis=1)
        p_n = pltpu.roll(pressure, ROWS - 1, axis=0)

        a_e = FACE * (u + u_e)
        a_n = FACE * (v + v_n)
        ahead_e = jnp.where(wet_east, a_e - 1.0, 0.0)
        behind_e = jnp.where(wet_east, a_e + 1.0, 0.0)
        ahead_n = jnp.where(wet_north, a_n - 1.0, 0.0)
        behind_n = jnp.where(wet_north, a_n + 1.0, 0.0)

        def spread(f_e, f_n):
            return (f_e - pltpu.roll(f_e, 1, axis=1)) + (f_n - pltpu.roll(f_n, 1, axis=0))

        def tracer(q, q_e, q_n):
            f_e = ahead_e * q_e + behind_e * q
            f_n = ahead_n * q_n + behind_n * q
            return jnp.where(wet, q - DIFFUSE * spread(f_e, f_n), 0.0)

        warm_out[here] = tracer(t, t_e, t_n)
        salt_out[here] = tracer(s, s_e, s_n)

        du_e = jnp.where(wet_east, u_e - u, 0.0)
        dp_e = jnp.where(wet_east, p_e - pressure, 0.0)
        du_n = jnp.where(wet_north, u_n - u, 0.0)
        lap_u = ((du_e - dp_e) - pltpu.roll(du_e + dp_e, 1, axis=1)) + (
            du_n - pltpu.roll(du_n, 1, axis=0)
        )
        zonal_out[here] = jnp.where(wet, u + VISCOUS * lap_u + coriolis * v, 0.0)
        dv_n = jnp.where(wet_north, v_n - v, 0.0)
        dp_n = jnp.where(wet_north, p_n - pressure, 0.0)
        dv_e = jnp.where(wet_east, v_e - v, 0.0)
        lap_v = ((dv_n - dp_n) - pltpu.roll(dv_n + dp_n, 1, axis=0)) + (
            dv_e - pltpu.roll(dv_e, 1, axis=1)
        )
        merid_out[here] = jnp.where(wet, v + VISCOUS * lap_v - coriolis * u, 0.0)

        below = jnp.where(wet_below, mixing[here], 0.0)
        diagonal = (1.0 + below) + above * (1.0 - g_above)
        inv = inverse(diagonal)
        dragged = jnp.logical_and(depth_here == k + 1, wet)
        inv_m = inverse(diagonal + jnp.where(dragged, BOTTOM_DRAG, 0.0))
        link[pl.ds(start + ROWS, ROWS)] = below
        inv_tracer[here] = inv
        inv_momentum[here] = inv_m
        return below, below * inv, pressure_sum

    def open_pair(plane):
        wet = plane > 0.5
        wet_east = jnp.where(not_east, plane * pltpu.roll(plane, LANES - 1, axis=1), 0.0) > 0.5
        wet_north = jnp.where(not_north, plane * pltpu.roll(plane, ROWS - 1, axis=0), 0.0) > 0.5
        return wet, wet_east, wet_north

    carried = (nothing, nothing, nothing)
    carried = level(0, open_pair(open0) + (open0 * open1 > 0.5,), carried)
    carried = level(
        1,
        open_pair(open1) + (jnp.logical_and(open1 > 0.5, depth_here > 2),),
        carried,
    )

    def deeper(k, carried):
        masks = (depth_here > k, depth_east > k, depth_north > k, depth_here > k + 1)
        return level(k, masks, carried)

    def group(step, carried):
        pl.when(jnp.logical_and(first_north, north_turn == step + 1))(to_north.start)
        for n in range(UNROLL):
            carried = deeper(2 + UNROLL * step + n, carried)
        return carried

    lax.fori_loop(0, (LEVELS - 2) // UNROLL, group, carried)

    def forward(k, values):
        here = at_level(k)
        above = link[here]
        invs = (inv_tracer[here], inv_momentum[here])
        new = []
        for n in range(FIELDS):
            value = (outs[n][here] + above * values[n]) * invs[n // 2]
            outs[n][here] = value
            new.append(value)
        return tuple(new)

    values = lax.fori_loop(0, LEVELS, forward, (nothing,) * 4, unroll=2)

    def backward(step, values):
        k = LEVELS - 2 - step
        here = at_level(k)
        ratio = link[at_level(k + 1)] * inv_tracer[here]
        new = []
        for n in range(FIELDS):
            value = outs[n][here] + ratio * values[n]
            outs[n][here] = value
            new.append(value)
        return tuple(new)

    lax.fori_loop(0, LEVELS - 1, backward, values, unroll=2)

    for side, edge in ((0, 0), (1, ROWS - 1)):
        there = pl.ds(edge, LEVELS, stride=ROWS)
        above = link[there]
        below = link[pl.ds(ROWS + edge, LEVELS, stride=ROWS)]
        inv_t = inv_tracer[there]
        inv_m = inv_momentum[there]
        up = below * inv_t
        for n in range(FIELDS):
            to = pl.ds(side * FIELDS + n, LEVELS, stride=EDGE)
            edge_inv[to] = inv_m if n > 1 else inv_t
            edge_down[to] = above * (inv_m if n > 1 else inv_t)
            edge_up[to] = up
    packed = (nothing, nothing)
    packed = pack(lambda k: link[at_level(k)], 0, packed)
    packed = pack(lambda k: inv_tracer[at_level(k)], 1, packed)
    packed = pack(lambda k: inv_momentum[at_level(k)], 2, packed)
    packed = pack(lambda k: link[at_level(k + 1)], 3, packed)

    coefs = levels_first(pltpu.roll(packed[1], LANES - 1, axis=1), packed[0])
    above, inv_t, inv_m, below = (coefs[n * LEVELS : (n + 1) * LEVELS] for n in range(4))
    for n in range(FIELDS):
        to = pl.ds(2 * FIELDS + n, LEVELS, stride=EDGE)
        edge_inv[to] = inv_m if n > 1 else inv_t
        edge_down[to] = above * (inv_m if n > 1 else inv_t)
        edge_up[to] = below * inv_t
        spare = pl.ds(3 * FIELDS + n, LEVELS, stride=EDGE)
        edge_down[spare] = nothing
        edge_up[spare] = nothing
        edge_value[spare] = nothing
    edge_half[...] = jnp.zeros_like(edge_half)
    edge_weight[...] = jnp.zeros_like(edge_weight)

    def edge_level(k):
        return pl.ds(k * EDGE, EDGE)

    for start in range(0, LEVELS, BLOCK):
        down = up = None
        for n in range(BLOCK):
            k = start + n
            down = edge_down[edge_level(k)] if n == 0 else down * edge_down[edge_level(k)]
            edge_down_block[edge_level(k)] = down
            k = start + BLOCK - 1 - n
            up = edge_up[edge_level(k)] if n == 0 else up * edge_up[edge_level(k)]
            edge_up_block[edge_level(k)] = up

    def wet_levels(level_index, depth, first, second):
        return jnp.where(
            level_index == 0,
            first,
            jnp.where(
                level_index == 1,
                second,
                jnp.where(level_index.astype(jnp.float32) < depth, 1.0, 0.0),
            ),
        )

    def arrival(source, target, slot, sem):
        return pltpu.make_async_remote_copy(
            src_ref=source.at[slot],
            dst_ref=target.at[slot],
            send_sem=send_sem.at[sem],
            recv_sem=recv_sem.at[sem],
            device_id=east,
            device_id_type=MESH,
        )

    from_south = arrival(row_send, row_recv, 0, 0)
    from_north = arrival(row_send, row_recv, 1, 1)
    from_west = arrival(col_send, col_recv, 0, 2)
    from_east = arrival(col_send, col_recv, 1, 3)

    row_float = row.astype(jnp.float32)
    column_lane = lane < 2 * ROWS
    column_sign = jnp.where(lane < ROWS, -1.0, 1.0)

    def row_edge(fields_there, planes):
        wet = wet_levels(row, *planes)
        half = half_density(fields_there[0], fields_there[1], wet > 0.5, row_float)
        return fields_there, wet, half

    def column_edge(buffer, planes):
        turned = levels_first(*(buffer[side, pl.ds(0, ROWS)] for side in (0, 1)))
        return row_edge(
            [turned[n * LEVELS : (n + 1) * LEVELS] for n in range(FIELDS)],
            [planes[n : n + 1] for n in range(3)],
        )

    def edge_terms(group, here, there, sign, across, extent=None):
        own, own_wet, own_half = here
        other, other_wet, other_half = there
        face = own_wet * other_wet > 0.5
        if extent is not None:
            face = jnp.logical_and(face, extent)
        a = (sign * FACE) * (own[across] + other[across])
        for n in range(FIELDS):
            to = pl.ds(group * FIELDS + n, LEVELS, stride=EDGE)
            if n < 2:
                fix = -DIFFUSE * ((a - 1.0) * other[n] + (a + 1.0) * own[n])
            else:
                fix = VISCOUS * (other[n] - own[n])
            edge_value[to] = jnp.where(face, fix * edge_inv[to], 0.0)
        to = pl.ds(group * FIELDS + across, LEVELS, stride=EDGE)
        edge_half[to] = other_half - own_half
        edge_weight[to] = jnp.where(face, (-VISCOUS * sign) * edge_inv[to], 0.0)

    own_rows = [
        row_edge(
            [field[pl.ds(edge, LEVELS, stride=ROWS)] for field in fields],
            [plane[edge : edge + 1] for plane in mask_planes],
        )
        for edge in (0, ROWS - 1)
    ]
    own_columns = column_edge(col_send, own_planes)

    @pl.when(answers_north)
    def _():
        pl.semaphore_wait(go_north, 1)
        to_north.start()

    @pl.when(answers_east)
    def _():
        pl.semaphore_wait(go_east, 1)
        to_east.start()

    @pl.when(answers_west)
    def _():
        pl.semaphore_wait(go_west, 1)
        to_west.start()

    from_north.wait_recv()
    pl.when(lat > 0)(from_south.wait_recv)
    for side in (0, 1):
        there = row_edge(
            [row_recv[side, pl.ds(n * LEVELS, LEVELS)] for n in range(FIELDS)],
            [row_recv[side, pl.ds(MASK_ROW + n, 1)] for n in range(3)],
        )
        edge_terms(side, own_rows[side], there, 1.0 if side else -1.0, 3)

    from_east.wait_recv()
    from_west.wait_recv()
    planes = jnp.where(
        lane[:8] < ROWS, col_recv[0, pl.ds(ROWS, 8)], col_recv[1, pl.ds(ROWS, 8)]
    )
    edge_terms(2, own_columns, column_edge(col_recv, planes), column_sign, 2, column_lane)

    total = jnp.zeros((EDGE, LANES), jnp.float32)
    values = []
    for k in range(LEVELS):
        half = edge_half[edge_level(k)]
        total = total + half
        value = edge_value[edge_level(k)] + edge_weight[edge_level(k)] * total
        total = total + half
        if k % BLOCK:
            value = value + edge_down[edge_level(k)] * values[-1]
        values.append(value)
    for start in range(BLOCK, LEVELS, BLOCK):
        for k in range(start, start + BLOCK):
            values[k] = values[k] + edge_down_block[edge_level(k)] * values[start - 1]
    for k in range(LEVELS - 2, -1, -1):
        if (k + 1) % BLOCK:
            values[k] = values[k] + edge_up[edge_level(k)] * values[k + 1]
    for end in range(LEVELS - BLOCK, 0, -BLOCK):
        for k in range(end - BLOCK, end):
            values[k] = values[k] + edge_up_block[edge_level(k)] * values[end]
    for k in range(LEVELS):
        edge_value[edge_level(k)] = values[k]

    turned = jnp.concatenate(
        [edge_value[pl.ds(2 * FIELDS + n, LEVELS, stride=EDGE)] for n in range(FIELDS)], axis=0
    ).T
    west_fix = pltpu.roll(turned[:ROWS], 1, axis=1)
    east_fix = turned[ROWS : 2 * ROWS]
    even_lane = lax.rem(lane, 2) == 0
    col_out[pl.ds(0, ROWS)] = jnp.where(even_lane, east_fix, west_fix)
    col_out[pl.ds(ROWS, ROWS)] = jnp.where(even_lane, west_fix, east_fix)

    to_north.wait_send()
    to_east.wait_send()
    to_west.wait_send()

    @pl.when(lat > 0)
    def _():
        to_south.wait_send()


def finish(
    warm, salt, zonal, merid, col_fix, edge_value, warm_hbm, salt_hbm, zonal_hbm, merid_hbm, done, sem
):
    lane = iota(1)
    edge_lane = jnp.logical_or(lane == 0, lane == LANES - 1)
    sources = (warm, salt, zonal, merid)
    targets = (warm_hbm, salt_hbm, zonal_hbm, merid_hbm)
    stores = []
    for n in range(FIELDS):
        for part in range(PARTS):
            levels = LEVELS // PARTS
            first = part * levels
            for k in range(first, first + levels):
                here = pl.ds(k * ROWS, ROWS)
                fix = col_fix[pl.ds(k % 2 * ROWS, ROWS)]
                turned = pltpu.roll(fix, LANES - 1 - n * LEVELS - k, axis=1)
                done[n, here] = sources[n][here] + jnp.where(edge_lane, turned, 0.0)
            for side, edge in ((0, 0), (1, ROWS - 1)):
                there = pl.ds(first * ROWS + edge, levels, stride=ROWS)
                done[n, there] += edge_value[pl.ds(first * EDGE + side * FIELDS + n, levels, stride=EDGE)]
            cells = pl.ds(first * ROWS, levels * ROWS)
            store = pltpu.make_async_copy(done.at[n, cells], targets[n].at[cells], sem.at[n, part])
            store.start()
            stores.append(store)
    for store in stores:
        store.wait()


def result(space, rows):
    return space((rows, LANES), jnp.float32)


def keep_in(x, space):
    return pltpu.with_memory_space_constraint(x, space)


def solution(mesh):
    lat_count = mesh.shape["lat"]
    lon_count = mesh.shape["lon"]

    def step(warm, salt, zonal, merid, mixing, open_water, bottom):
        flat = [x.reshape(CELLS, LANES) for x in (warm, salt, zonal, merid, mixing, open_water)]
        f32 = jnp.float32
        solved = pl.pallas_call(
            functools.partial(kernel, lat_count, lon_count),
            out_shape=[
                *[result(pltpu.VMEM, CELLS)] * FIELDS,
                result(pltpu.VMEM, 2 * ROWS),
                result(pltpu.VMEM, (LEVELS + 1) * EDGE),
            ],
            in_specs=[pl.BlockSpec(memory_space=pl.ANY)] * 7,
            out_specs=[pl.BlockSpec(memory_space=pltpu.VMEM)] * (FIELDS + 2),
            scratch_shapes=[
                *[pltpu.VMEM((CELLS + ROWS, LANES), f32)] * FIELDS,
                pltpu.VMEM((CELLS, LANES), f32),
                pltpu.VMEM((2 * ROWS, LANES), jnp.int32),
                pltpu.VMEM((ROWS, LANES), jnp.int32),
                pltpu.VMEM((CELLS + 2 * ROWS, LANES), f32),
                pltpu.VMEM((CELLS + ROWS, LANES), f32),
                pltpu.VMEM((CELLS + ROWS, LANES), f32),
                pltpu.VMEM((2, MASK_ROW + 8, LANES), f32),
                pltpu.VMEM((2, MASK_ROW + 8, LANES), f32),
                pltpu.VMEM((2, ROWS + 8, LANES), f32),
                pltpu.VMEM((2, ROWS + 8, LANES), f32),
                *[pltpu.VMEM(((LEVELS + 1) * EDGE, LANES), f32)] * 7,
                pltpu.SemaphoreType.DMA((7,)),
                pltpu.SemaphoreType.DMA((4,)),
                pltpu.SemaphoreType.DMA((4,)),
                pltpu.SemaphoreType.REGULAR,
                pltpu.SemaphoreType.REGULAR,
                pltpu.SemaphoreType.REGULAR,
            ],
            compiler_params=pltpu.CompilerParams(
                collective_id=0, has_side_effects=True, vmem_limit_bytes=16 * 1024 * 1024
            ),
        )(*[keep_in(x, pltpu.HBM) for x in (*flat, bottom)])
        outs = pl.pallas_call(
            finish,
            out_shape=[result(pltpu.HBM, CELLS)] * FIELDS,
            in_specs=[pl.BlockSpec(memory_space=pltpu.VMEM)] * (FIELDS + 2),
            out_specs=[pl.BlockSpec(memory_space=pltpu.HBM)] * FIELDS,
            scratch_shapes=[
                pltpu.VMEM((FIELDS, CELLS + ROWS, LANES), f32),
                pltpu.SemaphoreType.DMA((FIELDS, PARTS)),
            ],
            compiler_params=pltpu.CompilerParams(vmem_limit_bytes=8 * 1024 * 1024),
        )(*[keep_in(x, pltpu.VMEM) for x in solved])
        return tuple(x.reshape(LEVELS, ROWS, LANES) for x in outs)

    tile = P(None, "lat", "lon")
    return jax.shard_map(
        step,
        mesh=mesh,
        in_specs=(tile,) * 6 + (P("lat", "lon"),),
        out_specs=(tile,) * 4,
        check_vma=False,
    )
```

```python
import functools
import math

import jax
import jax.numpy as jnp
from jax import lax
from jax.experimental import pallas as pl
from jax.experimental.pallas import tpu as pltpu
from jax.sharding import PartitionSpec as P

THERMAL_EXPAND = 0.1655
HALINE_CONTRACT = 0.76554
THERMAL_CABBELING = 0.05952
HALINE_CABBELING = 0.00074914
THERMAL_PRESSURE = 0.0001497
HALINE_PRESSURE = 1.109e-05
MIXED_CABBELING = 0.0024341
ADVECT = 0.2
DIFFUSE = 0.08
VISCOUS = 0.08
GRADIENT = 0.1
ROTATION = 0.25
BOTTOM_DRAG = 1.0
OCEAN_DEPTH = 4000.0

MESH = pl.DeviceIdType.MESH
LEVELS = 32
ROWS = 32
LANES = 128
CELLS = LEVELS * ROWS
FIELDS = 4
MASK_ROW = FIELDS * LEVELS
EDGE = 16
UNROLL = 3
BLOCK = 4
PARTS = 2
FOLD_TURNS = (0, 1, 3, 5, 0, 0, 0, 0)
PRESSURE_SCALE = 0.5 / LEVELS * (0.5 * GRADIENT / VISCOUS)
FACE = 0.25 * ADVECT / DIFFUSE


def half_density(warm, salt, wet, level):
    thermal = warm - 10.0
    haline = salt - 35.0
    depth = (level + 0.5) * (OCEAN_DEPTH / LEVELS)
    s = PRESSURE_SCALE
    by_thermal = -THERMAL_EXPAND * s - (THERMAL_EXPAND * THERMAL_PRESSURE * s) * depth
    by_haline = HALINE_CONTRACT * s - (HALINE_CONTRACT * HALINE_PRESSURE * s) * depth
    value = thermal * (
        by_thermal
        - (0.5 * THERMAL_EXPAND * THERMAL_CABBELING * s) * thermal
        - (MIXED_CABBELING * s) * haline
    ) + haline * (by_haline - (0.5 * HALINE_CONTRACT * HALINE_CABBELING * s) * haline)
    return jnp.where(wet, value, 0.0)


def inverse(x):
    r = pl.reciprocal(x, approx=True)
    return r * (2.0 - x * r)


def iota(axis):
    return lax.broadcasted_iota(jnp.int32, (ROWS, LANES), axis)


def kernel(
    lat_count,
    lon_count,
    warm_hbm,
    salt_hbm,
    zonal_hbm,
    merid_hbm,
    mixing_hbm,
    open_hbm,
    bottom_hbm,
    warm_out,
    salt_out,
    zonal_out,
    merid_out,
    col_out,
    edge_value,
    warm,
    salt,
    zonal,
    merid,
    mixing,
    top_open,
    bottom,
    link,
    inv_tracer,
    inv_momentum,
    row_send,
    row_recv,
    col_send,
    col_recv,
    edge_inv,
    edge_down,
    edge_up,
    edge_down_block,
    edge_up_block,
    edge_half,
    edge_weight,
    load_sem,
    send_sem,
    recv_sem,
    go_west,
    go_north,
):
    lat = lax.axis_index("lat")
    lon = lax.axis_index("lon")
    is_south = lat == 0
    is_north = lat == lat_count - 1
    east = {"lon": lax.rem(lon + 1, lon_count)}
    west = {"lon": lax.rem(lon + lon_count - 1, lon_count)}
    south = {"lat": jnp.maximum(lat - 1, 0)}
    north_lat = jnp.minimum(lat + 1, lat_count - 1)
    north_lon = jnp.where(is_north, lon_count - 1 - lon, lon)
    north = {"lat": north_lat, "lon": north_lon}
    fields = (warm, salt, zonal, merid)
    outs = (warm_out, salt_out, zonal_out, merid_out)

    span = lon_count // 2
    place = lax.rem(lon, span)
    is_last = place == span - 1
    lat_odd = lax.rem(lat, 2) == 1
    answers_west = jnp.logical_or(place == 0, is_last)
    fold_late = jnp.logical_and(is_north, place >= span // 2)
    answers_north = jnp.logical_and(lat_odd, jnp.logical_not(fold_late))
    first_west = jnp.logical_not(answers_west)
    first_north = jnp.logical_not(answers_north)

    barrier = pltpu.get_barrier_semaphore()

    def greet(target):
        pl.semaphore_signal(barrier, inc=1, device_id=target, device_id_type=MESH)

    pl.when(jnp.logical_not(fold_late))(lambda: greet(north))
    pl.when(lat_odd)(lambda: greet(south))
    pl.when(place < span - 2)(lambda: greet(east))
    greet(west)
    greetings = (
        1
        + jnp.where(first_west, 1, 0)
        + jnp.where(first_north, 1, 0)
        + jnp.where(is_south, 0, 1)
    )

    meets_early = jnp.logical_and(is_last, lax.rem(lat, 4) != 0)

    def meet():
        pl.semaphore_wait(barrier, greetings)

        def go(sem, target):
            pl.semaphore_signal(sem, inc=1, device_id=target, device_id_type=MESH)

        pl.when(place >= span - 2)(lambda: go(go_west, east))
        pl.when(jnp.logical_and(jnp.logical_not(lat_odd), lat > 0))(lambda: go(go_north, south))
        pl.when(fold_late)(lambda: go(go_north, north))

    loads = [
        pltpu.make_async_copy(src, dst, load_sem.at[n])
        for n, (src, dst) in enumerate(
            (
                (bottom_hbm, bottom),
                (open_hbm.at[pl.ds(0, 2 * ROWS)], top_open),
                (warm_hbm, warm.at[pl.ds(0, CELLS)]),
                (salt_hbm, salt.at[pl.ds(0, CELLS)]),
                (zonal_hbm, zonal.at[pl.ds(0, CELLS)]),
                (merid_hbm, merid.at[pl.ds(0, CELLS)]),
                (mixing_hbm, mixing),
            )
        )
    ]
    for load in loads[:6]:
        load.start()

    lane = iota(1)
    row = iota(0)
    nothing = jnp.zeros((ROWS, LANES), jnp.float32)
    for field in fields:
        field[pl.ds(CELLS, 8)] = jnp.zeros((8, LANES), jnp.float32)

    @pl.when(is_south)
    def _():
        row_recv[0] = jnp.zeros((MASK_ROW + 8, LANES), jnp.float32)

    row_global = (lat * ROWS + row).astype(jnp.float32)
    coriolis = ROTATION * jnp.sin(
        math.pi / 180.0 * (-80.0 + 170.0 * (row_global + 0.5) / (ROWS * lat_count))
    )

    def at_level(k):
        return pl.ds(k * ROWS if isinstance(k, int) else pl.multiple_of(k * ROWS, ROWS), ROWS)

    def pack(source, n, sums):
        easts, wests = sums
        for k in range(LEVELS):
            at = n * LEVELS + k
            turned = pltpu.roll(source(k), (at + 1) % LANES, axis=1)
            easts = jnp.where(lane == at, turned, easts)
            wests = jnp.where(lane == (at + 1) % LANES, turned, wests)
        return easts, wests

    pl.when(meets_early)(meet)
    loads[0].wait()
    loads[1].wait()
    deep = bottom[...].astype(jnp.float32)
    open0 = top_open[pl.ds(0, ROWS)].astype(jnp.float32)
    open1 = top_open[pl.ds(ROWS, ROWS)].astype(jnp.float32)
    mask_planes = (deep, open0, open1)
    for side, edge in ((0, 0), (1, ROWS - 1)):
        for n, plane in enumerate(mask_planes):
            row_send[side, pl.ds(MASK_ROW + n, 1)] = plane[edge : edge + 1]
        row_send[side, pl.ds(MASK_ROW + 3, 5)] = jnp.zeros((5, LANES), jnp.float32)
    east_masks = nothing
    west_masks = nothing
    for n, plane in enumerate(mask_planes):
        turned = pltpu.roll(plane, n + 1, axis=1)
        east_masks = jnp.where(lane == n, turned, east_masks)
        west_masks = jnp.where(lane == n + 1, turned, west_masks)
    west_masks = pltpu.roll(west_masks, LANES - 1, axis=1)
    turned = jnp.concatenate([east_masks, west_masks, west_masks, east_masks], axis=0).T[:8]
    col_send[1, pl.ds(ROWS, 8)] = turned
    col_send[0, pl.ds(ROWS, 8)] = turned
    own_planes = pltpu.roll(turned, LANES - 2 * ROWS, axis=1)
    packed = (nothing, nothing)
    for n, field in enumerate(fields):
        loads[2 + n].wait()
        if n == 1:
            loads[6].start()
        for side, edge in ((0, 0), (1, ROWS - 1)):
            row_send[side, pl.ds(n * LEVELS, LEVELS)] = field[pl.ds(edge, LEVELS, stride=ROWS)]
        packed = pack(lambda k, field=field: field[at_level(k)], n, packed)
    col_send[1, pl.ds(0, ROWS)] = packed[0]
    col_send[0, pl.ds(0, ROWS)] = pltpu.roll(packed[1], LANES - 1, axis=1)

    @pl.when(is_north)
    def _():
        flip = (LANES - 1) - lax.broadcasted_iota(jnp.int32, (8, LANES), 1)
        for tile in range((MASK_ROW + 8) // 8):
            there = pl.ds(tile * 8, 8)
            turned = jnp.take_along_axis(row_send[1, there], flip, axis=1)
            if 2 * LEVELS <= tile * 8 < 4 * LEVELS:
                turned = -turned
            row_send[1, there] = turned

    to_north = pltpu.make_async_remote_copy(
        src_ref=row_send.at[1],
        dst_ref=row_recv.at[jnp.where(is_north, 1, 0)],
        send_sem=send_sem.at[1],
        recv_sem=recv_sem.at[jnp.where(is_north, 1, 0)],
        device_id=north,
        device_id_type=MESH,
    )
    to_south = pltpu.make_async_remote_copy(
        src_ref=row_send.at[0],
        dst_ref=row_recv.at[1],
        send_sem=send_sem.at[0],
        recv_sem=recv_sem.at[1],
        device_id=south,
        device_id_type=MESH,
    )
    to_east = pltpu.make_async_remote_copy(
        src_ref=col_send.at[1],
        dst_ref=col_recv.at[0],
        send_sem=send_sem.at[3],
        recv_sem=recv_sem.at[2],
        device_id=east,
        device_id_type=MESH,
    )
    to_west = pltpu.make_async_remote_copy(
        src_ref=col_send.at[0],
        dst_ref=col_recv.at[1],
        send_sem=send_sem.at[2],
        recv_sem=recv_sem.at[3],
        device_id=west,
        device_id_type=MESH,
    )
    pl.when(jnp.logical_not(meets_early))(meet)
    north_turn = 0
    for n, turn in enumerate(FOLD_TURNS):
        north_turn = jnp.where(jnp.logical_and(fold_late, place == span - 1 - n), turn, north_turn)
    to_east.start()
    pl.when(first_west)(to_west.start)
    pl.when(jnp.logical_and(first_north, north_turn == 0))(to_north.start)
    pl.when(lat > 0)(to_south.start)

    def levels_first(wests, easts):
        return jnp.concatenate([wests, easts, nothing, nothing], axis=0).T

    loads[6].wait()
    depth_here = bottom[...]
    not_east = lane < LANES - 1
    not_north = row < ROWS - 1
    depth_east = jnp.where(
        not_east, jnp.minimum(depth_here, pltpu.roll(depth_here, LANES - 1, axis=1)), 0
    )
    depth_north = jnp.where(
        not_north, jnp.minimum(depth_here, pltpu.roll(depth_here, ROWS - 1, axis=0)), 0
    )
    link[pl.ds(0, ROWS)] = nothing

    def level(k, masks, carried):
        above, g_above, pressure_sum = carried
        wet, wet_east, wet_north, wet_below = masks
        k_float = jnp.asarray(k, jnp.int32).astype(jnp.float32)
        start = k * ROWS
        here = pl.ds(start if isinstance(k, int) else pl.multiple_of(start, ROWS), ROWS)
        shifted = pl.ds(start + 1, ROWS)
        t, s, u, v = (field[here] for field in fields)
        t_n, s_n, u_n, v_n = (field[shifted] for field in fields)
        t_e, s_e, u_e, v_e = (pltpu.roll(x, LANES - 1, axis=1) for x in (t, s, u, v))

        half = half_density(t, s, wet, k_float)
        pressure = pressure_sum + half
        pressure_sum = pressure + half
        p_e = pltpu.roll(pressure, LANES - 1, axis=1)
        p_n = pltpu.roll(pressure, ROWS - 1, axis=0)

        a_e = FACE * (u + u_e)
        a_n = FACE * (v + v_n)
        ahead_e = jnp.where(wet_east, a_e - 1.0, 0.0)
        behind_e = jnp.where(wet_east, a_e + 1.0, 0.0)
        ahead_n = jnp.where(wet_north, a_n - 1.0, 0.0)
        behind_n = jnp.where(wet_north, a_n + 1.0, 0.0)

        def spread(f_e, f_n):
            return (f_e - pltpu.roll(f_e, 1, axis=1)) + (f_n - pltpu.roll(f_n, 1, axis=0))

        def tracer(q, q_e, q_n):
            f_e = ahead_e * q_e + behind_e * q
            f_n = ahead_n * q_n + behind_n * q
            return jnp.where(wet, q - DIFFUSE * spread(f_e, f_n), 0.0)

        warm_out[here] = tracer(t, t_e, t_n)
        salt_out[here] = tracer(s, s_e, s_n)

        du_e = jnp.where(wet_east, u_e - u, 0.0)
        dp_e = jnp.where(wet_east, p_e - pressure, 0.0)
        du_n = jnp.where(wet_north, u_n - u, 0.0)
        lap_u = ((du_e - dp_e) - pltpu.roll(du_e + dp_e, 1, axis=1)) + (
            du_n - pltpu.roll(du_n, 1, axis=0)
        )
        zonal_out[here] = jnp.where(wet, u + VISCOUS * lap_u + coriolis * v, 0.0)
        dv_n = jnp.where(wet_north, v_n - v, 0.0)
        dp_n = jnp.where(wet_north, p_n - pressure, 0.0)
        dv_e = jnp.where(wet_east, v_e - v, 0.0)
        lap_v = ((dv_n - dp_n) - pltpu.roll(dv_n + dp_n, 1, axis=0)) + (
            dv_e - pltpu.roll(dv_e, 1, axis=1)
        )
        merid_out[here] = jnp.where(wet, v + VISCOUS * lap_v - coriolis * u, 0.0)

        below = jnp.where(wet_below, mixing[here], 0.0)
        diagonal = (1.0 + below) + above * (1.0 - g_above)
        inv = inverse(diagonal)
        dragged = jnp.logical_and(depth_here == k + 1, wet)
        inv_m = inverse(diagonal + jnp.where(dragged, BOTTOM_DRAG, 0.0))
        link[pl.ds(start + ROWS, ROWS)] = below
        inv_tracer[here] = inv
        inv_momentum[here] = inv_m
        return below, below * inv, pressure_sum

    def open_pair(plane):
        wet = plane > 0.5
        wet_east = jnp.where(not_east, plane * pltpu.roll(plane, LANES - 1, axis=1), 0.0) > 0.5
        wet_north = jnp.where(not_north, plane * pltpu.roll(plane, ROWS - 1, axis=0), 0.0) > 0.5
        return wet, wet_east, wet_north

    carried = (nothing, nothing, nothing)
    carried = level(0, open_pair(open0) + (open0 * open1 > 0.5,), carried)
    carried = level(
        1,
        open_pair(open1) + (jnp.logical_and(open1 > 0.5, depth_here > 2),),
        carried,
    )

    def deeper(k, carried):
        masks = (depth_here > k, depth_east > k, depth_north > k, depth_here > k + 1)
        return level(k, masks, carried)

    def group(step, carried):
        pl.when(jnp.logical_and(first_north, north_turn == step + 1))(to_north.start)
        for n in range(UNROLL):
            carried = deeper(2 + UNROLL * step + n, carried)
        return carried

    lax.fori_loop(0, (LEVELS - 2) // UNROLL, group, carried)

    def forward(k, values):
        here = at_level(k)
        above = link[here]
        invs = (inv_tracer[here], inv_momentum[here])
        new = []
        for n in range(FIELDS):
            value = (outs[n][here] + above * values[n]) * invs[n // 2]
            outs[n][here] = value
            new.append(value)
        return tuple(new)

    values = lax.fori_loop(0, LEVELS, forward, (nothing,) * 4, unroll=2)

    def backward(step, values):
        k = LEVELS - 2 - step
        here = at_level(k)
        ratio = link[at_level(k + 1)] * inv_tracer[here]
        new = []
        for n in range(FIELDS):
            value = outs[n][here] + ratio * values[n]
            outs[n][here] = value
            new.append(value)
        return tuple(new)

    lax.fori_loop(0, LEVELS - 1, backward, values, unroll=2)

    for side, edge in ((0, 0), (1, ROWS - 1)):
        there = pl.ds(edge, LEVELS, stride=ROWS)
        above = link[there]
        below = link[pl.ds(ROWS + edge, LEVELS, stride=ROWS)]
        inv_t = inv_tracer[there]
        inv_m = inv_momentum[there]
        up = below * inv_t
        for n in range(FIELDS):
            to = pl.ds(side * FIELDS + n, LEVELS, stride=EDGE)
            edge_inv[to] = inv_m if n > 1 else inv_t
            edge_down[to] = above * (inv_m if n > 1 else inv_t)
            edge_up[to] = up
    packed = (nothing, nothing)
    packed = pack(lambda k: link[at_level(k)], 0, packed)
    packed = pack(lambda k: inv_tracer[at_level(k)], 1, packed)
    packed = pack(lambda k: inv_momentum[at_level(k)], 2, packed)
    packed = pack(lambda k: link[at_level(k + 1)], 3, packed)

    coefs = levels_first(pltpu.roll(packed[1], LANES - 1, axis=1), packed[0])
    above, inv_t, inv_m, below = (coefs[n * LEVELS : (n + 1) * LEVELS] for n in range(4))
    for n in range(FIELDS):
        to = pl.ds(2 * FIELDS + n, LEVELS, stride=EDGE)
        edge_inv[to] = inv_m if n > 1 else inv_t
        edge_down[to] = above * (inv_m if n > 1 else inv_t)
        edge_up[to] = below * inv_t
        spare = pl.ds(3 * FIELDS + n, LEVELS, stride=EDGE)
        edge_down[spare] = nothing
        edge_up[spare] = nothing
        edge_value[spare] = nothing
    edge_half[...] = jnp.zeros_like(edge_half)
    edge_weight[...] = jnp.zeros_like(edge_weight)

    def edge_level(k):
        return pl.ds(k * EDGE, EDGE)

    for start in range(0, LEVELS, BLOCK):
        down = up = None
        for n in range(BLOCK):
            k = start + n
            down = edge_down[edge_level(k)] if n == 0 else down * edge_down[edge_level(k)]
            edge_down_block[edge_level(k)] = down
            k = start + BLOCK - 1 - n
            up = edge_up[edge_level(k)] if n == 0 else up * edge_up[edge_level(k)]
            edge_up_block[edge_level(k)] = up

    def wet_levels(level_index, depth, first, second):
        return jnp.where(
            level_index == 0,
            first,
            jnp.where(
                level_index == 1,
                second,
                jnp.where(level_index.astype(jnp.float32) < depth, 1.0, 0.0),
            ),
        )

    def arrival(source, target, slot, sem):
        return pltpu.make_async_remote_copy(
            src_ref=source.at[slot],
            dst_ref=target.at[slot],
            send_sem=send_sem.at[sem],
            recv_sem=recv_sem.at[sem],
            device_id=east,
            device_id_type=MESH,
        )

    from_south = arrival(row_send, row_recv, 0, 0)
    from_north = arrival(row_send, row_recv, 1, 1)
    from_west = arrival(col_send, col_recv, 0, 2)
    from_east = arrival(col_send, col_recv, 1, 3)

    row_float = row.astype(jnp.float32)
    column_lane = lane < 2 * ROWS
    column_sign = jnp.where(lane < ROWS, -1.0, 1.0)

    def row_edge(fields_there, planes):
        wet = wet_levels(row, *planes)
        half = half_density(fields_there[0], fields_there[1], wet > 0.5, row_float)
        return fields_there, wet, half

    def column_edge(buffer, planes):
        turned = levels_first(*(buffer[side, pl.ds(0, ROWS)] for side in (0, 1)))
        return row_edge(
            [turned[n * LEVELS : (n + 1) * LEVELS] for n in range(FIELDS)],
            [planes[n : n + 1] for n in range(3)],
        )

    def edge_terms(group, here, there, sign, across, extent=None):
        own, own_wet, own_half = here
        other, other_wet, other_half = there
        face = own_wet * other_wet > 0.5
        if extent is not None:
            face = jnp.logical_and(face, extent)
        a = (sign * FACE) * (own[across] + other[across])
        for n in range(FIELDS):
            to = pl.ds(group * FIELDS + n, LEVELS, stride=EDGE)
            if n < 2:
                fix = -DIFFUSE * ((a - 1.0) * other[n] + (a + 1.0) * own[n])
            else:
                fix = VISCOUS * (other[n] - own[n])
            edge_value[to] = jnp.where(face, fix * edge_inv[to], 0.0)
        to = pl.ds(group * FIELDS + across, LEVELS, stride=EDGE)
        edge_half[to] = other_half - own_half
        edge_weight[to] = jnp.where(face, (-VISCOUS * sign) * edge_inv[to], 0.0)

    own_rows = [
        row_edge(
            [field[pl.ds(edge, LEVELS, stride=ROWS)] for field in fields],
            [plane[edge : edge + 1] for plane in mask_planes],
        )
        for edge in (0, ROWS - 1)
    ]
    own_columns = column_edge(col_send, own_planes)

    @pl.when(answers_north)
    def _():
        pl.semaphore_wait(go_north, 1)
        to_north.start()

    @pl.when(answers_west)
    def _():
        pl.semaphore_wait(go_west, 1)
        to_west.start()

    from_east.wait_recv()
    from_west.wait_recv()
    planes = jnp.where(
        lane[:8] < ROWS, col_recv[0, pl.ds(ROWS, 8)], col_recv[1, pl.ds(ROWS, 8)]
    )
    edge_terms(2, own_columns, column_edge(col_recv, planes), column_sign, 2, column_lane)

    from_north.wait_recv()
    pl.when(lat > 0)(from_south.wait_recv)
    for side in (0, 1):
        there = row_edge(
            [row_recv[side, pl.ds(n * LEVELS, LEVELS)] for n in range(FIELDS)],
            [row_recv[side, pl.ds(MASK_ROW + n, 1)] for n in range(3)],
        )
        edge_terms(side, own_rows[side], there, 1.0 if side else -1.0, 3)

    total = jnp.zeros((EDGE, LANES), jnp.float32)
    values = []
    for k in range(LEVELS):
        half = edge_half[edge_level(k)]
        total = total + half
        value = edge_value[edge_level(k)] + edge_weight[edge_level(k)] * total
        total = total + half
        if k % BLOCK:
            value = value + edge_down[edge_level(k)] * values[-1]
        values.append(value)
    for start in range(BLOCK, LEVELS, BLOCK):
        for k in range(start, start + BLOCK):
            values[k] = values[k] + edge_down_block[edge_level(k)] * values[start - 1]
    for k in range(LEVELS - 2, -1, -1):
        if (k + 1) % BLOCK:
            values[k] = values[k] + edge_up[edge_level(k)] * values[k + 1]
    for end in range(LEVELS - BLOCK, 0, -BLOCK):
        for k in range(end - BLOCK, end):
            values[k] = values[k] + edge_up_block[edge_level(k)] * values[end]
    for k in range(LEVELS):
        edge_value[edge_level(k)] = values[k]

    turned = jnp.concatenate(
        [edge_value[pl.ds(2 * FIELDS + n, LEVELS, stride=EDGE)] for n in range(FIELDS)], axis=0
    ).T
    west_fix = pltpu.roll(turned[:ROWS], 1, axis=1)
    east_fix = turned[ROWS : 2 * ROWS]
    even_lane = lax.rem(lane, 2) == 0
    col_out[pl.ds(0, ROWS)] = jnp.where(even_lane, east_fix, west_fix)
    col_out[pl.ds(ROWS, ROWS)] = jnp.where(even_lane, west_fix, east_fix)

    to_north.wait_send()
    to_east.wait_send()
    to_west.wait_send()

    @pl.when(lat > 0)
    def _():
        to_south.wait_send()


def finish(
    warm, salt, zonal, merid, col_fix, edge_value, warm_hbm, salt_hbm, zonal_hbm, merid_hbm, done, sem
):
    lane = iota(1)
    edge_lane = jnp.logical_or(lane == 0, lane == LANES - 1)
    sources = (warm, salt, zonal, merid)
    targets = (warm_hbm, salt_hbm, zonal_hbm, merid_hbm)
    stores = []
    for n in range(FIELDS):
        for part in range(PARTS):
            levels = LEVELS // PARTS
            first = part * levels
            for k in range(first, first + levels):
                here = pl.ds(k * ROWS, ROWS)
                fix = col_fix[pl.ds(k % 2 * ROWS, ROWS)]
                turned = pltpu.roll(fix, LANES - 1 - n * LEVELS - k, axis=1)
                done[n, here] = sources[n][here] + jnp.where(edge_lane, turned, 0.0)
            for side, edge in ((0, 0), (1, ROWS - 1)):
                there = pl.ds(first * ROWS + edge, levels, stride=ROWS)
                done[n, there] += edge_value[pl.ds(first * EDGE + side * FIELDS + n, levels, stride=EDGE)]
            cells = pl.ds(first * ROWS, levels * ROWS)
            store = pltpu.make_async_copy(done.at[n, cells], targets[n].at[cells], sem.at[n, part])
            store.start()
            stores.append(store)
    for store in stores:
        store.wait()


def result(space, rows):
    return space((rows, LANES), jnp.float32)


def keep_in(x, space):
    return pltpu.with_memory_space_constraint(x, space)


def solution(mesh):
    lat_count = mesh.shape["lat"]
    lon_count = mesh.shape["lon"]

    def step(warm, salt, zonal, merid, mixing, open_water, bottom):
        flat = [x.reshape(CELLS, LANES) for x in (warm, salt, zonal, merid, mixing, open_water)]
        f32 = jnp.float32
        solved = pl.pallas_call(
            functools.partial(kernel, lat_count, lon_count),
            out_shape=[
                *[result(pltpu.VMEM, CELLS)] * FIELDS,
                result(pltpu.VMEM, 2 * ROWS),
                result(pltpu.VMEM, (LEVELS + 1) * EDGE),
            ],
            in_specs=[pl.BlockSpec(memory_space=pl.ANY)] * 7,
            out_specs=[pl.BlockSpec(memory_space=pltpu.VMEM)] * (FIELDS + 2),
            scratch_shapes=[
                *[pltpu.VMEM((CELLS + ROWS, LANES), f32)] * FIELDS,
                pltpu.VMEM((CELLS, LANES), f32),
                pltpu.VMEM((2 * ROWS, LANES), jnp.int32),
                pltpu.VMEM((ROWS, LANES), jnp.int32),
                pltpu.VMEM((CELLS + 2 * ROWS, LANES), f32),
                pltpu.VMEM((CELLS + ROWS, LANES), f32),
                pltpu.VMEM((CELLS + ROWS, LANES), f32),
                pltpu.VMEM((2, MASK_ROW + 8, LANES), f32),
                pltpu.VMEM((2, MASK_ROW + 8, LANES), f32),
                pltpu.VMEM((2, ROWS + 8, LANES), f32),
                pltpu.VMEM((2, ROWS + 8, LANES), f32),
                *[pltpu.VMEM(((LEVELS + 1) * EDGE, LANES), f32)] * 7,
                pltpu.SemaphoreType.DMA((7,)),
                pltpu.SemaphoreType.DMA((4,)),
                pltpu.SemaphoreType.DMA((4,)),
                pltpu.SemaphoreType.REGULAR,
                pltpu.SemaphoreType.REGULAR,
            ],
            compiler_params=pltpu.CompilerParams(
                collective_id=0, has_side_effects=True, vmem_limit_bytes=16 * 1024 * 1024
            ),
        )(*[keep_in(x, pltpu.HBM) for x in (*flat, bottom)])
        outs = pl.pallas_call(
            finish,
            out_shape=[result(pltpu.HBM, CELLS)] * FIELDS,
            in_specs=[pl.BlockSpec(memory_space=pltpu.VMEM)] * (FIELDS + 2),
            out_specs=[pl.BlockSpec(memory_space=pltpu.HBM)] * FIELDS,
            scratch_shapes=[
                pltpu.VMEM((FIELDS, CELLS + ROWS, LANES), f32),
                pltpu.SemaphoreType.DMA((FIELDS, PARTS)),
            ],
            compiler_params=pltpu.CompilerParams(vmem_limit_bytes=8 * 1024 * 1024),
        )(*[keep_in(x, pltpu.VMEM) for x in solved])
        return tuple(x.reshape(LEVELS, ROWS, LANES) for x in outs)

    tile = P(None, "lat", "lon")
    return jax.shard_map(
        step,
        mesh=mesh,
        in_specs=(tile,) * 6 + (P("lat", "lon"),),
        out_specs=(tile,) * 4,
        check_vma=False,
    )
```
